32 devices in a mesh: dp: 8 (over z, y), seq: 4 (over x, core).
Axes of the slice: x: 2, y: 2, z: 4, core: 2. Of those that a mesh axis runs over, the one named last changes fastest.
Arguments:
- frames: bfloat16 [8, 1280, 1024], P('dp', 'seq'), may hold values from -6 to 6
- frame_seg: int32 [8, 1280], P('dp'), may hold values from 0 to 3, as said below
- text_states: bfloat16 [8, 64, 1024], P('dp'), may hold values from -6 to 6
- text_len: int32 [8, 4], P('dp'), may hold values from 1 to 16
- norm_gain: bfloat16 [1024, 3], P(('dp', 'seq')), may hold values from 0.5 to 1.5
- norm_bias: bfloat16 [1024, 3], P(('dp', 'seq')), may hold values from -3 to 3
- self_qkv: bfloat16 [1024, 3072], P(('dp', 'seq')), may hold values from -0.25 to 0.25
- self_out: bfloat16 [1024, 1024], P(('dp', 'seq')), may hold values from -0.375 to 0.375
- cross_qkv: bfloat16 [1024, 3072], P(('dp', 'seq')), may hold values from -0.25 to 0.25
- cross_out: bfloat16 [1024, 1024], P(('dp', 'seq')), may hold values from -0.1875 to 0.1875
- ffn_up: bfloat16 [1024, 4096], P(('dp', 'seq')), may hold values from -0.1875 to 0.1875
- ffn_down: bfloat16 [4096, 1024], P(('dp', 'seq')), may hold values from -0.09375 to 0.09375
- cotangent: bfloat16 [8, 1280, 1024], P('dp', 'seq'), may hold values from -6 to 6
Outputs:
- frames_out: bfloat16 [8, 1280, 1024], P('dp', 'seq')
- frames_grad: bfloat16 [8, 1280, 1024], P('dp', 'seq')
- text_grad: bfloat16 [8, 64, 1024], P('dp', 'seq')
- gain_grad: float32 [1024, 3], P(('dp', 'seq'))
- bias_grad: float32 [1024, 3], P(('dp', 'seq'))
- self_qkv_grad: float32 [1024, 3072], P(('dp', 'seq'))
- self_out_grad: float32 [1024, 1024], P(('dp', 'seq'))
- cross_qkv_grad: float32 [1024, 3072], P(('dp', 'seq'))
- cross_out_grad: float32 [1024, 1024], P(('dp', 'seq'))
- up_grad: float32 [1024, 4096], P(('dp', 'seq'))
- down_grad: float32 [4096, 1024], P(('dp', 'seq'))
The draws below stay inside these ranges and needn't reach their ends.
Inputs may be any that keep to these rules, and one draw needn't show every extreme that they name: `frame_seg`: clip numbers never fall along a row, and every clip 0 to 3 has at least one frame in each row.
All inputs are finite; a program needn't handle non-finite values.
Results may differ from the reference program's by a relative error of at most 0.02.
Values may be sent and summed in bfloat16 or wider, within the bound.
A program may use at most 256 MiB of HBM per device.

```python
import jax
import jax.numpy as jnp
from jax import lax

D = 1024
HEADS = 16
HEAD_DIM = 64
FF = 4096
ROW_LEN = 1280
TEXT_LEN = 64
CLIPS = 4
ROWS = 8
N_SEQ = 4


def draw_frame_seg(key, part):
    key = jax.random.fold_in(key, 11)
    width = ROW_LEN // N_SEQ
    step_most = width // CLIPS
    keys = jax.random.split(key, 3)
    long_clip = jax.random.randint(keys[0], (ROWS, 1), 0, CLIPS)
    head = jnp.cumsum(jax.random.randint(keys[1], (ROWS, CLIPS - 1), 1, step_most + 1), axis=1)
    tail = jnp.cumsum(jax.random.randint(keys[2], (ROWS, CLIPS - 1), 1, step_most + 1), axis=1)
    order = jnp.arange(1, CLIPS, dtype=jnp.int32)
    bounds = jnp.where(order[None, :] <= long_clip, head, ROW_LEN - tail[:, ::-1])
    positions = jnp.arange(ROW_LEN, dtype=jnp.int32)
    return jnp.sum((positions[None, :, None] >= bounds[:, None, :]).astype(jnp.int32), axis=2)


def plant(drawn, rng, low, top_value):
    shape = drawn.shape
    spot = [jax.random.randint(jax.random.fold_in(rng, axis), (), 0, shape[axis]) for axis in range(len(shape))]
    drawn = drawn.at[tuple(spot)].set(low)
    longest = shape.index(max(shape))
    spot[longest] = (spot[longest] + 1) % shape[longest]
    return drawn.at[tuple(spot)].set(top_value)


def strengthened(array, rng, source, target, parts, factor):
    owner, partner = [(jnp.arange(array.shape[dim]) // (array.shape[dim] // parts)).reshape([-1 if axis == dim else 1 for axis in range(array.ndim)]) for dim in (source, target)]
    chosen = jax.random.permutation(rng, parts)[partner]
    strong = (owner == chosen) | (owner == (partner + parts // 2) % parts)
    return jnp.where(strong, factor * array, array)


def level_of(rng, extent, cuts, smallest, high):
    level, own = 1.0, jax.random.fold_in(rng, 6)
    for dim, blocks in cuts:
        draws = jnp.exp(jax.random.uniform(jax.random.fold_in(own, dim), (blocks,), jnp.float32, smallest / len(cuts), high / len(cuts)))
        level = level * jnp.repeat(draws, extent[dim] // blocks).reshape([-1 if axis == dim else 1 for axis in range(len(extent))])
    return level


def gaussian(key, dims, scale, reach, pieces=(), kind=jnp.bfloat16):
    result = scale * jax.random.normal(key, dims, jnp.float32)
    if pieces:
        result = result * level_of(key, dims, pieces, -0.22, 0.18)
    return jnp.clip(result, -reach, reach).astype(kind)


def noise_with(key, dims, scale, reach, cuts, heavy, kind=jnp.bfloat16):
    values = scale * jax.random.normal(key, dims, jnp.float32)
    if cuts:
        values = values * level_of(key, dims, cuts, -0.22, 0.18)
    return jnp.clip(strengthened(values, jax.random.fold_in(key, 3), *heavy), -reach, reach).astype(kind)


def setup_inputs(seed: int = 0) -> dict:
    streams_of = jax.random.split(jax.random.key(seed), 14)
    frames = noise_with(streams_of[0], (ROWS, ROW_LEN, D), 1.0, 6.0, ((0, 8), (1, 4)), (0, 2, 8, 2.0))
    frame_seg = draw_frame_seg(jax.random.fold_in(streams_of[13], 71), 0)
    text_states = gaussian(streams_of[2], (ROWS, TEXT_LEN, D), 1.0, 6.0, ((0, 8),))
    text_len = plant(jax.random.randint(streams_of[3], (ROWS, CLIPS), 1, TEXT_LEN // CLIPS + 1), jax.random.fold_in(streams_of[3], 1), 1, (TEXT_LEN // CLIPS + 1) - 1).astype(jnp.int32)
    norm_gain = jnp.clip(1.0 + 0.1 * jax.random.normal(streams_of[4], (D, 3), jnp.float32), 0.5, 1.5).astype(jnp.bfloat16)
    norm_bias = gaussian(streams_of[5], (D, 3), 0.5, 3.0, ((0, 32),))
    self_qkv = gaussian(streams_of[6], (D, 3 * D), (D // 2) ** -0.5, 0.25, ((0, 32),))
    self_out = gaussian(streams_of[7], (D, D), (D // 4) ** -0.5, 0.375, ((0, 32),))
    cross_qkv = gaussian(streams_of[8], (D, 3 * D), (D // 2) ** -0.5, 0.25, ((0, 32),))
    cross_out = gaussian(streams_of[9], (D, D), D ** -0.5, 0.1875, ((0, 32),))
    ffn_up = gaussian(streams_of[10], (D, FF), D ** -0.5, 0.1875, ((0, 32),))
    ffn_down = gaussian(streams_of[11], (FF, D), FF ** -0.5, 0.09375, ((0, 32),))
    cotangent = gaussian(streams_of[12], (ROWS, ROW_LEN, D), 1.0, 6.0, ((0, 8), (1, 4)))
    return {"frames": frames, "frame_seg": frame_seg, "text_states": text_states, "text_len": text_len, "norm_gain": norm_gain, "norm_bias": norm_bias, "self_qkv": self_qkv, "self_out": self_out, "cross_qkv": cross_qkv, "cross_out": cross_out, "ffn_up": ffn_up, "ffn_down": ffn_down, "cotangent": cotangent}


@jax.custom_vjp
def low(v):
    return lax.optimization_barrier(v.astype(jnp.bfloat16)).astype(jnp.float32)

@jax.custom_vjp
def low_back(v):
    return v

def low_keep(v):
    return (low(v), None)

def low_pass(kept, grad):
    return (grad,)

def back_keep(v):
    return (v, None)

def back_low(kept, grad):
    return (low(grad),)
low.defvjp(low_keep, low_pass)
low_back.defvjp(back_keep, back_low)

def layer_norm(values, gain, bias):
    center = values - lax.optimization_barrier(jnp.mean(values, axis=-1, keepdims=True))
    spread = lax.optimization_barrier(jnp.mean(center * center, axis=-1, keepdims=True))
    return center * lax.rsqrt(spread + 1e-05) * gain + bias

def product(left, right):
    return jnp.dot(left, right, precision=lax.Precision.HIGHEST, preferred_element_type=jnp.float32)

def text_segments(text_len):
    bounds = jnp.cumsum(text_len, axis=1)
    positions = jnp.arange(TEXT_LEN, dtype=jnp.int32)
    return lax.optimization_barrier(jnp.sum((positions[None, :, None] >= bounds[:, None, :]).astype(jnp.int32), axis=2))

def attend(queries, keys_in, values, allowed):
    factor = HEAD_DIM ** (-0.5)
    heads_q = queries.reshape(queries.shape[0], HEADS, HEAD_DIM)
    heads_k = keys_in.reshape(keys_in.shape[0], HEADS, HEAD_DIM)
    heads_v = values.reshape(values.shape[0], HEADS, HEAD_DIM)
    scores = low_back(factor * jnp.einsum('qhe,khe->hqk', heads_q, heads_k, precision=lax.Precision.HIGHEST))
    scores = jnp.where(allowed[None], scores, -1e+30)
    highest = lax.optimization_barrier(jnp.max(scores, axis=-1, keepdims=True))
    powered = jnp.exp(scores - highest)
    weights = low(powered / lax.optimization_barrier(jnp.sum(powered, axis=-1, keepdims=True)))
    context = jnp.einsum('hqk,khe->qhe', weights, heads_v, precision=lax.Precision.HIGHEST)
    return low_back(low(context.reshape(queries.shape[0], HEADS * HEAD_DIM)))

def row_layer(inputs, frame_row, text_row, text_row_seg, params):
    norm_gain, norm_bias, self_qkv, self_out, cross_qkv, cross_out, ffn_up, ffn_down = params
    positions = jnp.arange(ROW_LEN, dtype=jnp.int32)
    self_mask = (positions[:, None] >= positions[None, :]) & (frame_row[:, None] == frame_row[None, :])
    cross_mask = frame_row[:, None] == text_row_seg[None, :]
    normed_self = low(layer_norm(inputs, norm_gain[:, 0], norm_bias[:, 0]))
    queries = low_back(low(product(normed_self, self_qkv[:, :D])))
    keys_self = low_back(low(product(normed_self, self_qkv[:, D:2 * D])))
    values_self = low_back(low(product(normed_self, self_qkv[:, 2 * D:])))
    self_context = attend(queries, keys_self, values_self, self_mask)
    resid_one = inputs + low_back(product(self_context, self_out))
    normed_cross = low(layer_norm(resid_one, norm_gain[:, 1], norm_bias[:, 1]))
    cross_queries = low_back(low(product(normed_cross, cross_qkv[:, :D])))
    cross_keys = low_back(low(product(text_row, cross_qkv[:, D:2 * D])))
    cross_values = low_back(low(product(text_row, cross_qkv[:, 2 * D:])))
    cross_context = attend(cross_queries, cross_keys, cross_values, cross_mask)
    resid_two = resid_one + low_back(product(cross_context, cross_out))
    normed_ffn = low(layer_norm(resid_two, norm_gain[:, 2], norm_bias[:, 2]))
    hidden_pre = low_back(product(normed_ffn, ffn_up))
    activated = low(jax.nn.gelu(hidden_pre, approximate=False))
    return resid_two + low_back(product(activated, ffn_down))

def reference(frames, frame_seg, text_states, text_len, norm_gain, norm_bias, self_qkv, self_out, cross_qkv, cross_out, ffn_up, ffn_down, cotangent):
    text_seg = text_segments(text_len)
    params = jax.tree.map(lambda weight: weight.astype(jnp.float32), (norm_gain, norm_bias, self_qkv, self_out, cross_qkv, cross_out, ffn_up, ffn_down))

    def forward(inputs, texts, weights):

        def one_row(record):
            return row_layer(record[0], record[1], record[2], record[3], weights)
        return lax.map(jax.checkpoint(one_row), (inputs, frame_seg, texts, text_seg))
    outcome, pullback = jax.vjp(forward, frames.astype(jnp.float32), text_states.astype(jnp.float32), params)
    frames_grad, text_grad, grads = pullback(cotangent.astype(jnp.float32))
    return (outcome.astype(jnp.bfloat16), frames_grad.astype(jnp.bfloat16), text_grad.astype(jnp.bfloat16), grads[0], grads[1], grads[2], grads[3], grads[4], grads[5], grads[6], grads[7])
```

```python
import jax
import jax.numpy as jnp
from jax import lax
from jax.experimental import pallas as pl
from jax.experimental.pallas import tpu as pltpu
from jax.sharding import PartitionSpec as P

D = 1024
HEADS = 16
HEAD_DIM = 64
TEXT_LEN = 64


def layer_norm(values, gain, bias):
    center = values - jnp.mean(values, axis=-1, keepdims=True)
    spread = jnp.mean(center * center, axis=-1, keepdims=True)
    return center * lax.rsqrt(spread + 1e-05) * gain + bias


def norm_back(values, gain, bias, upstream):
    unused_value, pullback = jax.vjp(layer_norm, values, gain, bias)
    return pullback(upstream)


def exact_gelu(values):
    return jax.nn.gelu(values, approximate=False)


def split_heads(values):
    return values.reshape(values.shape[0], HEADS, HEAD_DIM)


def text_segments(text_len):
    bounds = jnp.cumsum(text_len, axis=1)
    positions = jnp.arange(TEXT_LEN, dtype=jnp.int32)
    return jnp.sum((positions[None, :, None] >= bounds[:, None, :]).astype(jnp.int32), axis=2)


def self_allowed(local_seg, full_seg, offset):
    row_pos = offset + jnp.arange(local_seg.shape[0], dtype=jnp.int32)
    col_pos = jnp.arange(full_seg.shape[0], dtype=jnp.int32)
    return (row_pos[:, None] >= col_pos[None, :]) & (local_seg[:, None] == full_seg[None, :])


def masked_scores(queries, keys_in, allowed):
    factor = HEAD_DIM ** (-0.5)
    scores = (
        jnp.einsum(
            "qhe,khe->hqk",
            split_heads(queries),
            split_heads(keys_in),
            preferred_element_type=jnp.float32,
        )
        * factor
    )
    return jnp.where(allowed[None], scores, -1e30)


def attend(queries, keys_in, values, allowed):
    scores = masked_scores(queries, keys_in, allowed)
    highest = jnp.max(scores, axis=-1, keepdims=True)
    powered = jnp.exp(scores - highest)
    totals = jnp.sum(powered, axis=-1, keepdims=True)
    weights = (powered / totals).astype(jnp.bfloat16)
    context = jnp.einsum(
        "hqk,khe->qhe", weights, split_heads(values), preferred_element_type=jnp.float32
    )
    return (context.reshape(queries.shape[0], -1), highest + jnp.log(totals))


def attend_back(queries, keys_in, values, allowed, logsum, upstream):
    factor = HEAD_DIM ** (-0.5)
    probs_full = jnp.exp(masked_scores(queries, keys_in, allowed) - logsum)
    grad_heads = split_heads(upstream)
    grad_probs = jnp.einsum(
        "qhe,khe->hqk", grad_heads, split_heads(values), preferred_element_type=jnp.float32
    )
    row_inner = jnp.sum(probs_full * grad_probs, axis=-1, keepdims=True)
    grad_scores = (probs_full * (grad_probs - row_inner)).astype(jnp.bfloat16)
    grad_queries = (
        jnp.einsum(
            "hqk,khe->qhe", grad_scores, split_heads(keys_in), preferred_element_type=jnp.float32
        )
        * factor
    )
    grad_keys = (
        jnp.einsum(
            "hqk,qhe->khe", grad_scores, split_heads(queries), preferred_element_type=jnp.float32
        )
        * factor
    )
    grad_values = jnp.einsum(
        "hqk,qhe->khe",
        probs_full.astype(jnp.bfloat16),
        grad_heads,
        preferred_element_type=jnp.float32,
    )
    return (
        grad_queries.reshape(queries.shape[0], -1),
        grad_keys.reshape(keys_in.shape[0], -1),
        grad_values.reshape(values.shape[0], -1),
    )


MESH = pl.DeviceIdType.MESH

def place():
    dp, seq = lax.axis_index("dp"), lax.axis_index("seq")
    return dp // 2, lax.rem(dp, 2), seq // 2, lax.rem(seq, 2)

def device(z, y, x, c):
    return (z * 2 + y, x * 2 + c)

def greet(z, y, x, c):
    barrier = pltpu.get_barrier_semaphore()
    others = [device(lax.rem(z + k, 4), y, x, c) for k in (1, 2, 3)]
    others += [device(z, 1 - y, x, c), device(z, y, 1 - x, c), device(z, y, x, 1 - c)]
    for other in others:
        pl.semaphore_signal(barrier, inc=1, device_id=other, device_id_type=MESH)
    pl.semaphore_wait(barrier, len(others))

def gather_kernel(ins, outs, send_sem, recv_sem, own_sem):
    z, y, x, c = place()
    frames, norms, sqkv, sout, cqkv, cout, up, down = ins
    frames_o, norms_o, sqkv_o, sout_o, cqkv_o, cout_o, up_o, down_o = outs
    units = []
    def cols(src, out, k):
        s = pl.ds(k * 1024, 1024)
        units.append((src.at[:, s], lambda zz, yy, xx, cc: out.at[zz, yy, xx, cc, :, s]))
    units.append((norms, lambda zz, yy, xx, cc: norms_o.at[zz, yy, xx, cc]))
    for k in range(3): cols(sqkv, sqkv_o, k)
    cols(sout, sout_o, 0)
    for k in range(3): cols(cqkv, cqkv_o, k)
    cols(cout, cout_o, 0)
    for k in range(4): cols(up, up_o, k)
    for k in range(4):
        units.append((down.at[k], lambda zz, yy, xx, cc, k=k: down_o.at[zz, yy, xx, cc, k]))
    n = len(units)
    every, low, high = pl.ds(0, 4), pl.ds(0, 2), pl.ds(2, 2)
    to_x, to_y, to_c = device(z, y, 1 - x, c), device(z, 1 - y, x, c), device(z, y, x, 1 - c)
    def copy(src, dst, u, k, dev):
        return pltpu.make_async_remote_copy(src_ref=src, dst_ref=dst, send_sem=send_sem.at[u, k], recv_sem=recv_sem.at[u, k], device_id=dev, device_id_type=MESH)
    def same(u, k, dev, *at):
        v = units[u][1](*at)
        return copy(v, v, u, k, dev)
    def zcopy(u, k):
        return copy(units[u][0], units[u][1](z, y, x, c), u, k - 1, device(lax.rem(z + k, 4), y, x, c))
    def own(u):
        return pltpu.make_async_copy(units[u][0], units[u][1](z, y, x, c), own_sem.at[u])
    greet(z, y, x, c)
    sent = []
    def go(d):
        d.start(); sent.append(d)
    f_sem = n
    def fcopy(k, dev, xx, cc):
        v = frames_o.at[xx, cc]
        return copy(v, v, f_sem, k, dev)
    own_f = pltpu.make_async_copy(frames, frames_o.at[x, c], own_sem.at[n])
    own_f.start()
    def z_start(u):
        own(u).start()
        for k in (1, 2, 3): go(zcopy(u, k))
    z_start(0); z_start(1); z_start(2)
    own_f.wait()
    go(fcopy(0, to_x, x, c)); go(fcopy(1, to_c, x, c))
    for t in range(n + 2):
        if t < n:
            for k in (1, 2, 3): zcopy(t, k).wait_recv()
            own(t).wait()
            go(same(t, 3, to_x, every, y, x, c)); go(same(t, 4, to_y, every, y, x, c)); go(same(t, 5, to_c, every, y, x, c))
            if t + 3 < n: z_start(t + 3)
        if t == 2:
            fcopy(0, to_x, 1 - x, c).wait_recv()
            go(fcopy(2, to_c, 1 - x, c))
        u = t - 1
        if 0 <= u < n:
            same(u, 3, to_x, every, y, 1 - x, c).wait_recv()
            go(same(u, 6, to_y, low, y, 1 - x, c)); go(same(u, 7, to_c, every, y, 1 - x, c))
            same(u, 4, to_y, every, 1 - y, x, c).wait_recv()
            go(same(u, 8, to_x, high, 1 - y, x, c)); go(same(u, 9, to_c, every, 1 - y, x, c))
        u = t - 2
        if 0 <= u < n:
            same(u, 6, to_y, low, 1 - y, 1 - x, c).wait_recv()
            go(same(u, 10, to_c, low, 1 - y, 1 - x, c))
            same(u, 8, to_x, high, 1 - y, 1 - x, c).wait_recv()
            go(same(u, 11, to_c, high, 1 - y, 1 - x, c))
    for u in range(n):
        same(u, 5, to_c, every, y, x, 1 - c).wait_recv()
        same(u, 7, to_c, every, y, 1 - x, 1 - c).wait_recv()
        same(u, 9, to_c, every, 1 - y, x, 1 - c).wait_recv()
        same(u, 10, to_c, low, 1 - y, 1 - x, 1 - c).wait_recv()
        same(u, 11, to_c, high, 1 - y, 1 - x, 1 - c).wait_recv()
    fcopy(1, to_c, x, 1 - c).wait_recv()
    fcopy(2, to_c, 1 - x, 1 - c).wait_recv()
    for d in sent: d.wait_send()

def gather(frames, norms, sqkv, sout, cqkv, cout, up, down):
    ins = (frames, norms, sqkv, sout, cqkv, cout, up, down)
    bf = jnp.bfloat16
    shapes = [(2, 2) + frames.shape] + [(4, 2, 2, 2) + a.shape for a in ins[1:]]
    n = 17
    def kernel(*refs):
        gather_kernel(refs[:8], refs[8:16], *refs[16:])
    return pl.pallas_call(kernel, out_shape=[jax.ShapeDtypeStruct(s, bf) for s in shapes],
        in_specs=[pl.BlockSpec(memory_space=pl.ANY)] * 8, out_specs=[pl.BlockSpec(memory_space=pl.ANY)] * 8,
        scratch_shapes=[pltpu.SemaphoreType.DMA((n + 1, 12)), pltpu.SemaphoreType.DMA((n + 1, 12)), pltpu.SemaphoreType.DMA((n + 1,))],
        compiler_params=pltpu.CompilerParams(collective_id=0, has_side_effects=True))(*ins)

def scatter_kernel(ins, outs, own, cr, xr, yr, cc, zr, nown, ncr, nxr, nyr, ncc, nzr, fown, fcr, fxr, town, tcr, txr, ss, rs, ls):
    z, y, x, c = place()
    sqkv, sout, cqkv, cout, up, down, norms, fpart, tpart = ins
    sqkv_o, sout_o, cqkv_o, cout_o, up_o, down_o, norms_o, f_o, t_o = outs
    units = []
    def cols(src, out, k):
        s = pl.ds(k * 1024, 1024)
        units.append((lambda c_: src.at[:, :, :, c_, :, s], out.at[:, s]))
    for k in range(4):
        units.append((lambda c_, k=k: down.at[:, :, :, c_, k], down_o.at[k]))
    for k in range(4): cols(up, up_o, k)
    cols(cout, cout_o, 0)
    for k in range(3): cols(cqkv, cqkv_o, k)
    cols(sout, sout_o, 0)
    for k in range(3): cols(sqkv, sqkv_o, k)
    units.append((lambda c_: norms.at[:, :, :, c_], norms_o))
    n = len(units)
    bufs = [[b.at[u] for b in (own, cr, xr, yr, cc, zr)] for u in range(16)] + [[nown, ncr, nxr, nyr, ncc, nzr]]
    to_x, to_y, to_c = device(z, y, 1 - x, c), device(z, 1 - y, x, c), device(z, y, x, 1 - c)
    def copy(src, dst, u, k, dev):
        return pltpu.make_async_remote_copy(src_ref=src, dst_ref=dst, send_sem=ss.at[u, k], recv_sem=rs.at[u, k], device_id=dev, device_id_type=MESH)
    sent = []
    def go(d):
        d.start(); sent.append(d)
    def add(dst, a, b, lead):
        total = 1
        for s in lead: total *= s
        def step(i, _):
            idx = []
            r = i
            for s in reversed(lead):
                idx.append(lax.rem(r, s)); r = r // s
            idx = tuple(reversed(idx))
            dst[idx] = (a[idx].astype(jnp.float32) + b[idx].astype(jnp.float32)).astype(dst.dtype)
            return 0
        lax.fori_loop(0, total, step, 0)
    greet(z, y, x, c)
    def load(u): return pltpu.make_async_copy(units[u][0](c), bufs[u][0], ls.at[u])
    def ccopy(u): return copy(units[u][0](1 - c), bufs[u][1], u, 0, to_c)
    def x1(u): return copy(bufs[u][0].at[0:2, :, 1 - x], bufs[u][2], u, 1, to_x)
    def y1(u): return copy(bufs[u][0].at[2:4, 1 - y], bufs[u][3], u, 2, to_y)
    def y2(u): return copy(bufs[u][2].at[:, 1 - y], bufs[u][4].at[0:2], u, 3, to_y)
    def x2(u): return copy(bufs[u][3].at[:, 1 - x], bufs[u][4].at[2:4], u, 4, to_x)
    def z1(u, k):
        to = lax.rem(z + k, 4)
        return copy(bufs[u][4].at[to], bufs[u][5].at[k - 1], u, 4 + k, device(to, y, x, c))
    fl = pltpu.make_async_copy(fpart.at[:, c], fown, ls.at[n])
    tl = pltpu.make_async_copy(tpart.at[:, c], town, ls.at[n + 1])
    fc, tc = copy(fpart.at[:, 1 - c], fcr, n, 0, to_c), copy(tpart.at[:, 1 - c], tcr, n, 1, to_c)
    fx, tx = copy(fown.at[1 - x], fxr, n, 2, to_x), copy(town.at[1 - x], txr, n, 3, to_x)
    def first(u):
        load(u).start(); go(ccopy(u))
    for u in range(4): first(u)
    for t in range(n + 3):
        if t < n:
            load(t).wait(); ccopy(t).wait_recv()
            b = bufs[t]
            add(b[0], b[0], b[1], (4, 2, 2))
            go(x1(t)); go(y1(t))
            if t + 4 < n: first(t + 4)
            elif t + 4 == n:
                fl.start(); tl.start(); go(fc); go(tc)
        u = t - 1
        if 0 <= u < n:
            b = bufs[u]
            x1(u).wait_recv()
            add(b[2], b[2], b[0].at[0:2, :, x], (2, 2))
            go(y2(u))
            y1(u).wait_recv()
            add(b[3], b[3], b[0].at[2:4, y], (2, 2))
            go(x2(u))
        u = t - 2
        if 0 <= u < n:
            b = bufs[u]
            y2(u).wait_recv()
            add(b[4].at[0:2], b[4].at[0:2], b[2].at[:, y], (2,))
            x2(u).wait_recv()
            add(b[4].at[2:4], b[4].at[2:4], b[3].at[:, x], (2,))
            for k in (1, 2, 3): go(z1(u, k))
        if t == n - 1:
            fl.wait(); tl.wait(); fc.wait_recv(); tc.wait_recv()
            def fstep(i, _):
                a = i // 5; s = pl.ds(pl.multiple_of(lax.rem(i, 5) * 64, 64), 64)
                fown[a, s] = (fown[a, s].astype(jnp.float32) + fcr[a, s].astype(jnp.float32)).astype(jnp.bfloat16)
                return 0
            lax.fori_loop(0, 10, fstep, 0)
            town[...] = (town[...].astype(jnp.float32) + tcr[...].astype(jnp.float32)).astype(jnp.bfloat16)
            go(fx); go(tx)
        u = t - 3
        if 0 <= u < n:
            b = bufs[u]
            for k in (1, 2, 3): z1(u, k).wait_recv()
            o = units[u][1]
            o[...] = ((b[4][z].astype(jnp.float32) + b[5][0].astype(jnp.float32)) + (b[5][1].astype(jnp.float32) + b[5][2].astype(jnp.float32)))
    fx.wait_recv(); tx.wait_recv()
    def ostep(i, _):
        s = pl.ds(pl.multiple_of(i * 64, 64), 64)
        f_o[s] = fown[x, s].astype(jnp.float32) + fxr[s].astype(jnp.float32)
        return 0
    lax.fori_loop(0, 5, ostep, 0)
    t_o[...] = (town[x].astype(jnp.float32) + txr[...].astype(jnp.float32)).astype(jnp.bfloat16)
    for d in sent: d.wait_send()

def scatter(sqkv, sout, cqkv, cout, up, down, norms, fpart, tpart):
    ins = (sqkv, sout, cqkv, cout, up, down, norms, fpart, tpart)
    bf, f32 = jnp.bfloat16, jnp.float32
    S = jax.ShapeDtypeStruct
    outs = [S((32, 3072), f32), S((32, 1024), f32), S((32, 3072), f32), S((32, 1024), f32), S((32, 4096), f32), S((4, 32, 1024), f32), S((32, 128), f32), S((320, 1024), f32), S((16, 1024), bf)]
    V = pltpu.VMEM
    def unit(lead, w, dt):
        return [V(lead + s + (32, w), dt) for s in ((4, 2, 2), (4, 2, 2), (2, 2), (2, 2), (4,), (3,))]
    def kernel(*refs):
        scatter_kernel(refs[:9], refs[9:18], *refs[18:])
    return pl.pallas_call(kernel, out_shape=outs, in_specs=[pl.BlockSpec(memory_space=pl.ANY)] * 9,
        out_specs=[pl.BlockSpec(memory_space=pltpu.VMEM)] * 9,
        scratch_shapes=unit((16,), 1024, bf) + unit((), 128, f32) + [V((2, 320, 1024), bf), V((2, 320, 1024), bf), V((320, 1024), bf), V((2, 16, 1024), bf), V((2, 16, 1024), bf), V((16, 1024), bf)]
        + [pltpu.SemaphoreType.DMA((18, 8)), pltpu.SemaphoreType.DMA((18, 8)), pltpu.SemaphoreType.DMA((19,))],
        compiler_params=pltpu.CompilerParams(collective_id=1, has_side_effects=True, vmem_limit_bytes=62 * 2**20))(*ins)

def fetch_all(norm_gain, norm_bias, self_qkv, self_out, cross_qkv, cross_out, ffn_up, ffn_down):
    first = (
        lax.all_gather(norm_gain, ("dp", "seq"), axis=0, tiled=True),
        lax.all_gather(norm_bias, ("dp", "seq"), axis=0, tiled=True),
        lax.all_gather(self_qkv, ("dp", "seq"), axis=0, tiled=True),
        lax.all_gather(self_out, ("dp", "seq"), axis=0, tiled=True),
    )
    second = (
        lax.all_gather(cross_qkv, ("dp", "seq"), axis=0, tiled=True),
        lax.all_gather(cross_out, ("dp", "seq"), axis=0, tiled=True),
    )
    third = (
        lax.all_gather(ffn_up, ("dp", "seq"), axis=0, tiled=True),
        lax.all_gather(ffn_down, ("dp", "seq"), axis=0, tiled=True),
    )
    return tuple(first) + tuple(second) + tuple(third)


def run_forward(frames, local_seg, frame_seg, text_seg, text_states, offset, weights):
    norm_gain, norm_bias, self_qkv, self_out, cross_qkv, cross_out, ffn_up, ffn_down = weights
    gains = norm_gain.astype(jnp.float32)
    biases = norm_bias.astype(jnp.float32)
    inputs = frames.astype(jnp.float32)
    normed_self = layer_norm(inputs, gains[:, 0], biases[:, 0]).astype(jnp.bfloat16)
    queries = jnp.dot(normed_self, self_qkv[:, :D], preferred_element_type=jnp.float32).astype(
        jnp.bfloat16
    )
    pair_weights = self_qkv[:, D:].reshape(D, 2, D)
    key_value = jnp.einsum(
        "rcd,dje->jrce", normed_self, pair_weights, preferred_element_type=jnp.float32
    ).astype(jnp.bfloat16)
    gathered = lax.all_gather(key_value, "seq", axis=2, tiled=True)
    self_context, self_logsum = lax.map(
        lambda record: attend(
            record[0], record[1], record[2], self_allowed(record[3], record[4], offset)
        ),
        (queries, gathered[0], gathered[1], local_seg, frame_seg),
    )
    self_context = self_context.astype(jnp.bfloat16)
    resid_one = inputs + jnp.dot(self_context, self_out, preferred_element_type=jnp.float32)
    normed_cross = layer_norm(resid_one, gains[:, 1], biases[:, 1]).astype(jnp.bfloat16)
    cross_queries = jnp.dot(
        normed_cross, cross_qkv[:, :D], preferred_element_type=jnp.float32
    ).astype(jnp.bfloat16)
    text_weights = cross_qkv[:, D:].reshape(D, 2, D)
    text_pair = jnp.einsum(
        "rtd,dje->jrte", text_states, text_weights, preferred_element_type=jnp.float32
    ).astype(jnp.bfloat16)
    cross_context, cross_logsum = lax.map(
        lambda record: attend(
            record[0], record[1], record[2], record[3][:, None] == record[4][None, :]
        ),
        (cross_queries, text_pair[0], text_pair[1], local_seg, text_seg),
    )
    cross_context = cross_context.astype(jnp.bfloat16)
    resid_two = resid_one + jnp.dot(cross_context, cross_out, preferred_element_type=jnp.float32)
    normed_ffn = layer_norm(resid_two, gains[:, 2], biases[:, 2]).astype(jnp.bfloat16)
    hidden_pre = jnp.dot(normed_ffn, ffn_up, preferred_element_type=jnp.float32)
    activated = exact_gelu(hidden_pre).astype(jnp.bfloat16)
    outcome = resid_two + jnp.dot(activated, ffn_down, preferred_element_type=jnp.float32)
    saved = (
        inputs,
        normed_self,
        queries,
        gathered,
        self_context,
        self_logsum,
        resid_one,
        normed_cross,
        cross_queries,
        text_pair,
        cross_context,
        cross_logsum,
        resid_two,
        normed_ffn,
        hidden_pre,
        activated,
    )
    return (outcome, saved)


def generic_body(
    frames,
    frame_seg,
    text_states,
    text_len,
    norm_gain,
    norm_bias,
    self_qkv,
    self_out,
    cross_qkv,
    cross_out,
    ffn_up,
    ffn_down,
    cotangent,
):
    width = frames.shape[1]
    offset = lax.axis_index("seq") * width
    local_seg = lax.dynamic_slice_in_dim(frame_seg, offset, width, 1)
    text_seg = text_segments(text_len)
    shards = (norm_gain, norm_bias, self_qkv, self_out, cross_qkv, cross_out, ffn_up, ffn_down)
    weights = fetch_all(*shards)
    outcome, saved = run_forward(
        frames, local_seg, frame_seg, text_seg, text_states, offset, weights
    )
    frames_out = outcome.astype(jnp.bfloat16)
    (
        inputs,
        normed_self,
        queries,
        gathered,
        self_context,
        self_logsum,
        resid_one,
        normed_cross,
        cross_queries,
        text_pair,
        cross_context,
        cross_logsum,
        resid_two,
        normed_ffn,
        hidden_pre,
        activated,
    ) = saved
    gain_full, bias_full, self_full, self_proj, cross_full, cross_proj, up_full, down_full = weights
    gains = gain_full.astype(jnp.float32)
    biases = bias_full.astype(jnp.float32)
    upstream = cotangent.astype(jnp.float32)
    down_grad = jnp.einsum("rcf,rcd->fd", activated, cotangent, preferred_element_type=jnp.float32)
    grad_act = jnp.einsum("rcd,fd->rcf", cotangent, down_full, preferred_element_type=jnp.float32)
    unused_value, gelu_pull = jax.vjp(exact_gelu, hidden_pre)
    grad_pre = gelu_pull(grad_act)[0].astype(jnp.bfloat16)
    up_grad = jnp.einsum("rcd,rcf->df", normed_ffn, grad_pre, preferred_element_type=jnp.float32)
    grad_normed = jnp.einsum("rcf,df->rcd", grad_pre, up_full, preferred_element_type=jnp.float32)
    grad_back, gain_two, bias_two = norm_back(resid_two, gains[:, 2], biases[:, 2], grad_normed)
    grad_resid_two = upstream + grad_back
    ffn_shares = (
        lax.psum_scatter(up_grad, ("dp", "seq"), scatter_dimension=0, tiled=True),
        lax.psum_scatter(down_grad, ("dp", "seq"), scatter_dimension=0, tiled=True),
    )
    branch_two = grad_resid_two.astype(jnp.bfloat16)
    cross_out_grad = jnp.einsum(
        "rcd,rce->de", cross_context, branch_two, preferred_element_type=jnp.float32
    )
    grad_context = jnp.einsum(
        "rce,de->rcd", branch_two, cross_proj, preferred_element_type=jnp.float32
    ).astype(jnp.bfloat16)
    grad_cross_q, grad_cross_k, grad_cross_v = lax.map(
        lambda record: attend_back(
            record[0],
            record[1],
            record[2],
            record[3][:, None] == record[4][None, :],
            record[5],
            record[6],
        ),
        (
            cross_queries,
            text_pair[0],
            text_pair[1],
            local_seg,
            text_seg,
            cross_logsum,
            grad_context,
        ),
    )
    text_joined = jnp.transpose(jnp.concatenate([grad_cross_k, grad_cross_v], axis=2), (1, 0, 2))
    text_summed = lax.psum_scatter(
        text_joined.astype(jnp.bfloat16), "seq", scatter_dimension=0, tiled=True
    ).astype(jnp.float32)
    text_shares = jnp.transpose(text_summed, (1, 0, 2)).astype(jnp.bfloat16)
    share = text_shares.shape[1]
    text_part = lax.dynamic_slice_in_dim(text_states, lax.axis_index("seq") * share, share, 1)
    text_kv_grad = jnp.einsum(
        "rtd,rte->de", text_part, text_shares, preferred_element_type=jnp.float32
    )
    text_grad = jnp.einsum(
        "rte,de->rtd", text_shares, cross_full[:, D:], preferred_element_type=jnp.float32
    ).astype(jnp.bfloat16)
    grad_cross_q = grad_cross_q.astype(jnp.bfloat16)
    cross_q_grad = jnp.einsum(
        "rcd,rce->de", normed_cross, grad_cross_q, preferred_element_type=jnp.float32
    )
    cross_qkv_grad = jnp.concatenate([cross_q_grad, text_kv_grad], axis=1)
    grad_normed = jnp.einsum(
        "rce,de->rcd", grad_cross_q, cross_full[:, :D], preferred_element_type=jnp.float32
    )
    grad_back, gain_one, bias_one = norm_back(resid_one, gains[:, 1], biases[:, 1], grad_normed)
    grad_resid_one = grad_resid_two + grad_back
    cross_shares = (
        lax.psum_scatter(cross_qkv_grad, ("dp", "seq"), scatter_dimension=0, tiled=True),
        lax.psum_scatter(cross_out_grad, ("dp", "seq"), scatter_dimension=0, tiled=True),
    )
    branch_one = grad_resid_one.astype(jnp.bfloat16)
    self_out_grad = jnp.einsum(
        "rcd,rce->de", self_context, branch_one, preferred_element_type=jnp.float32
    )
    grad_context = jnp.einsum(
        "rce,de->rcd", branch_one, self_proj, preferred_element_type=jnp.float32
    ).astype(jnp.bfloat16)
    grad_self_q, grad_self_k, grad_self_v = lax.map(
        lambda record: attend_back(
            record[0],
            record[1],
            record[2],
            self_allowed(record[3], record[4], offset),
            record[5],
            record[6],
        ),
        (queries, gathered[0], gathered[1], local_seg, frame_seg, self_logsum, grad_context),
    )
    joined = jnp.concatenate([grad_self_k, grad_self_v], axis=2)
    summed = lax.psum_scatter(
        jnp.transpose(joined, (1, 0, 2)).astype(jnp.bfloat16),
        "seq",
        scatter_dimension=0,
        tiled=True,
    ).astype(jnp.float32)
    key_shares = jnp.transpose(summed, (1, 0, 2)).astype(jnp.bfloat16)
    all_grads = jnp.concatenate([grad_self_q.astype(jnp.bfloat16), key_shares], axis=2)
    self_qkv_grad = jnp.einsum(
        "rcd,rce->de", normed_self, all_grads, preferred_element_type=jnp.float32
    )
    grad_normed = jnp.einsum(
        "rce,de->rcd", all_grads, self_full, preferred_element_type=jnp.float32
    )
    grad_back, gain_zero, bias_zero = norm_back(inputs, gains[:, 0], biases[:, 0], grad_normed)
    frames_grad = (grad_resid_one + grad_back).astype(jnp.bfloat16)
    gain_grad = jnp.stack([gain_zero, gain_one, gain_two], axis=1)
    bias_grad = jnp.stack([bias_zero, bias_one, bias_two], axis=1)
    self_shares = (
        lax.psum_scatter(gain_grad, ("dp", "seq"), scatter_dimension=0, tiled=True),
        lax.psum_scatter(bias_grad, ("dp", "seq"), scatter_dimension=0, tiled=True),
        lax.psum_scatter(self_qkv_grad, ("dp", "seq"), scatter_dimension=0, tiled=True),
        lax.psum_scatter(self_out_grad, ("dp", "seq"), scatter_dimension=0, tiled=True),
    )
    return (
        frames_out,
        frames_grad,
        text_grad,
        self_shares[0],
        self_shares[1],
        self_shares[2],
        self_shares[3],
        cross_shares[0],
        cross_shares[1],
        ffn_shares[0],
        ffn_shares[1],
    )


def dense(a, b):
    return jnp.dot(a, b, preferred_element_type=jnp.float32)


def dense_nt(a, b):
    return lax.dot_general(a, b, (((1,), (1,)), ((), ())), preferred_element_type=jnp.float32)


def dense_tn(a, b):
    return lax.dot_general(a, b, (((0,), (0,)), ((), ())), preferred_element_type=jnp.float32)


def fast_body(
    frames,
    frame_seg,
    text_states,
    text_len,
    norm_gain,
    norm_bias,
    self_qkv,
    self_out,
    cross_qkv,
    cross_out,
    ffn_up,
    ffn_down,
    cotangent,
):
    bf = jnp.bfloat16
    width = frames.shape[1]
    offset = lax.axis_index("seq") * width
    full_seg = frame_seg[0]
    local_seg = lax.dynamic_slice_in_dim(full_seg, offset, width, 0)
    text_seg = text_segments(text_len)[0]
    text = text_states[0]
    cot = cotangent[0]
    norms = jnp.pad(jnp.concatenate([norm_gain, norm_bias], axis=1), ((0, 0), (0, 122)))
    gathered = gather(
        frames[0], norms, self_qkv, self_out, cross_qkv, cross_out, ffn_up, ffn_down.reshape(4, 32, D)
    )
    whole_frames = gathered[0].reshape(-1, D).astype(jnp.float32)
    norm_full = gathered[1].reshape(D, 128)[:, :6].astype(jnp.float32)
    gains, biases = norm_full[:, :3], norm_full[:, 3:]
    w_self, w_so, w_cross, w_co, w_up = [g.reshape(D, -1) for g in gathered[2:7]]
    w_down = gathered[7].reshape(-1, D)

    inputs = frames[0].astype(jnp.float32)
    normed_all = layer_norm(whole_frames, gains[:, 0], biases[:, 0]).astype(bf)
    normed_self = lax.dynamic_slice_in_dim(normed_all, offset, width, 0)
    queries = dense(normed_self, w_self[:, :D]).astype(bf)
    keys = dense(normed_all, w_self[:, D : 2 * D]).astype(bf)
    values = dense(normed_all, w_self[:, 2 * D :]).astype(bf)
    allowed = self_allowed(local_seg, full_seg, offset)
    self_context, self_logsum = attend(queries, keys, values, allowed)
    self_context = self_context.astype(bf)
    resid_one = inputs + dense(self_context, w_so)
    normed_cross = layer_norm(resid_one, gains[:, 1], biases[:, 1]).astype(bf)
    cross_queries = dense(normed_cross, w_cross[:, :D]).astype(bf)
    text_pair = dense(text, w_cross[:, D:]).astype(bf)
    cross_allowed = local_seg[:, None] == text_seg[None, :]
    cross_context, cross_logsum = attend(
        cross_queries, text_pair[:, :D], text_pair[:, D:], cross_allowed
    )
    cross_context = cross_context.astype(bf)
    resid_two = resid_one + dense(cross_context, w_co)
    normed_ffn = layer_norm(resid_two, gains[:, 2], biases[:, 2]).astype(bf)
    hidden_pre = dense(normed_ffn, w_up)
    activated, gelu_pull = jax.vjp(exact_gelu, hidden_pre)
    activated = activated.astype(bf)
    frames_out = (resid_two + dense(activated, w_down)).astype(bf)

    upstream = cot.astype(jnp.float32)
    down_grad = dense_tn(activated, cot).astype(bf)
    grad_pre = gelu_pull(dense_nt(cot, w_down))[0].astype(bf)
    up_grad = dense_tn(normed_ffn, grad_pre).astype(bf)
    back, gain_two, bias_two = norm_back(
        resid_two, gains[:, 2], biases[:, 2], dense_nt(grad_pre, w_up)
    )
    grad_resid_two = upstream + back
    branch_two = grad_resid_two.astype(bf)
    cross_out_grad = dense_tn(cross_context, branch_two).astype(bf)
    grad_context = dense_nt(branch_two, w_co).astype(bf)
    grad_cq, grad_ck, grad_cv = attend_back(
        cross_queries,
        text_pair[:, :D],
        text_pair[:, D:],
        cross_allowed,
        cross_logsum,
        grad_context,
    )
    grad_cq = grad_cq.astype(bf)
    text_kv = jnp.concatenate([grad_ck, grad_cv], axis=1).astype(bf)
    text_part = dense_nt(text_kv, w_cross[:, D:]).astype(bf)
    cross_qkv_grad = jnp.concatenate(
        [dense_tn(normed_cross, grad_cq), dense_tn(text, text_kv)], axis=1
    ).astype(bf)
    back, gain_one, bias_one = norm_back(
        resid_one, gains[:, 1], biases[:, 1], dense_nt(grad_cq, w_cross[:, :D])
    )
    grad_resid_one = grad_resid_two + back
    branch_one = grad_resid_one.astype(bf)
    self_out_grad = dense_tn(self_context, branch_one).astype(bf)
    grad_context = dense_nt(branch_one, w_so).astype(bf)
    grad_q, grad_k, grad_v = attend_back(
        queries, keys, values, allowed, self_logsum, grad_context
    )
    grad_q = grad_q.astype(bf)
    grad_kv = jnp.concatenate([grad_k, grad_v], axis=1).astype(bf)
    self_qkv_grad = jnp.concatenate(
        [dense_tn(normed_self, grad_q), dense_tn(normed_all, grad_kv)], axis=1
    ).astype(bf)
    part = dense_nt(grad_kv, w_self[:, D:])
    mine = lax.dynamic_slice_in_dim(part, offset, width, 0) + dense_nt(grad_q, w_self[:, :D])
    part = lax.dynamic_update_slice_in_dim(part, mine, offset, 0)
    unused_back, gain_zero, bias_zero = norm_back(whole_frames, gains[:, 0], biases[:, 0], part)
    norm_grads = jnp.stack([gain_zero, gain_one, gain_two, bias_zero, bias_one, bias_two], axis=1)
    norm_grads = jnp.pad(norm_grads, ((0, 0), (0, 122)))

    def six(a):
        return a.reshape(4, 2, 2, 2, 32, a.shape[-1])

    shares = scatter(
        six(self_qkv_grad),
        six(self_out_grad),
        six(cross_qkv_grad),
        six(cross_out_grad),
        six(up_grad),
        down_grad.reshape(4, 2, 2, 2, 4, 32, D),
        six(norm_grads),
        part.astype(bf).reshape(2, 2, width, D),
        text_part.reshape(2, 2, -1, D),
    )
    back, unused_gain, unused_bias = norm_back(inputs, gains[:, 0], biases[:, 0], shares[7])
    frames_grad = (grad_resid_one + back).astype(bf)
    return (
        frames_out[None],
        frames_grad[None],
        shares[8][None],
        shares[6][:, :3],
        shares[6][:, 3:6],
        shares[0],
        shares[1],
        shares[2],
        shares[3],
        shares[4],
        shares[5].reshape(-1, D),
    )


def solution(mesh):
    return jax.shard_map(
        fast_body if dict(mesh.shape) == {"dp": 8, "seq": 4} else generic_body,
        mesh=mesh,
        in_specs=(
            P("dp", "seq", None),
            P("dp", None),
            P("dp", None, None),
            P("dp", None),
            P(("dp", "seq"), None),
            P(("dp", "seq"), None),
            P(("dp", "seq"), None),
            P(("dp", "seq"), None),
            P(("dp", "seq"), None),
            P(("dp", "seq"), None),
            P(("dp", "seq"), None),
            P(("dp", "seq"), None),
            P("dp", "seq", None),
        ),
        out_specs=(
            P("dp", "seq", None),
            P("dp", "seq", None),
            P("dp", "seq", None),
            P(("dp", "seq"), None),
            P(("dp", "seq"), None),
            P(("dp", "seq"), None),
            P(("dp", "seq"), None),
            P(("dp", "seq"), None),
            P(("dp", "seq"), None),
            P(("dp", "seq"), None),
            P(("dp", "seq"), None),
        ),
        check_vma=False,
    )
```

```python
import jax
import jax.numpy as jnp
from jax import lax
from jax.experimental import pallas as pl
from jax.experimental.pallas import tpu as pltpu
from jax.sharding import PartitionSpec as P

D = 1024
HEADS = 16
HEAD_DIM = 64
TEXT_LEN = 64


def layer_norm(values, gain, bias):
    center = values - jnp.mean(values, axis=-1, keepdims=True)
    spread = jnp.mean(center * center, axis=-1, keepdims=True)
    return center * lax.rsqrt(spread + 1e-05) * gain + bias


def norm_back(values, gain, bias, upstream):
    unused_value, pullback = jax.vjp(layer_norm, values, gain, bias)
    return pullback(upstream)


def exact_gelu(values):
    return jax.nn.gelu(values, approximate=False)


def split_heads(values):
    return values.reshape(values.shape[0], HEADS, HEAD_DIM)


def text_segments(text_len):
    bounds = jnp.cumsum(text_len, axis=1)
    positions = jnp.arange(TEXT_LEN, dtype=jnp.int32)
    return jnp.sum((positions[None, :, None] >= bounds[:, None, :]).astype(jnp.int32), axis=2)


def self_allowed(local_seg, full_seg, offset):
    row_pos = offset + jnp.arange(local_seg.shape[0], dtype=jnp.int32)
    col_pos = jnp.arange(full_seg.shape[0], dtype=jnp.int32)
    return (row_pos[:, None] >= col_pos[None, :]) & (local_seg[:, None] == full_seg[None, :])


def masked_scores(queries, keys_in, allowed):
    factor = HEAD_DIM ** (-0.5)
    scores = (
        jnp.einsum(
            "qhe,khe->hqk",
            split_heads(queries),
            split_heads(keys_in),
            preferred_element_type=jnp.float32,
        )
        * factor
    )
    return jnp.where(allowed[None], scores, -1e30)


def attend(queries, keys_in, values, allowed):
    scores = masked_scores(queries, keys_in, allowed)
    highest = jnp.max(scores, axis=-1, keepdims=True)
    powered = jnp.exp(scores - highest)
    totals = jnp.sum(powered, axis=-1, keepdims=True)
    weights = (powered / totals).astype(jnp.bfloat16)
    context = jnp.einsum(
        "hqk,khe->qhe", weights, split_heads(values), preferred_element_type=jnp.float32
    )
    return (context.reshape(queries.shape[0], -1), highest + jnp.log(totals))


def attend_back(queries, keys_in, values, allowed, logsum, upstream):
    factor = HEAD_DIM ** (-0.5)
    probs_full = jnp.exp(masked_scores(queries, keys_in, allowed) - logsum)
    grad_heads = split_heads(upstream)
    grad_probs = jnp.einsum(
        "qhe,khe->hqk", grad_heads, split_heads(values), preferred_element_type=jnp.float32
    )
    row_inner = jnp.sum(probs_full * grad_probs, axis=-1, keepdims=True)
    grad_scores = (probs_full * (grad_probs - row_inner)).astype(jnp.bfloat16)
    grad_queries = (
        jnp.einsum(
            "hqk,khe->qhe", grad_scores, split_heads(keys_in), preferred_element_type=jnp.float32
        )
        * factor
    )
    grad_keys = (
        jnp.einsum(
            "hqk,qhe->khe", grad_scores, split_heads(queries), preferred_element_type=jnp.float32
        )
        * factor
    )
    grad_values = jnp.einsum(
        "hqk,qhe->khe",
        probs_full.astype(jnp.bfloat16),
        grad_heads,
        preferred_element_type=jnp.float32,
    )
    return (
        grad_queries.reshape(queries.shape[0], -1),
        grad_keys.reshape(keys_in.shape[0], -1),
        grad_values.reshape(values.shape[0], -1),
    )


F32, BF16 = jnp.float32, jnp.bfloat16
MESH = pl.DeviceIdType.MESH
VMEM_BYTES = 64 * 2**20
BLOCK = 256


def place():
    dp, seq = lax.axis_index("dp"), lax.axis_index("seq")
    return dp // 2, lax.rem(dp, 2), seq // 2, lax.rem(seq, 2)


def device(z, y, x, c):
    return (z * 2 + y, x * 2 + c)


def greet(z, y, x, c):
    barrier = pltpu.get_barrier_semaphore()
    others = [device(lax.rem(z + k, 4), y, x, c) for k in (1, 2, 3)]
    others += [device(z, 1 - y, x, c), device(z, y, 1 - x, c), device(z, y, x, 1 - c)]
    for other in others:
        pl.semaphore_signal(barrier, inc=1, device_id=other, device_id_type=MESH)
    pl.semaphore_wait(barrier, len(others))


def dot_nn(a, b):
    return jnp.dot(a, b, preferred_element_type=F32)


def dot_nt(a, b):
    return lax.dot_general(a, b, (((1,), (1,)), ((), ())), preferred_element_type=F32)


def dot_tn(a, b):
    return lax.dot_general(a, b, (((0,), (0,)), ((), ())), preferred_element_type=F32)


def tiles(count, size):
    def run(step):
        def one(i, carry):
            step(i, pl.ds(pl.multiple_of(i * size, size), size))
            return carry

        lax.fori_loop(0, count, one, 0)

    return run


def normalize(block, gain, bias):
    center = block - jnp.mean(block, axis=-1, keepdims=True)
    spread = jnp.mean(center * center, axis=-1, keepdims=True)
    return center * lax.rsqrt(spread + 1e-05) * gain + bias


def stack_heads(dst, src, group, factor):
    rows = src.shape[0]
    part = src[:, group * 256 : group * 256 + 256]
    if factor != 1.0:
        part = part * jnp.asarray(factor, part.dtype)
    head = lax.broadcasted_iota(jnp.int32, part.shape, 1) // HEAD_DIM
    for h in range(4):
        dst[h * rows : (h + 1) * rows, :] = jnp.where(head == h, part, jnp.zeros_like(part))


def unstack_heads(wide, rows):
    parts = [wide[h * 64 : (h + 1) * 64, h * rows : (h + 1) * rows] for h in range(4)]
    return jnp.concatenate(parts, axis=0).T


def attend_group(group, q, k, v, bias, stacked, scores, total, context, logsum, between):
    rows, keys = q.shape[0], k.shape[0]
    size = min(BLOCK, keys)
    cols = slice(group * 256, group * 256 + 256)
    stack_heads(stacked, q, group, HEAD_DIM**-0.5)

    def score(i, highest):
        at = pl.ds(pl.multiple_of(i * size, size), size)
        s = dot_nt(k[at, cols], stacked[...]) + bias[at, :].astype(F32)
        scores[at, :] = s
        return jnp.maximum(highest, jnp.max(s, axis=0, keepdims=True))

    highest = lax.fori_loop(0, keys // size, score, jnp.full((1, 4 * rows), -3e38, F32))
    between()
    total[...] = jnp.zeros_like(total)

    def weigh(i, summed):
        at = pl.ds(pl.multiple_of(i * size, size), size)
        p = jnp.exp(scores[at, :] - highest)
        total[...] += dot_tn(v[at, cols], p.astype(BF16))
        return summed + jnp.sum(p, axis=0, keepdims=True)

    summed = lax.fori_loop(0, keys // size, weigh, jnp.zeros((1, 4 * rows), F32))
    logsum[group : group + 1, :] = highest + jnp.log(summed)
    context[:, cols] = unstack_heads(total[...] / summed, rows).astype(BF16)


class Gathering:
    def __init__(self, at, units, send_sem, recv_sem, own_sem):
        self.at, self.units, self.n = at, units, len(units)
        self.send_sem, self.recv_sem, self.own_sem = send_sem, recv_sem, own_sem
        self.sent, self.step = [], 0
        z, y, x, c = at
        self.to_x, self.to_y, self.to_c = device(z, y, 1 - x, c), device(z, 1 - y, x, c), device(z, y, x, 1 - c)

    def copy(self, src, dst, u, k, dev):
        return pltpu.make_async_remote_copy(
            src_ref=src,
            dst_ref=dst,
            send_sem=self.send_sem.at[u, k],
            recv_sem=self.recv_sem.at[u, k],
            device_id=dev,
            device_id_type=MESH,
        )

    def go(self, copy):
        copy.start()
        self.sent.append(copy)

    def same(self, u, k, dev, *spot):
        view = self.units[u][1](*spot)
        return self.copy(view, view, u, k, dev)

    def across(self, u, k):
        z, y, x, c = self.at
        src, dst = self.units[u][0], self.units[u][1](z, y, x, c)
        return self.copy(src, dst, u, k - 1, device(lax.rem(z + k, 4), y, x, c))

    def own(self, u):
        return pltpu.make_async_copy(self.units[u][0], self.units[u][1](*self.at), self.own_sem.at[u])

    def first(self, u):
        if u < self.n:
            self.own(u).start()
            for k in (1, 2, 3):
                self.go(self.across(u, k))

    def pump(self):
        z, y, x, c = self.at
        every, low, high = pl.ds(0, 4), pl.ds(0, 2), pl.ds(2, 2)
        t, n, same, go = self.step, self.n, self.same, self.go
        if t >= n + 2:
            return
        self.step += 1
        if t < n:
            for k in (1, 2, 3):
                self.across(t, k).wait_recv()
            self.own(t).wait()
            go(same(t, 3, self.to_x, every, y, x, c))
            go(same(t, 4, self.to_y, every, y, x, c))
            go(same(t, 5, self.to_c, every, y, x, c))
            self.first(t + 3)
        u = t - 1
        if 0 <= u < n:
            same(u, 3, self.to_x, every, y, 1 - x, c).wait_recv()
            go(same(u, 6, self.to_y, low, y, 1 - x, c))
            go(same(u, 7, self.to_c, every, y, 1 - x, c))
            same(u, 4, self.to_y, every, 1 - y, x, c).wait_recv()
            go(same(u, 8, self.to_x, high, 1 - y, x, c))
            go(same(u, 9, self.to_c, every, 1 - y, x, c))
        u = t - 2
        if 0 <= u < n:
            same(u, 6, self.to_y, low, 1 - y, 1 - x, c).wait_recv()
            go(same(u, 10, self.to_c, low, 1 - y, 1 - x, c))
            same(u, 8, self.to_x, high, 1 - y, 1 - x, c).wait_recv()
            go(same(u, 11, self.to_c, high, 1 - y, 1 - x, c))

    def need(self, u):
        z, y, x, c = self.at
        every, low, high = pl.ds(0, 4), pl.ds(0, 2), pl.ds(2, 2)
        while self.step <= u + 2:
            self.pump()
        self.same(u, 5, self.to_c, every, y, x, 1 - c).wait_recv()
        self.same(u, 7, self.to_c, every, y, 1 - x, 1 - c).wait_recv()
        self.same(u, 9, self.to_c, every, 1 - y, x, 1 - c).wait_recv()
        self.same(u, 10, self.to_c, low, 1 - y, 1 - x, 1 - c).wait_recv()
        self.same(u, 11, self.to_c, high, 1 - y, 1 - x, 1 - c).wait_recv()


FORWARD_IN = ("frames", "norms", "sqkv", "sout", "cqkv", "cout", "up", "down", "cot", "text", "seg_rows", "seg_cols", "text_len")
FORWARD_OUT = ("norms", "sqkv", "sout", "cqkv", "cout", "up", "down", "gb", "frames", "normed", "q", "k", "v", "ctx", "lse", "r1", "nc", "cq", "ck", "cv", "cctx", "clse", "r2", "out", "dn", "ddown", "dup")
SAVED = ("gb", "frames", "normed", "q", "k", "v", "ctx", "lse", "r1", "nc", "cq", "ck", "cv", "cctx", "clse", "r2", "out", "dn")


def forward_kernel(i, o, s):
    at = place()
    z, y, x, c = at
    seq = x * 2 + c
    units = [(i["norms"], lambda zz, yy, xx, cc: o["norms"].at[zz, yy, xx, cc])]

    def columns(name, count):
        for k in range(count):
            cut = pl.ds(k * 1024, 1024)
            units.append(
                (
                    i[name].at[:, cut],
                    lambda zz, yy, xx, cc, cut=cut: o[name].at[zz, yy, xx, cc, :, cut],
                )
            )

    columns("sqkv", 3)
    columns("sout", 1)
    columns("cqkv", 3)
    columns("cout", 1)
    columns("up", 4)
    for k in range(4):
        units.append(
            (i["down"].at[k], lambda zz, yy, xx, cc, k=k: o["down"].at[zz, yy, xx, cc, k])
        )
    comm = Gathering(at, units, s["send"], s["recv"], s["own"])
    greet(*at)
    fr = s["frames"]
    f = comm.n

    def share(k, dev, xx, cc):
        view = fr.at[xx, cc]
        return comm.copy(view, view, f, k, dev)

    own_frames = pltpu.make_async_copy(i["frames"], fr.at[x, c], s["own"].at[f])
    own_frames.start()
    cot_copy = pltpu.make_async_copy(i["cot"], s["cot"], s["own"].at[f + 1])
    cot_copy.start()
    text_copy = pltpu.make_async_copy(i["text"], s["text"], s["own"].at[f + 2])
    text_copy.start()
    for u in range(3):
        comm.first(u)
    own_frames.wait()
    comm.go(share(0, comm.to_x, x, c))
    comm.go(share(1, comm.to_c, x, c))

    saves = []

    def save(name, src):
        copy = pltpu.make_async_copy(src, o[name], s["save"].at[len(saves)])
        copy.start()
        saves.append(copy)

    seg_row = i["seg_rows"][seq]

    def mask(b, rows):
        key = lax.broadcasted_iota(jnp.int32, (64, 320), 0) + b * 64
        query = lax.broadcasted_iota(jnp.int32, (64, 320), 1) + seq * 320
        seen = (key <= query) & (i["seg_cols"][rows] == seg_row)
        block = jnp.where(seen, 0.0, -1e30).astype(F32)
        s["bias"][rows, :] = jnp.concatenate([block] * 4, axis=1).astype(BF16)

    tiles(20, 64)(mask)
    slot = lax.broadcasted_iota(jnp.int32, (TEXT_LEN, 320), 0)
    text_seg = jnp.zeros((TEXT_LEN, 320), jnp.int32)
    bound = jnp.int32(0)
    for k in range(4):
        bound = bound + i["text_len"][0, k]
        text_seg = text_seg + (slot >= bound).astype(jnp.int32)
    block = jnp.where(text_seg == seg_row, 0.0, -1e30).astype(F32)
    s["cbias"][...] = jnp.concatenate([block] * 4, axis=1).astype(BF16)

    def weight(u, where):
        comm.need(u)
        src = units[u][1](pl.ds(0, 4), pl.ds(0, 2), pl.ds(0, 2), pl.ds(0, 2))
        dst = s["w"].at[where]
        copy = pltpu.make_async_copy(src, dst.reshape(4, 2, 2, 2, 32, 1024), s["load"].at[u])
        copy.start()
        copy.wait()
        return dst

    def norm(dst, src_block, k, count):
        gain, bias = s["gb"][k : k + 1, :], s["gb"][3 + k : 4 + k, :]

        def one(b, rows):
            dst[rows, :] = normalize(src_block(b, rows), gain, bias).astype(BF16)

        tiles(count, 64)(one)

    share(0, comm.to_x, 1 - x, c).wait_recv()
    comm.go(share(2, comm.to_c, 1 - x, c))
    comm.need(0)
    copy = pltpu.make_async_copy(o["norms"], s["norms"].reshape(4, 2, 2, 2, 32, 128), s["load"].at[0])
    copy.start()
    copy.wait()
    s["gb"][...] = s["norms"][...].astype(F32).T[:8]
    share(1, comm.to_c, x, 1 - c).wait_recv()
    share(2, comm.to_c, 1 - x, 1 - c).wait_recv()
    normed = s["normed"]

    def frame_block(b, rows):
        return fr[b // 10, lax.rem(b // 5, 2), pl.ds(pl.multiple_of(lax.rem(b, 5) * 64, 64), 64), :].astype(F32)

    norm(normed, frame_block, 0, 20)
    save("gb", s["gb"])
    save("frames", fr)
    save("normed", normed)

    mine = pl.ds(pl.multiple_of(seq * 320, 64), 320)

    def project(dst, src, w, rows):
        def one(n, cut):
            dst[:, cut] = dot_nn(src[rows, :], w[:, cut]).astype(BF16)

        tiles(4, 256)(one)

    def project_all(dst, w):
        def one(b, rows):
            def two(n, cut):
                dst[rows, cut] = dot_nn(normed[rows, :], w[:, cut]).astype(BF16)

            tiles(4, 256)(two)

        tiles(4, 320)(one)

    every_row = pl.ds(0, 320)
    q, k, v = s["q"], s["k"], s["v"]
    project(q, normed, weight(1, 0), mine)
    project_all(k, weight(2, 1))
    project_all(v, weight(3, 2))
    save("q", q)
    save("k", k)
    save("v", v)
    for g in range(4):
        attend_group(
            g, q, k, v, s["bias"], s["stacked"], s["scores"], s["total"], s["ctx"], s["lse"], comm.pump
        )
    save("ctx", s["ctx"])
    save("lse", s["lse"])

    def add_project(dst, base, src, w):
        def one(n, cut):
            dst[:, cut] = base(cut) + dot_nn(src[...], w[:, cut])

        tiles(4, 256)(one)

    add_project(s["r1"], lambda cut: fr[x, c, :, cut].astype(F32), s["ctx"], weight(4, 0))
    save("r1", s["r1"])
    norm(s["nc"], lambda b, rows: s["r1"][rows, :], 1, 5)
    save("nc", s["nc"])
    project(s["cq"], s["nc"], weight(5, 1), every_row)
    save("cq", s["cq"])
    text_copy.wait()
    text_rows = pl.ds(0, TEXT_LEN)
    project(s["ck"], s["text"], weight(6, 2), text_rows)
    project(s["cv"], s["text"], weight(7, 0), text_rows)
    save("ck", s["ck"])
    save("cv", s["cv"])
    for g in range(4):
        attend_group(
            g,
            s["cq"],
            s["ck"],
            s["cv"],
            s["cbias"],
            s["stacked"],
            s["scores"],
            s["total"],
            s["cctx"],
            s["clse"],
            lambda: None,
        )
    save("cctx", s["cctx"])
    save("clse", s["clse"])
    comm.pump()
    add_project(s["r2"], lambda cut: s["r1"][:, cut], s["cctx"], weight(8, 1))
    save("r2", s["r2"])
    norm(s["nf"], lambda b, rows: s["r2"][rows, :], 2, 5)
    cot_copy.wait()
    act, slope, nf, cot = s["act"], s["scores"], s["nf"], s["cot"]
    grads = []

    def gradient(name, j, left, right):
        m = len(grads)
        if m >= 2:
            grads[m - 2].wait()
        stage = s["stage"].at[m % 2]

        def one(n, cut):
            stage[:, cut] = dot_tn(left(), right(cut)).astype(BF16)

        tiles(4, 256)(one)
        copy = pltpu.make_async_copy(stage, o[name].at[j], s["grad"].at[m])
        copy.start()
        grads.append(copy)

    for j in range(4):
        w = weight(9 + j, 3 + j)

        def one(n, cut):
            h = dot_nn(nf[...], w[:, cut])
            below = 0.5 * (1.0 + lax.erf(h * 0.7071067811865476))
            act[j, :, cut] = (h * below).astype(BF16)
            slope[j * 320 : (j + 1) * 320, cut] = below + h * jnp.exp(-0.5 * h * h) * 0.3989422804014327

        tiles(4, 256)(one)
        gradient("ddown", j, lambda: act[j], lambda cut: cot[:, cut])
    for j in range(4):
        w, w_up = weight(13 + j, j % 3), s["w"].at[3 + j]

        def back(n, rows):
            g = dot_nt(cot[...], w[rows, :]) * slope[j * 320 : (j + 1) * 320, rows]
            s["gpre"][:, rows] = g.astype(BF16)

        tiles(4, 256)(back)
        gradient("dup", j, lambda: nf[...], lambda cut: s["gpre"][:, cut])

        def onward(n, rows):
            add = dot_nt(s["gpre"][...], w_up[rows, :])
            s["dn"][:, rows] = add if j == 0 else s["dn"][:, rows] + add
            more = dot_nn(act[j], w[:, rows])
            s["r2"][:, rows] = s["r2"][:, rows] + more

        if j == 0:
            for copy in saves:
                copy.wait()
            saves.clear()
        tiles(4, 256)(onward)
    s["out"][...] = s["r2"][...].astype(BF16)
    saves_base = 17
    for m, name in enumerate(("out", "dn")):
        copy = pltpu.make_async_copy(s[name], o[name], s["save"].at[saves_base + m])
        copy.start()
        saves.append(copy)
    for copy in saves + grads[-2:]:
        copy.wait()
    for copy in comm.sent:
        copy.wait_send()


def run_forward_kernel(args):
    S, V, D_SEM = jax.ShapeDtypeStruct, pltpu.VMEM, pltpu.SemaphoreType.DMA
    whole = {n: (4, 2, 2, 2) + args[n].shape for n in ("norms", "sqkv", "sout", "cqkv", "cout", "up", "down")}
    shapes = {n: S(d, BF16) for n, d in whole.items()}
    rows = (320, 1024)
    scratch = dict(
        send=D_SEM((18, 12)), recv=D_SEM((18, 12)), own=D_SEM((20,)), save=D_SEM((20,)), load=D_SEM((17,)), grad=D_SEM((8,)),
        frames=V((2, 2, 320, 1024), BF16), cot=V(rows, BF16), text=V((64, 1024), BF16), norms=V((1024, 128), BF16), gb=V((8, 1024), F32),
        bias=V((1280, 1280), BF16), cbias=V((64, 1280), BF16), w=V((7, 1024, 1024), BF16), normed=V((1280, 1024), BF16),
        q=V(rows, BF16), k=V((1280, 1024), BF16), v=V((1280, 1024), BF16), stacked=V((1280, 256), BF16), scores=V((1280, 1280), F32),
        total=V((256, 1280), F32), ctx=V(rows, BF16), lse=V((4, 1280), F32), r1=V(rows, F32), nc=V(rows, BF16), cq=V(rows, BF16),
        ck=V((64, 1024), BF16), cv=V((64, 1024), BF16), cctx=V(rows, BF16), clse=V((4, 1280), F32), r2=V(rows, F32), nf=V(rows, BF16),
        act=V((4, 320, 1024), BF16), gpre=V(rows, BF16), dn=V(rows, F32), out=V(rows, BF16), stage=V((2, 1024, 1024), BF16),
    )
    for n in SAVED:
        shapes[n] = S(scratch[n].shape, scratch[n].dtype)
    shapes["ddown"] = shapes["dup"] = S((4, 1024, 1024), BF16)
    in_spec = {n: pl.BlockSpec(memory_space=pl.ANY) for n in FORWARD_IN}
    for n in ("seg_rows", "seg_cols"):
        in_spec[n] = pl.BlockSpec(memory_space=pltpu.VMEM)
    in_spec["text_len"] = pl.BlockSpec(memory_space=pltpu.SMEM)

    def kernel(*refs):
        a, b = len(FORWARD_IN), len(FORWARD_IN) + len(FORWARD_OUT)
        forward_kernel(
            dict(zip(FORWARD_IN, refs[:a])),
            dict(zip(FORWARD_OUT, refs[a:b])),
            dict(zip(scratch, refs[b:])),
        )

    outs = pl.pallas_call(
        kernel,
        out_shape=[shapes[n] for n in FORWARD_OUT],
        in_specs=[in_spec[n] for n in FORWARD_IN],
        out_specs=[pl.BlockSpec(memory_space=pl.ANY)] * len(FORWARD_OUT),
        scratch_shapes=list(scratch.values()),
        compiler_params=pltpu.CompilerParams(
            collective_id=0, has_side_effects=True, vmem_limit_bytes=VMEM_BYTES
        ),
    )(*[args[n] for n in FORWARD_IN])
    return dict(zip(FORWARD_OUT, outs))


def attend_back_group(group, q, k, v, up, context, bias, logsum, stacked_q, stacked_g, total, grad_q, between):
    rows, keys = q.shape[0], k.shape[0]
    size = min(BLOCK, keys)
    cols = slice(group * 256, group * 256 + 256)
    stack_heads(stacked_q, q, group, HEAD_DIM**-0.5)
    stack_heads(stacked_g, up, group, 1.0)
    four = jnp.concatenate([context[:, cols].astype(F32)] * 4, axis=0)
    inner = lax.dot_general(
        jnp.ones((8, 256), F32),
        stacked_g[...].astype(F32) * four,
        (((1,), (1,)), ((), ())),
        precision=lax.Precision.HIGHEST,
        preferred_element_type=F32,
    )[:1]
    shift = logsum[group : group + 1, :]
    total[...] = jnp.zeros_like(total)

    def step(i, carry):
        at = pl.ds(pl.multiple_of(i * size, size), size)
        key, value = k[at, cols], v[at, cols]
        half = bias[at, :].astype(F32)
        s = dot_nt(key, stacked_q[...]) + jnp.concatenate([half, half], axis=1)
        p = jnp.exp(s - shift)
        ds = (p * (dot_nt(value, stacked_g[...]) - inner)).astype(BF16)
        v[at, cols] = dot_nn(p.astype(BF16), stacked_g[...]).astype(BF16)
        k[at, cols] = dot_nn(ds, stacked_q[...]).astype(BF16)
        total[...] += dot_tn(key, ds)
        return carry

    lax.fori_loop(0, keys // size, step, 0)
    between()
    grad_q[:, cols] = (unstack_heads(total[...], rows) * HEAD_DIM**-0.5).astype(BF16)


class Scattering:
    def __init__(self, at, i, o, s):
        self.at, self.o, self.s = at, o, s
        self.n, self.begun, self.done1, self.done2, self.done3 = 17, 0, 0, 0, 0
        self.sent, self.source = {}, {}
        z, y, x, c = at
        self.to_x, self.to_y, self.to_c = device(z, y, 1 - x, c), device(z, 1 - y, x, c), device(z, y, x, 1 - c)

    def copy(self, src, dst, u, k, dev):
        return pltpu.make_async_remote_copy(
            src_ref=src,
            dst_ref=dst,
            send_sem=self.s["send"].at[u, k],
            recv_sem=self.s["recv"].at[u, k],
            device_id=dev,
            device_id_type=MESH,
        )

    def go(self, u, k, copy):
        copy.start()
        self.sent[u, k] = copy

    def left(self, u, k):
        copy = self.sent.pop((u, k), None)
        if copy is not None:
            copy.wait_send()

    def buffer(self, name, u):
        if u == 16:
            return self.s["n" + name]
        return self.s[name].at[u % 4 if name in ("sum", "core") else u]

    def from_core(self, u, src):
        return self.copy(src, self.buffer("core", u), u, 0, self.to_c)

    def first_x(self, u):
        return self.copy(self.buffer("sum", u).at[0:2, :, 1 - self.at[2]], self.buffer("xr", u), u, 1, self.to_x)

    def first_y(self, u):
        return self.copy(self.buffer("sum", u).at[2:4, 1 - self.at[1]], self.buffer("yr", u), u, 2, self.to_y)

    def second_y(self, u):
        return self.copy(self.buffer("xr", u).at[:, 1 - self.at[1]], self.buffer("cc", u).at[0:2], u, 3, self.to_y)

    def second_x(self, u):
        return self.copy(self.buffer("yr", u).at[:, 1 - self.at[2]], self.buffer("cc", u).at[2:4], u, 4, self.to_x)

    def final(self, u):
        return self.o["nfin"] if u == 16 else self.o["fin"].at[u]

    def across(self, u, k):
        z, y, x, c = self.at
        to = lax.rem(z + k, 4)
        return self.copy(self.buffer("cc", u).at[to], self.final(u).at[k - 1], u, 4 + k, device(to, y, x, c))

    def keep(self, u):
        return pltpu.make_async_copy(self.buffer("cc", u).at[self.at[0]], self.final(u).at[3], self.s["keep"].at[u])

    def load(self, u):
        return pltpu.make_async_copy(self.source[u].at[:, :, :, self.at[3]], self.buffer("sum", u), self.s["own"].at[u])

    def begin(self, u, source, in_hbm):
        assert u == self.begun
        while self.done2 < u - 3 and u < 16:
            self.pump()
        self.begun += 1
        self.source[u] = source
        if 4 <= u < 16:
            pl.semaphore_wait(self.s["free"], 1)
        if in_hbm:
            self.left(u - 4, 1)
            self.left(u - 4, 2)
            self.load(u).start()
        self.go(u, 0, self.from_core(u, source.at[:, :, :, 1 - self.at[3]]))

    def pump(self):
        z, y, x, c = self.at
        before1, before2 = self.done1, self.done2
        if self.done1 < self.begun:
            self.stage1(self.done1)
            self.done1 += 1
        if self.done2 < (before1 if self.done1 > before1 else self.done1):
            self.stage2(self.done2)
            self.done2 += 1
        if self.done3 < (before2 if self.done2 > before2 else self.done2):
            self.stage3(self.done3)
            self.done3 += 1

    def stage1(self, u):
        z, y, x, c = self.at
        total, got, source = self.buffer("sum", u), self.buffer("core", u), self.source[u]
        if u < 8:
            self.load(u).wait()
        elif u < 16:
            self.left(u - 4, 1)
            self.left(u - 4, 2)
        self.from_core(u, source.at[:, :, :, 1 - c]).wait_recv()

        def add(j, carry):
            at = (j // 4, lax.rem(j // 2, 2), lax.rem(j, 2))
            own = total[at] if u < 8 else source[at + (c,)]
            total[at] = own + got[at]
            return carry

        lax.fori_loop(0, 16, add, 0)
        if u < 12:
            pl.semaphore_signal(self.s["free"], inc=1, device_id=self.to_c, device_id_type=MESH)
        self.go(u, 1, self.first_x(u))
        self.go(u, 2, self.first_y(u))

    def stage2(self, u):
        z, y, x, c = self.at
        total, xr, yr = self.buffer("sum", u), self.buffer("xr", u), self.buffer("yr", u)
        self.first_x(u).wait_recv()

        def add_x(j, carry):
            a, b = j // 2, lax.rem(j, 2)
            xr[a, b] = xr[a, b] + total[a, b, x]
            return carry

        lax.fori_loop(0, 4, add_x, 0)
        self.go(u, 3, self.second_y(u))
        self.first_y(u).wait_recv()

        def add_y(j, carry):
            a, b = j // 2, lax.rem(j, 2)
            yr[a, b] = yr[a, b] + total[2 + a, y, b]
            return carry

        lax.fori_loop(0, 4, add_y, 0)
        self.go(u, 4, self.second_x(u))

    def stage3(self, u):
        z, y, x, c = self.at
        xr, yr, cc = self.buffer("xr", u), self.buffer("yr", u), self.buffer("cc", u)
        self.second_y(u).wait_recv()
        for a in range(2):
            cc[a] = cc[a] + xr[a, y]
        self.second_x(u).wait_recv()
        for a in range(2):
            cc[2 + a] = cc[2 + a] + yr[a, x]
        for k in (1, 2, 3):
            self.go(u, 4 + k, self.across(u, k))
        self.keep(u).start()

    def finish(self):
        while self.done3 < self.n:
            self.pump()
        for u in range(self.n):
            for k in (1, 2, 3):
                self.across(u, k).wait_recv()
            self.keep(u).wait()
        for key in list(self.sent):
            self.left(*key)


BACKWARD_IN = tuple(
    (
        "ddown",
        "dup",
        "dn",
        "cot",
        "gb",
        "r2",
        "r1",
        "cctx",
        "ctx",
        "cq",
        "ck",
        "cv",
        "clse",
        "nc",
        "text",
        "q",
        "k",
        "v",
        "lse",
        "normed",
        "frames",
        "cout",
        "cqkv",
        "sout",
        "sqkv",
        "seg_rows",
        "seg_cols",
        "text_len",
    )
)
BACKWARD_OUT = ("fin", "nfin", "fmine", "tmine", "gr")


def backward_kernel(i, o, s):
    at = place()
    z, y, x, c = at
    seq = x * 2 + c
    comm = Scattering(at, i, o, s)
    greet(*at)
    six = (4, 2, 2, 2, 32, 1024)
    waits = {}

    def fetch(name, dst, slot):
        copy = pltpu.make_async_copy(i[name], dst, s["fetch"].at[slot])
        copy.start()
        waits[name] = copy

    def have(*names):
        for name in names:
            waits.pop(name).wait()

    def weight(name, k, slot):
        src = i[name].at[:, :, :, :, :, pl.ds(k * 1024, 1024)]
        copy = pltpu.make_async_copy(src, s["w"].at[slot].reshape(*six), s["load"].at[slot])
        copy.start()
        waits["w", slot] = copy

    def loaded(slot):
        waits.pop(("w", slot)).wait()
        return s["w"].at[slot]

    fetch("gb", s["gb"], 0)
    fetch("r2", s["r"], 1)
    fetch("dn", s["g"], 2)
    fetch("cot", s["cot"], 3)
    fetch("cctx", s["ctx"], 4)
    fetch("cq", s["q"], 5)
    fetch("ck", s["ck"], 6)
    fetch("cv", s["cv"], 7)
    fetch("clse", s["clse"], 8)
    fetch("nc", s["nc"], 9)
    fetch("text", s["text"], 10)
    weight("cout", 0, 0)
    weight("cqkv", 0, 1)
    comm.begin(0, i["ddown"].at[0], True)
    comm.begin(1, i["ddown"].at[1], True)
    fetch("k", s["k"], 11)
    fetch("v", s["v"], 12)
    fetch("lse", s["lse"], 13)
    fetch("normed", s["normed"], 14)

    def ffn(u):
        comm.begin(u, i["ddown" if u < 4 else "dup"].at[u % 4], True)

    def advance():
        comm.pump()
        if comm.begun < 8 and comm.begun < comm.done1 + 2:
            ffn(comm.begun)

    seg_row = i["seg_rows"][seq]

    def mask(b, rows):
        key = lax.broadcasted_iota(jnp.int32, (64, 320), 0) + b * 64
        query = lax.broadcasted_iota(jnp.int32, (64, 320), 1) + seq * 320
        seen = (key <= query) & (i["seg_cols"][rows] == seg_row)
        block = jnp.where(seen, 0.0, -1e30).astype(F32)
        s["bias"][rows, :] = jnp.concatenate([block] * 2, axis=1).astype(BF16)

    tiles(20, 64)(mask)
    slot = lax.broadcasted_iota(jnp.int32, (TEXT_LEN, 320), 0)
    text_seg = jnp.zeros((TEXT_LEN, 320), jnp.int32)
    bound = jnp.int32(0)
    for k in range(4):
        bound = bound + i["text_len"][0, k]
        text_seg = text_seg + (slot >= bound).astype(jnp.int32)
    block = jnp.where(text_seg == seg_row, 0.0, -1e30).astype(F32)
    s["cbias"][...] = jnp.concatenate([block] * 2, axis=1).astype(BF16)

    s["ng"][...] = jnp.zeros_like(s["ng"])
    have("gb")

    def norm_back(values, upstream, k, put):
        gain = s["gb"][k : k + 1, :]
        center = values - jnp.mean(values, axis=-1, keepdims=True)
        scale = lax.rsqrt(jnp.mean(center * center, axis=-1, keepdims=True) + 1e-05)
        hat = center * scale
        s["ng"][k : k + 1, :] += jnp.sum(upstream * hat, axis=0, keepdims=True)
        s["ng"][3 + k : 4 + k, :] += jnp.sum(upstream, axis=0, keepdims=True)
        if put is not None:
            h = upstream * gain
            put((h - jnp.mean(h, axis=-1, keepdims=True) - hat * jnp.mean(h * hat, axis=-1, keepdims=True)) * scale)

    gr, branch, g = s["gr"], s["branch"], s["g"]
    have("r2", "dn", "cot")

    def back_two(b, rows):
        def put(grad):
            total = s["cot"][rows, :].astype(F32) + grad
            gr[rows, :] = total
            branch[rows, :] = total.astype(BF16)

        norm_back(s["r"][rows, :], g[rows, :], 2, put)

    tiles(5, 64)(back_two)
    fetch("r1", s["r"], 1)
    advance()

    def gradient(u, left, right):
        while comm.done1 < u - 1:
            comm.pump()
        comm.left(u - 2, 0)
        dw = s["dw"].at[u % 2]

        def one(n, cut):
            dw[:, cut] = dot_tn(left(), right(cut)).astype(BF16)

        tiles(4, 256)(one)

        def send():
            comm.begin(u, dw.reshape(*six), False)

        return send

    def through(dst, src, w, put=None):
        def one(n, rows):
            value = dot_nt(src[...], w[rows, :])
            dst[:, rows] = value.astype(dst.dtype)

        tiles(4, 256)(one)

    w = loaded(0)
    through(s["up"], branch, w)
    weight("cqkv", 1, 0)
    weight("cqkv", 2, 2)
    advance()
    have("cctx", "cq", "ck", "cv", "clse")
    for group in range(4):
        attend_back_group(
            group,
            s["q"],
            s["ck"],
            s["cv"],
            s["up"],
            s["ctx"],
            s["cbias"],
            s["clse"],
            s["stacked_q"],
            s["stacked_g"],
            s["total"],
            s["dq"],
            advance if group % 2 else lambda: None,
        )
    fetch("q", s["q"], 5)
    w = loaded(1)
    through(g, s["dq"], w)
    weight("sout", 0, 1)
    s["branch2"][...] = branch[...]
    have("r1")

    def back_one(b, rows):
        def put(grad):
            total = gr[rows, :] + grad
            gr[rows, :] = total
            branch[rows, :] = total.astype(BF16)

        norm_back(s["r"][rows, :], g[rows, :], 1, put)

    tiles(5, 64)(back_one)
    save_gr = pltpu.make_async_copy(gr, o["gr"], s["fetch"].at[16])
    save_gr.start()
    advance()
    w_key, w_value = loaded(0), loaded(2)

    def text_part(n, rows):
        value = dot_nt(s["ck"][...], w_key[rows, :]) + dot_nt(s["cv"][...], w_value[rows, :])
        s["tpart"][:, :, :, rows] = value.astype(BF16).reshape(2, 2, 16, 256)

    tiles(4, 256)(text_part)
    text_core = comm.copy(s["tpart"].at[:, 1 - c], s["tcore"], 17, 0, comm.to_c)
    comm.go(17, 0, text_core)
    weight("sqkv", 0, 0)
    weight("sqkv", 1, 2)
    through(s["up"], branch, loaded(1))
    weight("sqkv", 2, 1)
    advance()
    while comm.begun < 8:
        advance()
    send = gradient(8, lambda: s["ctx"][...], lambda cut: s["branch2"][:, cut])
    send()
    fetch("ctx", s["ctx"], 4)
    text_core.wait_recv()
    s["tsum"][...] = s["tpart"][:, c] + s["tcore"][...]
    text_x = comm.copy(s["tsum"].at[1 - x], o["tmine"].at[1], 17, 1, comm.to_x)
    comm.go(17, 1, text_x)
    text_keep = pltpu.make_async_copy(s["tsum"].at[x], o["tmine"].at[0], s["keep"].at[17])
    text_keep.start()
    have("nc", "text")
    send = gradient(9, lambda: s["nc"][...], lambda cut: s["dq"][:, cut])
    send()
    have("ctx", "q", "k", "v", "lse")
    todo = [
        lambda: gradient(10, lambda: s["text"][...], lambda cut: s["ck"][:, cut])(),
        lambda: gradient(11, lambda: s["text"][...], lambda cut: s["cv"][:, cut])(),
        lambda: gradient(12, lambda: s["ctx"][...], lambda cut: branch[:, cut])(),
        advance,
    ]
    for group in range(4):
        attend_back_group(
            group,
            s["q"],
            s["k"],
            s["v"],
            s["up"],
            s["ctx"],
            s["bias"],
            s["lse"],
            s["stacked_q"],
            s["stacked_g"],
            s["total"],
            s["dq"],
            advance,
        )
        todo[group]()
    have("normed")
    mine = pl.ds(pl.multiple_of(seq * 320, 64), 320)
    wq, wk, wv = loaded(0), loaded(2), loaded(1)

    def frames_part(b, rows):
        block = pltpu.make_async_copy(i["frames"].at[b // 2, lax.rem(b, 2)], s["cot"], s["fetch"].at[15])
        block.start()

        def one(n, cut):
            g[:, cut] = dot_nt(s["k"][rows, :], wk[cut, :]) + dot_nt(s["v"][rows, :], wv[cut, :])

        tiles(4, 256)(one)

        @pl.when(b == seq)
        def _():
            def two(n, cut):
                g[:, cut] = g[:, cut] + dot_nt(s["dq"][...], wq[cut, :])

            tiles(4, 256)(two)

        block.wait()

        def three(r, part):
            norm_back(s["cot"][part, :].astype(F32), g[part, :], 0, None)
            s["fpart"][b // 2, lax.rem(b, 2), part, :] = g[part, :].astype(BF16)

        tiles(5, 64)(three)

    gradient(13, lambda: s["normed"][mine, :], lambda cut: s["dq"][:, cut])()
    advance()
    tiles(4, 320)(frames_part)
    frames_core = comm.copy(s["fpart"].at[:, 1 - c], s["fcore"], 17, 2, comm.to_c)
    comm.go(17, 2, frames_core)
    gradient(14, lambda: s["normed"][...], lambda cut: s["k"][:, cut])()
    advance()
    frames_core.wait_recv()

    def frames_sum(b, carry):
        rows = pl.ds(pl.multiple_of(lax.rem(b, 5) * 64, 64), 64)
        s["fcore"][b // 5, rows] = s["fcore"][b // 5, rows] + s["fpart"][b // 5, c, rows]
        return carry

    lax.fori_loop(0, 10, frames_sum, 0)
    frames_x = comm.copy(s["fcore"].at[1 - x], o["fmine"].at[1], 17, 3, comm.to_x)
    comm.go(17, 3, frames_x)
    frames_keep = pltpu.make_async_copy(s["fcore"].at[x], o["fmine"].at[0], s["keep"].at[18])
    frames_keep.start()
    gradient(15, lambda: s["normed"][...], lambda cut: s["v"][:, cut])()
    advance()
    flat = jnp.concatenate([s["ng"][...], jnp.zeros((120, 1024), F32)], axis=0).T
    s["nown"][...] = flat.reshape(4, 2, 2, 2, 32, 128)
    comm.begin(16, s["nown"], False)
    comm.finish()
    text_x.wait_recv()
    frames_x.wait_recv()
    text_keep.wait()
    frames_keep.wait()
    save_gr.wait()


def run_backward_kernel(args):
    S, V, D_SEM = jax.ShapeDtypeStruct, pltpu.VMEM, pltpu.SemaphoreType.DMA
    rows, block = (320, 1024), (32, 1024)
    shapes = dict(
        fin=S((16, 4) + block, BF16), nfin=S((4, 32, 128), F32), fmine=S((2,) + rows, BF16), tmine=S((2, 16, 1024), BF16), gr=S(rows, F32)
    )
    scratch = dict(
        send=D_SEM((18, 8)), recv=D_SEM((18, 8)), own=D_SEM((8,)), keep=D_SEM((19,)), fetch=D_SEM((17,)), load=D_SEM((3,)),
        free=pltpu.SemaphoreType.REGULAR,
        sum=V((4, 4, 2, 2) + block, BF16), core=V((4, 4, 2, 2) + block, BF16), xr=V((16, 2, 2) + block, BF16),
        yr=V((16, 2, 2) + block, BF16), cc=V((16, 4) + block, BF16),
        nsum=V((4, 2, 2, 32, 128), F32), ncore=V((4, 2, 2, 32, 128), F32), nxr=V((2, 2, 32, 128), F32), nyr=V((2, 2, 32, 128), F32),
        ncc=V((4, 32, 128), F32), nown=V((4, 2, 2, 2, 32, 128), F32),
        gb=V((8, 1024), F32), r=V(rows, F32), g=V(rows, F32), cot=V(rows, BF16), ctx=V(rows, BF16), q=V(rows, BF16),
        ck=V((64, 1024), BF16), cv=V((64, 1024), BF16), clse=V((4, 1280), F32), nc=V(rows, BF16), text=V((64, 1024), BF16),
        k=V((1280, 1024), BF16), v=V((1280, 1024), BF16), lse=V((4, 1280), F32), normed=V((1280, 1024), BF16), w=V((3, 1024, 1024), BF16),
        bias=V((1280, 640), BF16), cbias=V((64, 640), BF16), ng=V((8, 1024), F32), gr=V(rows, F32), branch=V(rows, BF16),
        branch2=V(rows, BF16), up=V(rows, BF16), dq=V(rows, BF16), stacked_q=V((1280, 256), BF16), stacked_g=V((1280, 256), BF16),
        total=V((256, 1280), F32), dw=V((2, 1024, 1024), BF16), tpart=V((2, 2, 16, 1024), BF16), tcore=V((2, 16, 1024), BF16),
        tsum=V((2, 16, 1024), BF16), fpart=V((2, 2) + rows, BF16), fcore=V((2,) + rows, BF16),
    )
    in_spec = {n: pl.BlockSpec(memory_space=pl.ANY) for n in BACKWARD_IN}
    for n in ("seg_rows", "seg_cols"):
        in_spec[n] = pl.BlockSpec(memory_space=pltpu.VMEM)
    in_spec["text_len"] = pl.BlockSpec(memory_space=pltpu.SMEM)

    def kernel(*refs):
        a, b = len(BACKWARD_IN), len(BACKWARD_IN) + len(BACKWARD_OUT)
        backward_kernel(
            dict(zip(BACKWARD_IN, refs[:a])),
            dict(zip(BACKWARD_OUT, refs[a:b])),
            dict(zip(scratch, refs[b:])),
        )

    outs = pl.pallas_call(
        kernel,
        out_shape=[shapes[n] for n in BACKWARD_OUT],
        in_specs=[in_spec[n] for n in BACKWARD_IN],
        out_specs=[pl.BlockSpec(memory_space=pl.ANY)] * len(BACKWARD_OUT),
        scratch_shapes=list(scratch.values()),
        compiler_params=pltpu.CompilerParams(
            collective_id=1, has_side_effects=True, vmem_limit_bytes=VMEM_BYTES
        ),
    )(*[args[n] for n in BACKWARD_IN])
    return dict(zip(BACKWARD_OUT, outs))


RESULT_UNITS = dict(down=(0, 1, 2, 3), up=(4, 5, 6, 7), cout=(8,), cqkv=(9, 10, 11), sout=(12,), sqkv=(13, 14, 15))


def finish_kernel(fin, nfin, fmine, tmine, gr, frames, gb, out, o_out, o_frames, o_text, o_gain, o_bias, o_sqkv, o_sout, o_cqkv, o_cout, o_up, o_down):
    def total(u):
        parts = [fin[u, k].astype(F32) for k in range(4)]
        return (parts[0] + parts[1]) + (parts[2] + parts[3])

    for ref, units in ((o_sqkv, (13, 14, 15)), (o_sout, (12,)), (o_cqkv, (9, 10, 11)), (o_cout, (8,))):
        for k, u in enumerate(units):
            ref[:, k * 1024 : (k + 1) * 1024] = total(u)
    for k in range(4):
        o_down[k * 32 : (k + 1) * 32, :] = total(k)
    parts = [total(4 + j) for j in range(4)]
    lane = lax.broadcasted_iota(jnp.int32, (32, 128), 1) // 32
    for m in range(32):
        block = jnp.zeros((32, 128), F32)
        for j in range(4):
            chunk = parts[j][:, m // 4 * 128 : m // 4 * 128 + 128]
            moved = pltpu.roll(chunk, (j - m % 4) % 4 * 32, 1) if j != m % 4 else chunk
            block = jnp.where(lane == j, moved, block)
        o_up[:, m * 128 : (m + 1) * 128] = block
    n = (nfin[0] + nfin[1]) + (nfin[2] + nfin[3])
    o_gain[...] = n[:, :3]
    o_bias[...] = n[:, 3:6]
    o_text[...] = (tmine[0].astype(F32) + tmine[1].astype(F32)).astype(BF16)
    o_out[...] = out[...]
    gain = gb[0:1, :]

    def rows_of(b, rows):
        values = frames[rows, :].astype(F32)
        center = values - jnp.mean(values, axis=-1, keepdims=True)
        scale = lax.rsqrt(jnp.mean(center * center, axis=-1, keepdims=True) + 1e-05)
        hat = center * scale
        h = (fmine[0, rows, :].astype(F32) + fmine[1, rows, :].astype(F32)) * gain
        back = (h - jnp.mean(h, axis=-1, keepdims=True) - hat * jnp.mean(h * hat, axis=-1, keepdims=True)) * scale
        o_frames[rows, :] = (gr[rows, :] + back).astype(BF16)

    tiles(5, 64)(rows_of)


def run_finish_kernel(*args):
    S = jax.ShapeDtypeStruct
    return pl.pallas_call(
        finish_kernel,
        out_shape=[
            S((320, 1024), BF16),
            S((320, 1024), BF16),
            S((16, 1024), BF16),
            S((32, 3), F32),
            S((32, 3), F32),
            S((32, 3072), F32),
            S((32, 1024), F32),
            S((32, 3072), F32),
            S((32, 1024), F32),
            S((32, 4096), F32),
            S((128, 1024), F32),
        ],
        in_specs=[pl.BlockSpec(memory_space=pltpu.VMEM)] * len(args),
        out_specs=[pl.BlockSpec(memory_space=pltpu.VMEM)] * 11,
        compiler_params=pltpu.CompilerParams(vmem_limit_bytes=VMEM_BYTES),
    )(*args)


def fetch_all(norm_gain, norm_bias, self_qkv, self_out, cross_qkv, cross_out, ffn_up, ffn_down):
    first = (
        lax.all_gather(norm_gain, ("dp", "seq"), axis=0, tiled=True),
        lax.all_gather(norm_bias, ("dp", "seq"), axis=0, tiled=True),
        lax.all_gather(self_qkv, ("dp", "seq"), axis=0, tiled=True),
        lax.all_gather(self_out, ("dp", "seq"), axis=0, tiled=True),
    )
    second = (
        lax.all_gather(cross_qkv, ("dp", "seq"), axis=0, tiled=True),
        lax.all_gather(cross_out, ("dp", "seq"), axis=0, tiled=True),
    )
    third = (
        lax.all_gather(ffn_up, ("dp", "seq"), axis=0, tiled=True),
        lax.all_gather(ffn_down, ("dp", "seq"), axis=0, tiled=True),
    )
    return tuple(first) + tuple(second) + tuple(third)


def run_forward(frames, local_seg, frame_seg, text_seg, text_states, offset, weights):
    norm_gain, norm_bias, self_qkv, self_out, cross_qkv, cross_out, ffn_up, ffn_down = weights
    gains = norm_gain.astype(jnp.float32)
    biases = norm_bias.astype(jnp.float32)
    inputs = frames.astype(jnp.float32)
    normed_self = layer_norm(inputs, gains[:, 0], biases[:, 0]).astype(jnp.bfloat16)
    queries = jnp.dot(normed_self, self_qkv[:, :D], preferred_element_type=jnp.float32).astype(
        jnp.bfloat16
    )
    pair_weights = self_qkv[:, D:].reshape(D, 2, D)
    key_value = jnp.einsum(
        "rcd,dje->jrce", normed_self, pair_weights, preferred_element_type=jnp.float32
    ).astype(jnp.bfloat16)
    gathered = lax.all_gather(key_value, "seq", axis=2, tiled=True)
    self_context, self_logsum = lax.map(
        lambda record: attend(
            record[0], record[1], record[2], self_allowed(record[3], record[4], offset)
        ),
        (queries, gathered[0], gathered[1], local_seg, frame_seg),
    )
    self_context = self_context.astype(jnp.bfloat16)
    resid_one = inputs + jnp.dot(self_context, self_out, preferred_element_type=jnp.float32)
    normed_cross = layer_norm(resid_one, gains[:, 1], biases[:, 1]).astype(jnp.bfloat16)
    cross_queries = jnp.dot(
        normed_cross, cross_qkv[:, :D], preferred_element_type=jnp.float32
    ).astype(jnp.bfloat16)
    text_weights = cross_qkv[:, D:].reshape(D, 2, D)
    text_pair = jnp.einsum(
        "rtd,dje->jrte", text_states, text_weights, preferred_element_type=jnp.float32
    ).astype(jnp.bfloat16)
    cross_context, cross_logsum = lax.map(
        lambda record: attend(
            record[0], record[1], record[2], record[3][:, None] == record[4][None, :]
        ),
        (cross_queries, text_pair[0], text_pair[1], local_seg, text_seg),
    )
    cross_context = cross_context.astype(jnp.bfloat16)
    resid_two = resid_one + jnp.dot(cross_context, cross_out, preferred_element_type=jnp.float32)
    normed_ffn = layer_norm(resid_two, gains[:, 2], biases[:, 2]).astype(jnp.bfloat16)
    hidden_pre = jnp.dot(normed_ffn, ffn_up, preferred_element_type=jnp.float32)
    activated = exact_gelu(hidden_pre).astype(jnp.bfloat16)
    outcome = resid_two + jnp.dot(activated, ffn_down, preferred_element_type=jnp.float32)
    saved = (
        inputs,
        normed_self,
        queries,
        gathered,
        self_context,
        self_logsum,
        resid_one,
        normed_cross,
        cross_queries,
        text_pair,
        cross_context,
        cross_logsum,
        resid_two,
        normed_ffn,
        hidden_pre,
        activated,
    )
    return (outcome, saved)


def generic_body(
    frames,
    frame_seg,
    text_states,
    text_len,
    norm_gain,
    norm_bias,
    self_qkv,
    self_out,
    cross_qkv,
    cross_out,
    ffn_up,
    ffn_down,
    cotangent,
):
    width = frames.shape[1]
    offset = lax.axis_index("seq") * width
    local_seg = lax.dynamic_slice_in_dim(frame_seg, offset, width, 1)
    text_seg = text_segments(text_len)
    shards = (norm_gain, norm_bias, self_qkv, self_out, cross_qkv, cross_out, ffn_up, ffn_down)
    weights = fetch_all(*shards)
    outcome, saved = run_forward(
        frames, local_seg, frame_seg, text_seg, text_states, offset, weights
    )
    frames_out = outcome.astype(jnp.bfloat16)
    (
        inputs,
        normed_self,
        queries,
        gathered,
        self_context,
        self_logsum,
        resid_one,
        normed_cross,
        cross_queries,
        text_pair,
        cross_context,
        cross_logsum,
        resid_two,
        normed_ffn,
        hidden_pre,
        activated,
    ) = saved
    gain_full, bias_full, self_full, self_proj, cross_full, cross_proj, up_full, down_full = weights
    gains = gain_full.astype(jnp.float32)
    biases = bias_full.astype(jnp.float32)
    upstream = cotangent.astype(jnp.float32)
    down_grad = jnp.einsum("rcf,rcd->fd", activated, cotangent, preferred_element_type=jnp.float32)
    grad_act = jnp.einsum("rcd,fd->rcf", cotangent, down_full, preferred_element_type=jnp.float32)
    unused_value, gelu_pull = jax.vjp(exact_gelu, hidden_pre)
    grad_pre = gelu_pull(grad_act)[0].astype(jnp.bfloat16)
    up_grad = jnp.einsum("rcd,rcf->df", normed_ffn, grad_pre, preferred_element_type=jnp.float32)
    grad_normed = jnp.einsum("rcf,df->rcd", grad_pre, up_full, preferred_element_type=jnp.float32)
    grad_back, gain_two, bias_two = norm_back(resid_two, gains[:, 2], biases[:, 2], grad_normed)
    grad_resid_two = upstream + grad_back
    ffn_shares = (
        lax.psum_scatter(up_grad, ("dp", "seq"), scatter_dimension=0, tiled=True),
        lax.psum_scatter(down_grad, ("dp", "seq"), scatter_dimension=0, tiled=True),
    )
    branch_two = grad_resid_two.astype(jnp.bfloat16)
    cross_out_grad = jnp.einsum(
        "rcd,rce->de", cross_context, branch_two, preferred_element_type=jnp.float32
    )
    grad_context = jnp.einsum(
        "rce,de->rcd", branch_two, cross_proj, preferred_element_type=jnp.float32
    ).astype(jnp.bfloat16)
    grad_cross_q, grad_cross_k, grad_cross_v = lax.map(
        lambda record: attend_back(
            record[0],
            record[1],
            record[2],
            record[3][:, None] == record[4][None, :],
            record[5],
            record[6],
        ),
        (
            cross_queries,
            text_pair[0],
            text_pair[1],
            local_seg,
            text_seg,
            cross_logsum,
            grad_context,
        ),
    )
    text_joined = jnp.transpose(jnp.concatenate([grad_cross_k, grad_cross_v], axis=2), (1, 0, 2))
    text_summed = lax.psum_scatter(
        text_joined.astype(jnp.bfloat16), "seq", scatter_dimension=0, tiled=True
    ).astype(jnp.float32)
    text_shares = jnp.transpose(text_summed, (1, 0, 2)).astype(jnp.bfloat16)
    share = text_shares.shape[1]
    text_part = lax.dynamic_slice_in_dim(text_states, lax.axis_index("seq") * share, share, 1)
    text_kv_grad = jnp.einsum(
        "rtd,rte->de", text_part, text_shares, preferred_element_type=jnp.float32
    )
    text_grad = jnp.einsum(
        "rte,de->rtd", text_shares, cross_full[:, D:], preferred_element_type=jnp.float32
    ).astype(jnp.bfloat16)
    grad_cross_q = grad_cross_q.astype(jnp.bfloat16)
    cross_q_grad = jnp.einsum(
        "rcd,rce->de", normed_cross, grad_cross_q, preferred_element_type=jnp.float32
    )
    cross_qkv_grad = jnp.concatenate([cross_q_grad, text_kv_grad], axis=1)
    grad_normed = jnp.einsum(
        "rce,de->rcd", grad_cross_q, cross_full[:, :D], preferred_element_type=jnp.float32
    )
    grad_back, gain_one, bias_one = norm_back(resid_one, gains[:, 1], biases[:, 1], grad_normed)
    grad_resid_one = grad_resid_two + grad_back
    cross_shares = (
        lax.psum_scatter(cross_qkv_grad, ("dp", "seq"), scatter_dimension=0, tiled=True),
        lax.psum_scatter(cross_out_grad, ("dp", "seq"), scatter_dimension=0, tiled=True),
    )
    branch_one = grad_resid_one.astype(jnp.bfloat16)
    self_out_grad = jnp.einsum(
        "rcd,rce->de", self_context, branch_one, preferred_element_type=jnp.float32
    )
    grad_context = jnp.einsum(
        "rce,de->rcd", branch_one, self_proj, preferred_element_type=jnp.float32
    ).astype(jnp.bfloat16)
    grad_self_q, grad_self_k, grad_self_v = lax.map(
        lambda record: attend_back(
            record[0],
            record[1],
            record[2],
            self_allowed(record[3], record[4], offset),
            record[5],
            record[6],
        ),
        (queries, gathered[0], gathered[1], local_seg, frame_seg, self_logsum, grad_context),
    )
    joined = jnp.concatenate([grad_self_k, grad_self_v], axis=2)
    summed = lax.psum_scatter(
        jnp.transpose(joined, (1, 0, 2)).astype(jnp.bfloat16),
        "seq",
        scatter_dimension=0,
        tiled=True,
    ).astype(jnp.float32)
    key_shares = jnp.transpose(summed, (1, 0, 2)).astype(jnp.bfloat16)
    all_grads = jnp.concatenate([grad_self_q.astype(jnp.bfloat16), key_shares], axis=2)
    self_qkv_grad = jnp.einsum(
        "rcd,rce->de", normed_self, all_grads, preferred_element_type=jnp.float32
    )
    grad_normed = jnp.einsum(
        "rce,de->rcd", all_grads, self_full, preferred_element_type=jnp.float32
    )
    grad_back, gain_zero, bias_zero = norm_back(inputs, gains[:, 0], biases[:, 0], grad_normed)
    frames_grad = (grad_resid_one + grad_back).astype(jnp.bfloat16)
    gain_grad = jnp.stack([gain_zero, gain_one, gain_two], axis=1)
    bias_grad = jnp.stack([bias_zero, bias_one, bias_two], axis=1)
    self_shares = (
        lax.psum_scatter(gain_grad, ("dp", "seq"), scatter_dimension=0, tiled=True),
        lax.psum_scatter(bias_grad, ("dp", "seq"), scatter_dimension=0, tiled=True),
        lax.psum_scatter(self_qkv_grad, ("dp", "seq"), scatter_dimension=0, tiled=True),
        lax.psum_scatter(self_out_grad, ("dp", "seq"), scatter_dimension=0, tiled=True),
    )
    return (
        frames_out,
        frames_grad,
        text_grad,
        self_shares[0],
        self_shares[1],
        self_shares[2],
        self_shares[3],
        cross_shares[0],
        cross_shares[1],
        ffn_shares[0],
        ffn_shares[1],
    )


def fast_body(
    frames,
    frame_seg,
    text_states,
    text_len,
    norm_gain,
    norm_bias,
    self_qkv,
    self_out,
    cross_qkv,
    cross_out,
    ffn_up,
    ffn_down,
    cotangent,
):
    width = frames.shape[1]
    norms = jnp.pad(jnp.concatenate([norm_gain, norm_bias], axis=1), ((0, 0), (0, 122)))
    up_local = ffn_up.reshape(32, 32, 4, 32).transpose(0, 2, 1, 3).reshape(32, 4096)
    args = dict(
        frames=frames[0],
        norms=norms,
        sqkv=self_qkv,
        sout=self_out,
        cqkv=cross_qkv,
        cout=cross_out,
        up=up_local,
        down=ffn_down.reshape(4, 32, D),
        cot=cotangent[0],
        text=text_states[0],
        seg_rows=frame_seg.reshape(4, 1, width),
        seg_cols=frame_seg.reshape(4 * width, 1),
        text_len=text_len,
    )
    got = run_forward_kernel(args)
    for name in ("cot", "text", "seg_rows", "seg_cols", "text_len"):
        got[name] = args[name]
    for name in ("ddown", "dup"):
        got[name] = got[name].reshape(4, 4, 2, 2, 2, 32, D)
    back = run_backward_kernel(got)
    outs = run_finish_kernel(
        back["fin"], back["nfin"], back["fmine"], back["tmine"], back["gr"], frames[0], got["gb"], got["out"]
    )
    return (outs[0][None], outs[1][None], outs[2][None]) + tuple(outs[3:])


def solution(mesh):
    return jax.shard_map(
        fast_body if dict(mesh.shape) == {"dp": 8, "seq": 4} else generic_body,
        mesh=mesh,
        in_specs=(
            P("dp", "seq", None),
            P("dp", None),
            P("dp", None, None),
            P("dp", None),
            P(("dp", "seq"), None),
            P(("dp", "seq"), None),
            P(("dp", "seq"), None),
            P(("dp", "seq"), None),
            P(("dp", "seq"), None),
            P(("dp", "seq"), None),
            P(("dp", "seq"), None),
            P(("dp", "seq"), None),
            P("dp", "seq", None),
        ),
        out_specs=(
            P("dp", "seq", None),
            P("dp", "seq", None),
            P("dp", "seq", None),
            P(("dp", "seq"), None),
            P(("dp", "seq"), None),
            P(("dp", "seq"), None),
            P(("dp", "seq"), None),
            P(("dp", "seq"), None),
            P(("dp", "seq"), None),
            P(("dp", "seq"), None),
            P(("dp", "seq"), None),
        ),
        check_vma=False,
    )
```

```python
import types

import jax
import jax.numpy as jnp
from jax import lax
from jax.experimental import pallas as pl
from jax.experimental.pallas import tpu as pltpu
from jax.sharding import PartitionSpec as P

D = 1024
HEADS = 16
HEAD_DIM = 64
TEXT_LEN = 64


def layer_norm(values, gain, bias):
    center = values - jnp.mean(values, axis=-1, keepdims=True)
    spread = jnp.mean(center * center, axis=-1, keepdims=True)
    return center * lax.rsqrt(spread + 1e-05) * gain + bias


def norm_back(values, gain, bias, upstream):
    unused_value, pullback = jax.vjp(layer_norm, values, gain, bias)
    return pullback(upstream)


def exact_gelu(values):
    return jax.nn.gelu(values, approximate=False)


def split_heads(values):
    return values.reshape(values.shape[0], HEADS, HEAD_DIM)


def text_segments(text_len):
    bounds = jnp.cumsum(text_len, axis=1)
    positions = jnp.arange(TEXT_LEN, dtype=jnp.int32)
    return jnp.sum((positions[None, :, None] >= bounds[:, None, :]).astype(jnp.int32), axis=2)


def self_allowed(local_seg, full_seg, offset):
    row_pos = offset + jnp.arange(local_seg.shape[0], dtype=jnp.int32)
    col_pos = jnp.arange(full_seg.shape[0], dtype=jnp.int32)
    return (row_pos[:, None] >= col_pos[None, :]) & (local_seg[:, None] == full_seg[None, :])


def masked_scores(queries, keys_in, allowed):
    factor = HEAD_DIM ** (-0.5)
    scores = (
        jnp.einsum(
            "qhe,khe->hqk",
            split_heads(queries),
            split_heads(keys_in),
            preferred_element_type=jnp.float32,
        )
        * factor
    )
    return jnp.where(allowed[None], scores, -1e30)


def attend(queries, keys_in, values, allowed):
    scores = masked_scores(queries, keys_in, allowed)
    highest = jnp.max(scores, axis=-1, keepdims=True)
    powered = jnp.exp(scores - highest)
    totals = jnp.sum(powered, axis=-1, keepdims=True)
    weights = (powered / totals).astype(jnp.bfloat16)
    context = jnp.einsum(
        "hqk,khe->qhe", weights, split_heads(values), preferred_element_type=jnp.float32
    )
    return (context.reshape(queries.shape[0], -1), highest + jnp.log(totals))


def attend_back(queries, keys_in, values, allowed, logsum, upstream):
    factor = HEAD_DIM ** (-0.5)
    probs_full = jnp.exp(masked_scores(queries, keys_in, allowed) - logsum)
    grad_heads = split_heads(upstream)
    grad_probs = jnp.einsum(
        "qhe,khe->hqk", grad_heads, split_heads(values), preferred_element_type=jnp.float32
    )
    row_inner = jnp.sum(probs_full * grad_probs, axis=-1, keepdims=True)
    grad_scores = (probs_full * (grad_probs - row_inner)).astype(jnp.bfloat16)
    grad_queries = (
        jnp.einsum(
            "hqk,khe->qhe", grad_scores, split_heads(keys_in), preferred_element_type=jnp.float32
        )
        * factor
    )
    grad_keys = (
        jnp.einsum(
            "hqk,qhe->khe", grad_scores, split_heads(queries), preferred_element_type=jnp.float32
        )
        * factor
    )
    grad_values = jnp.einsum(
        "hqk,qhe->khe",
        probs_full.astype(jnp.bfloat16),
        grad_heads,
        preferred_element_type=jnp.float32,
    )
    return (
        grad_queries.reshape(queries.shape[0], -1),
        grad_keys.reshape(keys_in.shape[0], -1),
        grad_values.reshape(values.shape[0], -1),
    )


F32, BF16 = jnp.float32, jnp.bfloat16
MESH = pl.DeviceIdType.MESH
VMEM_BYTES = 64 * 2**20
BLOCK = 256
LEAD = 4
PACE_FORWARD = 7.0
PACE_BACKWARD = 7.0
AHEAD = 1


def place():
    dp, seq = lax.axis_index("dp"), lax.axis_index("seq")
    return dp // 2, lax.rem(dp, 2), seq // 2, lax.rem(seq, 2)


def device(z, y, x, c):
    return (z * 2 + y, x * 2 + c)


def greet(z, y, x, c):
    barrier = pltpu.get_barrier_semaphore()
    others = [device(lax.rem(z + k, 4), y, x, c) for k in (1, 2, 3)]
    others += [device(z, 1 - y, x, c), device(z, y, 1 - x, c), device(z, y, x, 1 - c)]
    for other in others:
        pl.semaphore_signal(barrier, inc=1, device_id=other, device_id_type=MESH)
    pl.semaphore_wait(barrier, len(others))


def dot_nn(a, b):
    return jnp.dot(a, b, preferred_element_type=F32)


def dot_nt(a, b):
    return lax.dot_general(a, b, (((1,), (1,)), ((), ())), preferred_element_type=F32)


def dot_tn(a, b):
    return lax.dot_general(a, b, (((0,), (0,)), ((), ())), preferred_element_type=F32)


def tiles(count, size):
    def run(step):
        def one(i, carry):
            step(i, pl.ds(pl.multiple_of(i * size, size), size))
            return carry

        lax.fori_loop(0, count, one, 0)

    return run


def normalize(block, gain, bias):
    center = block - jnp.mean(block, axis=-1, keepdims=True)
    spread = jnp.mean(center * center, axis=-1, keepdims=True)
    return center * lax.rsqrt(spread + 1e-05) * gain + bias


def stack_heads(dst, src, group, factor):
    rows = src.shape[0]
    part = src[:, group * 256 : group * 256 + 256]
    if factor != 1.0:
        part = part * jnp.asarray(factor, part.dtype)
    head = lax.broadcasted_iota(jnp.int32, part.shape, 1) // HEAD_DIM
    for h in range(4):
        dst[h * rows : (h + 1) * rows, :] = jnp.where(head == h, part, jnp.zeros_like(part))


def unstack_heads(wide, rows):
    parts = [wide[h * 64 : (h + 1) * 64, h * rows : (h + 1) * rows] for h in range(4)]
    return jnp.concatenate(parts, axis=0).T


def attend_group(group, q, k, v, bias, stacked, scores, total, context, logsum, between):
    rows, keys = q.shape[0], k.shape[0]
    size = min(BLOCK, keys)
    cols = slice(group * 256, group * 256 + 256)
    stack_heads(stacked, q, group, HEAD_DIM**-0.5)

    def score(i, highest):
        at = pl.ds(pl.multiple_of(i * size, size), size)
        s = dot_nt(k[at, cols], stacked[...]) + bias[at, :].astype(F32)
        scores[at, :] = s
        return jnp.maximum(highest, jnp.max(s, axis=0, keepdims=True))

    highest = lax.fori_loop(0, keys // size, score, jnp.full((1, 4 * rows), -3e38, F32))
    between()
    total[...] = jnp.zeros_like(total)

    def weigh(i, summed):
        at = pl.ds(pl.multiple_of(i * size, size), size)
        p = jnp.exp(scores[at, :] - highest)
        total[...] += dot_tn(v[at, cols], p.astype(BF16))
        return summed + jnp.sum(p, axis=0, keepdims=True)

    summed = lax.fori_loop(0, keys // size, weigh, jnp.zeros((1, 4 * rows), F32))
    logsum[group : group + 1, :] = highest + jnp.log(summed)
    context[:, cols] = unstack_heads(total[...] / summed, rows).astype(BF16)


class Gathering:
    def __init__(self, at, units, over_y, wide, send_sem, recv_sem, own_sem):
        self.at, self.units, self.n = at, units, len(units)
        self.over_y, self.wide = over_y, wide
        self.order = [u for u in range(self.n) if u not in wide]
        self.send_sem, self.recv_sem, self.own_sem = send_sem, recv_sem, own_sem
        self.sent, self.step, self.ahead, self.since = [], 0, 0, 0.0
        z, y, x, c = at
        self.to_x, self.to_y, self.to_c = device(z, y, 1 - x, c), device(z, 1 - y, x, c), device(z, y, x, 1 - c)

    def copy(self, src, dst, u, k, dev):
        return pltpu.make_async_remote_copy(
            src_ref=src,
            dst_ref=dst,
            send_sem=self.send_sem.at[u, k],
            recv_sem=self.recv_sem.at[u, k],
            device_id=dev,
            device_id_type=MESH,
        )

    def go(self, copy):
        copy.start()
        self.sent.append(copy)

    def same(self, u, k, dev, *spot):
        view = self.units[u][1](*spot)
        return self.copy(view, view, u, k, dev)

    def across(self, u, k):
        z, y, x, c = self.at
        src, dst = self.units[u][0], self.units[u][1](z, y, x, c)
        return self.copy(src, dst, u, k - 1, device(lax.rem(z + k, 4), y, x, c))

    def own(self, u):
        return pltpu.make_async_copy(self.units[u][0], self.units[u][1](*self.at), self.own_sem.at[u])

    def first(self, p):
        if p < len(self.order):
            u = self.order[p]
            self.own(u).start()
            for k in (1, 2, 3):
                self.go(self.across(u, k))

    def cuts(self, u):
        if u in self.over_y:
            return pl.ds(0, 4), None
        return pl.ds(0, 2), pl.ds(2, 2)

    def spread(self, p):
        z, y, x, c = self.at
        every, u, same, go = pl.ds(0, 4), self.order[p], self.same, self.go
        for k in (1, 2, 3):
            self.across(u, k).wait_recv()
        self.own(u).wait()
        go(same(u, 3, self.to_x, every, y, x, c))
        go(same(u, 4, self.to_y, every, y, x, c))
        go(same(u, 5, self.to_c, every, y, x, c))
        self.first(p + LEAD)

    def work(self, us):
        self.since += us
        if self.since >= PACE_FORWARD:
            self.pump()

    def pump(self):
        z, y, x, c = self.at
        every = pl.ds(0, 4)
        self.since = 0.0
        t, n, same, go = self.step, len(self.order), self.same, self.go
        if t >= n + 2:
            return
        self.step += 1
        while self.ahead < min(n, t + AHEAD):
            self.spread(self.ahead)
            self.ahead += 1
        if 0 <= t - 1 < n:
            u = self.order[t - 1]
            low, high = self.cuts(u)
            same(u, 3, self.to_x, every, y, 1 - x, c).wait_recv()
            go(same(u, 6, self.to_y, low, y, 1 - x, c))
            go(same(u, 7, self.to_c, every, y, 1 - x, c))
            same(u, 4, self.to_y, every, 1 - y, x, c).wait_recv()
            if high is not None:
                go(same(u, 8, self.to_x, high, 1 - y, x, c))
            go(same(u, 9, self.to_c, every, 1 - y, x, c))
        if 0 <= t - 2 < n:
            u = self.order[t - 2]
            low, high = self.cuts(u)
            same(u, 6, self.to_y, low, 1 - y, 1 - x, c).wait_recv()
            go(same(u, 10, self.to_c, low, 1 - y, 1 - x, c))
            if high is not None:
                same(u, 8, self.to_x, high, 1 - y, 1 - x, c).wait_recv()
                go(same(u, 11, self.to_c, high, 1 - y, 1 - x, c))
        for u, steps in self.wide.items():
            for stage in range(4):
                if steps[stage] == t:
                    self.widen(u, stage)

    def half(self, u, k, dev, h, *spot):
        view = self.units[u][1](*spot).at[h * 16 : h * 16 + 16]
        return self.copy(view, view, u, k, dev)

    def plane(self, u, k, dev, zz, cc):
        return self.same(u, k, dev, zz, pl.ds(0, 2), pl.ds(0, 2), cc)

    def widen(self, u, stage):
        z, y, x, c = self.at
        go = self.go
        if stage == 0:
            self.own(u).start()
            src, dst = self.units[u][0], self.units[u][1](z, y, x, c)
            go(self.copy(src, dst, u, 0, self.to_x))
            go(self.copy(src, dst, u, 1, self.to_y))
        elif stage == 1:
            self.same(u, 0, self.to_x, z, y, 1 - x, c).wait_recv()
            go(self.half(u, 2, self.to_y, 0, z, y, 1 - x, c))
            self.same(u, 1, self.to_y, z, 1 - y, x, c).wait_recv()
            go(self.half(u, 3, self.to_x, 1, z, 1 - y, x, c))
        elif stage == 2:
            self.own(u).wait()
            self.half(u, 2, self.to_y, 0, z, 1 - y, 1 - x, c).wait_recv()
            self.half(u, 3, self.to_x, 1, z, 1 - y, 1 - x, c).wait_recv()
            for k in (1, 2, 3):
                go(self.plane(u, 3 + k, device(lax.rem(z + k, 4), y, x, c), z, c))
            go(self.plane(u, 7, self.to_c, z, c))
        else:
            for k in (1, 2, 3):
                other = lax.rem(z + 4 - k, 4)
                self.plane(u, 3 + k, self.to_c, other, c).wait_recv()
                go(self.plane(u, 7 + k, self.to_c, other, c))

    def need(self, u):
        z, y, x, c = self.at
        every = pl.ds(0, 4)
        if u in self.wide:
            while self.step <= self.wide[u][3]:
                self.pump()
            self.plane(u, 7, self.to_c, z, 1 - c).wait_recv()
            for k in (1, 2, 3):
                self.plane(u, 7 + k, self.to_c, lax.rem(z + 4 - k, 4), 1 - c).wait_recv()
            return
        while self.step <= self.order.index(u) + 2:
            self.pump()
        low, high = self.cuts(u)
        self.same(u, 5, self.to_c, every, y, x, 1 - c).wait_recv()
        self.same(u, 7, self.to_c, every, y, 1 - x, 1 - c).wait_recv()
        self.same(u, 9, self.to_c, every, 1 - y, x, 1 - c).wait_recv()
        self.same(u, 10, self.to_c, low, 1 - y, 1 - x, 1 - c).wait_recv()
        if high is not None:
            self.same(u, 11, self.to_c, high, 1 - y, 1 - x, 1 - c).wait_recv()


def same_clip(seg, seq):
    own = seg[:, 0:320]
    for k in range(1, 4):
        own = jnp.where(seq == k, seg[:, k * 320 : (k + 1) * 320], own)

    def down(b):
        part = seg[:, pl.ds(pl.multiple_of(b * 128, 128), 128)]
        return jnp.broadcast_to(part, (128, 128)).T[:, :1]

    return own, down


def set_masks(i, seq, bias, text_bias, copies):
    own, down = same_clip(i.seg, seq)

    def mask(b, rows):
        key = lax.broadcasted_iota(jnp.int32, (128, 320), 0) + b * 128
        query = lax.broadcasted_iota(jnp.int32, (128, 320), 1) + seq * 320
        seen = (key <= query) & (down(b) == own)
        block = jnp.where(seen, 0.0, -1e30).astype(F32)
        bias[rows, :] = jnp.concatenate([block] * copies, axis=1).astype(BF16)

    tiles(10, 128)(mask)
    slot = lax.broadcasted_iota(jnp.int32, (TEXT_LEN, 320), 0)
    clip = jnp.zeros((TEXT_LEN, 320), jnp.int32)
    bound = jnp.int32(0)
    for k in range(4):
        bound = bound + i.text_len[0, k]
        clip = clip + (slot >= bound).astype(jnp.int32)
    block = jnp.where(clip == own, 0.0, -1e30).astype(F32)
    text_bias[...] = jnp.concatenate([block] * copies, axis=1).astype(BF16)


def shuffle_columns(part, put, back):
    lane = lax.broadcasted_iota(jnp.int32, (32, 128), 1) // 32
    for b in range(32):
        block = jnp.zeros((32, 128), F32)
        for q in range(4):
            source, quarter = (q * 8 + b // 4, b % 4) if back else (b % 8 * 4 + q, b // 8)
            chunk = part(source)
            moved = pltpu.roll(chunk, (q - quarter) % 4 * 32, 1) if q != quarter else chunk
            block = jnp.where(lane == q, moved, block)
        put(b, block)


def forward_kernel(i, o, s):
    at = place()
    z, y, x, c = at
    seq = x * 2 + c
    units = [(s.nin, lambda zz, yy, xx, cc: o.norms.at[zz, yy, xx, cc])]

    def columns(shard, full, count):
        for k in range(count):
            cut = pl.ds(k * 1024, 1024)
            units.append(
                (shard.at[:, cut], lambda zz, yy, xx, cc, cut=cut: full.at[zz, yy, xx, cc, :, cut])
            )

    columns(i.sqkv, o.sqkv, 3)
    columns(i.sout, o.sout, 1)
    columns(i.cqkv, o.cqkv, 3)
    columns(i.cout, o.cout, 1)
    columns(s.upin, o.up, 4)
    for k in range(4):
        units.append(
            (i.down.at[k], lambda zz, yy, xx, cc, k=k: o.down.at[zz, yy, xx, cc, k])
        )
        wide = {12: (0, 1, 2, 10), 16: (6, 7, 8, 16)}
    comm = Gathering(at, units, (1, 2), wide, s.send, s.recv, s.own)
    up_copy = pltpu.make_async_copy(i.up, s.upraw, s.own.at[comm.n + 3])
    up_copy.start()
    s.flat[...] = jnp.zeros_like(s.flat)
    s.flat[0:3, 0:32] = i.gain[...].astype(F32)
    s.flat[3:6, 0:32] = i.shift[...].astype(F32)
    s.nin[...] = s.flat[...].T[:32].astype(BF16)
    greet(*at)
    fr = s.frames
    f = comm.n

    def share(k, dev, xx, cc):
        view = fr.at[xx, cc]
        return comm.copy(view, view, f, k, dev)

    own_frames = pltpu.make_async_copy(i.frames, fr.at[x, c], s.own.at[f])
    own_frames.start()
    cot_copy = pltpu.make_async_copy(i.cot, s.cot, s.own.at[f + 1])
    cot_copy.start()
    text_copy = pltpu.make_async_copy(i.text, s.text, s.own.at[f + 2])
    text_copy.start()
    for u in range(LEAD):
        comm.first(u)
    own_frames.wait()
    comm.go(share(0, comm.to_x, x, c))
    comm.go(share(1, comm.to_c, x, c))
    up_copy.wait()

    def put_up(b, block):
        s.upin[:, b * 128 : b * 128 + 128] = block.astype(BF16)

    shuffle_columns(lambda b: s.upraw[:, b * 128 : b * 128 + 128].astype(F32), put_up, False)

    saves = []

    def save(src, dst):
        copy = pltpu.make_async_copy(src, dst, s.save.at[len(saves)])
        copy.start()
        saves.append(copy)

    set_masks(i, seq, s.bias, s.cbias, 4)

    def weight(u, where):
        comm.need(u)
        src = units[u][1](pl.ds(0, 4), pl.ds(0, 2), pl.ds(0, 2), pl.ds(0, 2))
        dst = s.w.at[where]
        copy = pltpu.make_async_copy(src, dst.reshape(4, 2, 2, 2, 32, 1024), s.load.at[u])
        copy.start()
        copy.wait()
        return dst

    def norm(dst, src_block, k, count):
        gain, bias = s.gb[k : k + 1, :], s.gb[3 + k : 4 + k, :]

        def one(b, rows):
            dst[rows, :] = normalize(src_block(b, rows), gain, bias).astype(BF16)

        tiles(count, 64)(one)

    share(0, comm.to_x, 1 - x, c).wait_recv()
    comm.go(share(2, comm.to_c, 1 - x, c))
    comm.need(0)
    copy = pltpu.make_async_copy(o.norms, s.norms.reshape(4, 2, 2, 2, 32, 128), s.load.at[0])
    copy.start()
    copy.wait()
    s.gb[...] = s.norms[...].astype(F32).T[:8]
    share(1, comm.to_c, x, 1 - c).wait_recv()
    share(2, comm.to_c, 1 - x, 1 - c).wait_recv()
    normed = s.normed

    def frame_block(b, rows):
        return fr[b // 10, lax.rem(b // 5, 2), pl.ds(pl.multiple_of(lax.rem(b, 5) * 64, 64), 64), :].astype(F32)

    norm(normed, frame_block, 0, 20)
    comm.work(4.0)
    save(s.gb, o.gb)
    save(fr, o.frames)
    save(normed, o.normed)

    mine = pl.ds(pl.multiple_of(seq * 320, 64), 320)

    def project(dst, src, w, rows):
        def one(n, cut):
            dst[:, cut] = dot_nn(src[rows, :], w[:, cut]).astype(BF16)

        tiles(4, 256)(one)

    def project_all(dst, w):
        def one(b, rows):
            def two(n, cut):
                dst[rows, cut] = dot_nn(normed[rows, :], w[:, cut]).astype(BF16)

            tiles(4, 256)(two)

        for b in range(4):
            one(b, pl.ds(b * 320, 320))
            comm.work(1.8)

    every_row = pl.ds(0, 320)
    q, k, v = s.q, s.k, s.v
    project(q, normed, weight(1, 0), mine)
    project_all(k, weight(2, 1))
    project_all(v, weight(3, 2))
    save(q, o.q)
    save(k, o.k)
    save(v, o.v)
    for g in range(4):
        attend_group(
            g, q, k, v, s.bias, s.stacked, s.scores, s.total, s.ctx, s.lse, lambda: comm.work(2.0)
        )
        comm.work(2.0)
    save(s.ctx, o.ctx)
    save(s.lse, o.lse)

    def add_project(dst, base, src, w):
        def one(n, cut):
            dst[:, cut] = base(cut) + dot_nn(src[...], w[:, cut])

        tiles(4, 256)(one)

    add_project(s.r1, lambda cut: fr[x, c, :, cut].astype(F32), s.ctx, weight(4, 0))
    save(s.r1, o.r1)
    norm(s.nc, lambda b, rows: s.r1[rows, :], 1, 5)
    save(s.nc, o.nc)
    project(s.cq, s.nc, weight(5, 1), every_row)
    save(s.cq, o.cq)
    text_copy.wait()
    text_rows = pl.ds(0, TEXT_LEN)
    project(s.ck, s.text, weight(6, 2), text_rows)
    project(s.cv, s.text, weight(7, 0), text_rows)
    save(s.ck, o.ck)
    save(s.cv, o.cv)
    for g in range(4):
        attend_group(
            g,
            s.cq,
            s.ck,
            s.cv,
            s.cbias,
            s.stacked,
            s.scores,
            s.total,
            s.cctx,
            s.clse,
            lambda: None,
        )
        comm.work(0.6)
    save(s.cctx, o.cctx)
    save(s.clse, o.clse)
    add_project(s.r2, lambda cut: s.r1[:, cut], s.cctx, weight(8, 1))
    save(s.r2, o.r2)
    norm(s.nf, lambda b, rows: s.r2[rows, :], 2, 5)
    cot_copy.wait()
    act, slope, nf, cot = s.act, s.slope, s.nf, s.cot
    save(nf, o.nf)
    grads = []

    def gradient(dst, left, right):
        m = len(grads)
        if m >= 2:
            grads[m - 2].wait()
        stage = s.stage.at[m % 2]

        def one(n, cut):
            stage[:, cut] = dot_tn(left(), right(cut)).astype(BF16)

        tiles(4, 256)(one)
        copy = pltpu.make_async_copy(stage, dst, s.grad.at[m])
        copy.start()
        grads.append(copy)

    for j in range(4):
        w = weight(9 + j, j % 3)

        def one(n, cut):
            h = dot_nn(nf[...], w[:, cut])
            below = 0.5 * (1.0 + lax.erf(h * 0.7071067811865476))
            act[j, :, cut] = (h * below).astype(BF16)
            slope[j * 320 : (j + 1) * 320, cut] = (
                below + h * jnp.exp(-0.5 * h * h) * 0.3989422804014327
            ).astype(BF16)

        tiles(4, 256)(one)
        comm.work(3.5)
        gradient(o.ddown.at[j], lambda: act[j], lambda cut: cot[:, cut])
        comm.work(2.0)
    save(slope, o.slope)
    for copy in saves:
        copy.wait()
    for j in range(4):
        w = weight(13 + j, j % 3)

        def onward(n, cut):
            s.r2[:, cut] = s.r2[:, cut] + dot_nn(act[j], w[:, cut])

        tiles(4, 256)(onward)
    s.out[...] = s.r2[...].astype(BF16)
    copy = pltpu.make_async_copy(s.out, o.out, s.save.at[len(saves)])
    copy.start()
    copy.wait()
    for copy in grads[-2:]:
        copy.wait()
    for copy in comm.sent:
        copy.wait_send()


def pallas(kernel, args, shapes, scratch, apart, params):
    def named(*refs):
        a, b = len(args), len(args) + len(shapes)
        kernel(
            types.SimpleNamespace(**dict(zip(args, refs[:a]))),
            types.SimpleNamespace(**dict(zip(shapes, refs[a:b]))),
            types.SimpleNamespace(**dict(zip(scratch, refs[b:]))),
        )

    outs = pl.pallas_call(
        named,
        out_shape=list(shapes.values()),
        in_specs=[pl.BlockSpec(memory_space=apart.get(n, pl.ANY)) for n in args],
        out_specs=[pl.BlockSpec(memory_space=pl.ANY)] * len(shapes),
        scratch_shapes=list(scratch.values()),
        compiler_params=pltpu.CompilerParams(
            has_side_effects=True, vmem_limit_bytes=VMEM_BYTES, **params
        ),
    )(*args.values())
    return dict(zip(shapes, outs))


def run_forward_kernel(args):
    S, V, D_SEM = jax.ShapeDtypeStruct, pltpu.VMEM, pltpu.SemaphoreType.DMA
    a = types.SimpleNamespace(**args)
    rows = (320, 1024)
    scratch = dict(
        send=D_SEM((18, 12)), recv=D_SEM((18, 12)), own=D_SEM((21,)), save=D_SEM((24,)), load=D_SEM((17,)), grad=D_SEM((4,)),
        frames=V((2, 2, 320, 1024), BF16), cot=V(rows, BF16), text=V((64, 1024), BF16), norms=V((1024, 128), BF16), gb=V((8, 1024), F32),
        bias=V((1280, 1280), BF16), cbias=V((64, 1280), BF16), w=V((3, 1024, 1024), BF16), normed=V((1280, 1024), BF16),
        q=V(rows, BF16), k=V((1280, 1024), BF16), v=V((1280, 1024), BF16), stacked=V((1280, 256), BF16), scores=V((1280, 1280), F32),
        total=V((256, 1280), F32), ctx=V(rows, BF16), lse=V((4, 1280), F32), r1=V(rows, F32), nc=V(rows, BF16), cq=V(rows, BF16),
        ck=V((64, 1024), BF16), cv=V((64, 1024), BF16), cctx=V(rows, BF16), clse=V((4, 1280), F32), r2=V(rows, F32), nf=V(rows, BF16),
        act=V((4, 320, 1024), BF16), slope=V((1280, 1024), BF16), out=V(rows, BF16), nin=V((32, 128), BF16), flat=V((128, 128), F32),
        upraw=V((32, 4096), BF16), upin=V((32, 4096), BF16), stage=V((2, 1024, 1024), BF16),
    )
    m = types.SimpleNamespace(**scratch)
    shapes = dict(norms=m.nin, sqkv=a.sqkv, sout=a.sout, cqkv=a.cqkv, cout=a.cout, up=a.up, down=a.down)
    shapes = {n: S((4, 2, 2, 2) + v.shape, BF16) for n, v in shapes.items()}
    saved = dict(
        gb=m.gb, frames=m.frames, normed=m.normed, q=m.q, k=m.k, v=m.v, ctx=m.ctx, lse=m.lse, r1=m.r1, nc=m.nc, cq=m.cq, ck=m.ck,
        cv=m.cv, cctx=m.cctx, clse=m.clse, r2=m.r2, out=m.out, nf=m.nf, slope=m.slope,
    )
    shapes.update({n: S(v.shape, v.dtype) for n, v in saved.items()})
    shapes.update(ddown=S((4, 1024, 1024), BF16))
    apart = dict(seg=pltpu.VMEM, gain=pltpu.VMEM, shift=pltpu.VMEM, text_len=pltpu.SMEM)
    return pallas(forward_kernel, args, shapes, scratch, apart, dict(collective_id=0))


def attend_back_group(group, q, k, v, up, context, bias, logsum, stacked_q, stacked_g, total, grad_q, between):
    rows, keys = q.shape[0], k.shape[0]
    size = min(BLOCK, keys)
    cols = slice(group * 256, group * 256 + 256)
    stack_heads(stacked_q, q, group, HEAD_DIM**-0.5)
    stack_heads(stacked_g, up, group, 1.0)
    four = jnp.concatenate([context[:, cols].astype(F32)] * 4, axis=0)
    inner = lax.dot_general(
        jnp.ones((8, 256), F32),
        stacked_g[...].astype(F32) * four,
        (((1,), (1,)), ((), ())),
        precision=lax.Precision.HIGHEST,
        preferred_element_type=F32,
    )[:1]
    shift = logsum[group : group + 1, :]
    total[...] = jnp.zeros_like(total)

    def step(i, carry):
        at = pl.ds(pl.multiple_of(i * size, size), size)
        key, value = k[at, cols], v[at, cols]
        half = bias[at, :].astype(F32)
        s = dot_nt(key, stacked_q[...]) + jnp.concatenate([half, half], axis=1)
        p = jnp.exp(s - shift)
        ds = (p * (dot_nt(value, stacked_g[...]) - inner)).astype(BF16)
        v[at, cols] = dot_nn(p.astype(BF16), stacked_g[...]).astype(BF16)
        k[at, cols] = dot_nn(ds, stacked_q[...]).astype(BF16)
        total[...] += dot_tn(key, ds)
        return carry

    lax.fori_loop(0, keys // size, step, 0)
    between()
    grad_q[:, cols] = (unstack_heads(total[...], rows) * HEAD_DIM**-0.5).astype(BF16)


DOWN_UNITS = (1, 3, 0, 2)
WIDE = {1: (8, 9), 3: (10, 11)}


class Scattering:
    def __init__(self, at, i, o, s, n, last, wide, over_y):
        self.at, self.o, self.s, self.n, self.last = at, o, s, n, last
        self.wide, self.over_y = wide, over_y
        self.begun, self.done1, self.step = 0, 0, 0
        self.queue2, self.queue3, self.finished = [], [], []
        self.sent, self.source, self.since = {}, {}, 0.0
        z, y, x, c = at
        self.to_x, self.to_y, self.to_c = device(z, y, 1 - x, c), device(z, 1 - y, x, c), device(z, y, x, 1 - c)

    def copy(self, src, dst, u, k, dev):
        return pltpu.make_async_remote_copy(
            src_ref=src,
            dst_ref=dst,
            send_sem=self.s.send.at[u, k],
            recv_sem=self.s.recv.at[u, k],
            device_id=dev,
            device_id_type=MESH,
        )

    def go(self, u, k, copy):
        copy.start()
        self.sent[u, k] = copy

    def left(self, u, k):
        copy = self.sent.pop((u, k), None)
        if copy is not None:
            copy.wait_send()

    def buffer(self, main, last, u, slots=16):
        return last if u == self.last else main.at[u % slots]

    def total(self, u):
        if u in self.wide:
            m = list(self.wide).index(u)
            return self.s.big.at[m * 512 : m * 512 + 512].reshape(4, 2, 2, 32, 1024)
        return self.buffer(self.s.sum, self.s.nsum, u, 4)

    def xr(self, u):
        return self.buffer(self.s.xy, self.s.nxy, u).at[0 : self.cut(u)]

    def yr(self, u):
        return self.buffer(self.s.xy, self.s.nxy, u).at[self.cut(u) : 4]

    def cc(self, u):
        return self.buffer(self.s.cc, self.s.ncc, u)

    def from_core(self, u):
        src = self.source[u].at[:, :, :, 1 - self.at[3]]
        return self.copy(src, self.buffer(self.s.core, self.s.ncore, u, 4), u, 0, self.to_c)

    def cut(self, u):
        return 0 if u in self.over_y else 2

    def first_x(self, u):
        n = self.cut(u)
        return self.copy(self.total(u).at[0:n, :, 1 - self.at[2]], self.xr(u), u, 1, self.to_x)

    def first_y(self, u):
        n = self.cut(u)
        return self.copy(self.total(u).at[n:4, 1 - self.at[1]], self.yr(u), u, 2, self.to_y)

    def second_y(self, u):
        n = self.cut(u)
        return self.copy(self.xr(u).at[:, 1 - self.at[1]], self.cc(u).at[0:n], u, 3, self.to_y)

    def second_x(self, u):
        n = self.cut(u)
        return self.copy(self.yr(u).at[:, 1 - self.at[2]], self.cc(u).at[n:4], u, 4, self.to_x)

    def final(self, u):
        return self.o.nfin if u == self.last else self.o.fin.at[u]

    def across(self, u, k):
        z, y, x, c = self.at
        to = lax.rem(z + k, 4)
        return self.copy(self.cc(u).at[to], self.final(u).at[k - 1], u, 4 + k, device(to, y, x, c))

    def keep(self, u):
        return pltpu.make_async_copy(self.cc(u).at[self.at[0]], self.final(u).at[3], self.s.keep.at[u])

    def load(self, u):
        return pltpu.make_async_copy(self.source[u].at[:, :, :, self.at[3]], self.total(u), self.s.own.at[u])

    def begin(self, u, source, in_hbm):
        while self.done1 < u - 3:
            self.pump()
        self.begun += 1
        self.source[u] = source
        if 4 <= u < self.last:
            pl.semaphore_wait(self.s.free, 1)
        if in_hbm:
            self.load(u).start()
        self.go(u, 0, self.from_core(u))

    def work(self, us):
        self.since += us
        if self.since >= PACE_BACKWARD:
            self.pump()

    def pump(self):
        self.since = 0.0
        new, second = None, None
        if self.done1 < self.begun:
            new = self.done1
            self.done1 += 1
            self.stage1(new)
        if self.queue2:
            second = self.queue2.pop(0)
            self.stage2(second)
        if self.queue3:
            self.stage3(self.queue3.pop(0))
        if new is not None and new not in self.wide:
            self.queue2.append(new)
        if second is not None:
            self.queue3.append(second)
        for u, steps in self.wide.items():
            for stage in range(2):
                if steps[stage] == self.step:
                    (self.wide_plane, self.wide_last)[stage](u)
                    self.finished.append((u, stage))
        self.step += 1

    def stage1(self, u):
        z, y, x, c = self.at
        total, got, source = self.total(u), self.buffer(self.s.core, self.s.ncore, u, 4), self.source[u]
        in_hbm = u < 4
        if in_hbm:
            self.load(u).wait()
        else:
            self.left(u - 4, 1)
            self.left(u - 4, 2)
        self.from_core(u).wait_recv()

        def add(j, carry):
            at = (j // 4, lax.rem(j // 2, 2), lax.rem(j, 2))
            own = total[at] if in_hbm else source[at + (c,)]
            total[at] = own + got[at]
            return carry

        lax.fori_loop(0, 16, add, 0)
        if u + 4 < self.last:
            pl.semaphore_signal(self.s.free, inc=1, device_id=self.to_c, device_id_type=MESH)
        if u in self.wide:
            for k in (1, 2, 3):
                self.go(u, 4 + k, self.wide_across(u, k))
            return
        if self.cut(u):
            self.go(u, 1, self.first_x(u))
        self.go(u, 2, self.first_y(u))

    def stage2(self, u):
        z, y, x, c = self.at
        total, yr, n = self.total(u), self.yr(u), self.cut(u)
        if n:
            xr = self.xr(u)
            self.first_x(u).wait_recv()

            def add_x(j, carry):
                a, b = j // 2, lax.rem(j, 2)
                xr[a, b] = xr[a, b] + total[a, b, x]
                return carry

            lax.fori_loop(0, 2 * n, add_x, 0)
            self.go(u, 3, self.second_y(u))
        self.first_y(u).wait_recv()

        def add_y(j, carry):
            a, b = j // 2, lax.rem(j, 2)
            yr[a, b] = yr[a, b] + total[n + a, y, b]
            return carry

        lax.fori_loop(0, 8 - 2 * n, add_y, 0)
        self.go(u, 4, self.second_x(u))

    def stage3(self, u):
        z, y, x, c = self.at
        yr, cc, n = self.yr(u), self.cc(u), self.cut(u)
        if n:
            xr = self.xr(u)
            self.second_y(u).wait_recv()
            for a in range(n):
                cc[a] = cc[a] + xr[a, y]
        self.second_x(u).wait_recv()
        for a in range(4 - n):
            cc[n + a] = cc[n + a] + yr[a, x]
        for k in (1, 2, 3):
            self.go(u, 4 + k, self.across(u, k))
        self.keep(u).start()

    def wide_got(self, u, k):
        m = list(self.wide).index(u)
        at = 1024 + (m * 3 + k - 1) * 128
        return self.s.big.at[at : at + 128].reshape(2, 2, 32, 1024)

    def wide_across(self, u, k):
        z, y, x, c = self.at
        to = lax.rem(z + k, 4)
        return self.copy(self.total(u).at[to], self.wide_got(u, k), u, 4 + k, device(to, y, x, c))

    def wide_copy(self, u, which):
        z, y, x, c = self.at
        m, total = list(self.wide).index(u), self.total(u)
        xw, yw, top, low = self.s.xw.at[m], self.s.yw.at[m], pl.ds(0, 16), pl.ds(16, 16)
        if which == 0:
            return self.copy(total.at[z, :, 1 - x, top], xw, u, 1, self.to_x)
        if which == 1:
            return self.copy(total.at[z, 1 - y, :, low], yw, u, 2, self.to_y)
        if which == 2:
            return self.copy(xw.at[1 - y], self.o.fin.at[u, 1, top], u, 3, self.to_y)
        if which == 3:
            return self.copy(yw.at[1 - x], self.o.fin.at[u, 1, low], u, 4, self.to_x)
        if which == 4:
            return pltpu.make_async_copy(xw.at[y], self.o.fin.at[u, 0, top], self.s.keep.at[u])
        return pltpu.make_async_copy(yw.at[x], self.o.fin.at[u, 0, low], self.s.own.at[4 + m])

    def wide_plane(self, u):
        z, y, x, c = self.at
        total, got = self.total(u), [self.wide_got(u, k) for k in (1, 2, 3)]
        for k in (1, 2, 3):
            self.wide_across(u, k).wait_recv()

        def add(j, carry):
            a, b = j // 2, lax.rem(j, 2)
            own = total[z, a, b].astype(F32) + got[0][a, b].astype(F32)
            more = got[1][a, b].astype(F32) + got[2][a, b].astype(F32)
            total[z, a, b] = (own + more).astype(BF16)
            return carry

        lax.fori_loop(0, 4, add, 0)
        self.go(u, 1, self.wide_copy(u, 0))
        self.go(u, 2, self.wide_copy(u, 1))

    def wide_last(self, u):
        z, y, x, c = self.at
        m, total = list(self.wide).index(u), self.total(u)
        xw, yw = self.s.xw.at[m], self.s.yw.at[m]
        self.wide_copy(u, 0).wait_recv()
        for a in range(2):
            xw[a] = xw[a] + total[z, a, x, 0:16]
        self.go(u, 3, self.wide_copy(u, 2))
        self.wide_copy(u, 4).start()
        self.wide_copy(u, 1).wait_recv()
        for a in range(2):
            yw[a] = yw[a] + total[z, y, a, 16:32]
        self.go(u, 4, self.wide_copy(u, 3))
        self.wide_copy(u, 5).start()

    def settle(self):
        while len(self.finished) < 2 * len(self.wide):
            self.pump()
        for u in self.wide:
            for k in (1, 2, 5, 6, 7):
                self.left(u, k)

    def finish(self):
        while self.queue2 or self.queue3 or self.done1 < self.begun:
            self.pump()
        for u in range(self.n):
            if u in self.wide:
                for which in (2, 3):
                    self.wide_copy(u, which).wait_recv()
                for which in (4, 5):
                    self.wide_copy(u, which).wait()
                continue
            for k in (1, 2, 3):
                self.across(u, k).wait_recv()
            self.keep(u).wait()
        for key in list(self.sent):
            self.left(*key)


def backward_kernel(i, o, s):
    at = place()
    z, y, x, c = at
    seq = x * 2 + c
    comm = Scattering(at, i, o, s, 17, 16, WIDE, ())
    greet(*at)
    six = (4, 2, 2, 2, 32, 1024)
    for u in range(4):
        comm.begin(u, i.ddown.at[DOWN_UNITS.index(u)], True)
    waits = {}

    def fetch(src, dst, slot):
        copy = pltpu.make_async_copy(src, dst, s.fetch.at[slot])
        copy.start()
        waits[slot] = copy

    def have(*slots):
        for slot in slots:
            waits.pop(slot).wait()

    def block(full, k):
        return full.at[:, :, :, :, :, pl.ds(k * 1024, 1024)]

    stream = []
    for j in range(4):
        stream += [i.down.at[:, :, :, :, j], block(i.up, j)]
    stream += [block(i.cout, 0), block(i.cqkv, 1), block(i.cqkv, 2), block(i.cqkv, 0), block(i.sout, 0)]
    stream += [block(i.sqkv, k) for k in range(3)]

    def weight(n):
        dst = s.w.at[n % 3]
        return pltpu.make_async_copy(stream[n], dst.reshape(*six), s.load.at[n % 3])

    def loaded(n):
        weight(n).wait()
        return s.w.at[n % 3]

    def used(n):
        if n + 3 < len(stream):
            weight(n + 3).start()

    for n in range(3):
        weight(n).start()
    fetch(i.cot, s.cot, 3)
    fetch(i.slope, s.k, 11)
    fetch(i.nf, s.up, 5)
    fetch(i.gb, s.gb, 0)
    fetch(i.r2, s.r, 1)
    fetch(i.cctx, s.ctx, 4)
    fetch(i.ck, s.ck, 6)
    fetch(i.cv, s.cv, 7)
    fetch(i.clse, s.clse, 8)
    fetch(i.nc, s.nc, 9)
    fetch(i.text, s.text, 10)
    fetch(i.v, s.v, 12)
    fetch(i.lse, s.lse, 13)
    fetch(i.normed, s.normed, 14)
    comm.pump()
    set_masks(i, seq, s.bias, s.cbias, 2)
    s.ng[...] = jnp.zeros_like(s.ng)
    have(0)

    def norm_back(values, upstream, k, put):
        gain = s.gb[k : k + 1, :]
        center = values - jnp.mean(values, axis=-1, keepdims=True)
        scale = lax.rsqrt(jnp.mean(center * center, axis=-1, keepdims=True) + 1e-05)
        hat = center * scale
        s.ng[k : k + 1, :] += jnp.sum(upstream * hat, axis=0, keepdims=True)
        s.ng[3 + k : 4 + k, :] += jnp.sum(upstream, axis=0, keepdims=True)
        if put is not None:
            h = upstream * gain
            put((h - jnp.mean(h, axis=-1, keepdims=True) - hat * jnp.mean(h * hat, axis=-1, keepdims=True)) * scale)

    def gradient(u, left, right, cost=2.2):
        while u > 5 and comm.done1 < u - 1:
            comm.pump()
        comm.left(u - 2, 0)
        dw = s.dw.at[u % 2]

        def one(n, cut):
            dw[:, cut] = dot_tn(left(), right(cut)).astype(BF16)

        tiles(4, 256)(one)
        comm.begin(u, dw.reshape(*six), False)
        comm.work(cost)

    gr, branch, g = s.gr, s.branch, s.g
    for j in range(4):
        w, w_up = loaded(2 * j), None
        if j == 0:
            have(3, 5, 11)

        def back(n, rows):
            slope = s.k[j * 320 : (j + 1) * 320, rows].astype(F32)
            branch[:, rows] = (dot_nt(s.cot[...], w[rows, :]) * slope).astype(BF16)

        tiles(4, 256)(back)
        used(2 * j)
        gradient(4 + j, lambda: s.up[...], lambda cut: branch[:, cut])
        w_up = loaded(2 * j + 1)

        def onward(n, rows):
            more = dot_nt(branch[...], w_up[rows, :])
            g[:, rows] = more if j == 0 else g[:, rows] + more

        tiles(4, 256)(onward)
        used(2 * j + 1)
        comm.work(3.5)
    fetch(i.k, s.k, 11)
    fetch(i.cq, s.q, 5)
    have(1)

    def back_two(b, rows):
        def put(grad):
            total = s.cot[rows, :].astype(F32) + grad
            gr[rows, :] = total
            branch[rows, :] = total.astype(BF16)

        norm_back(s.r[rows, :], g[rows, :], 2, put)

    tiles(5, 64)(back_two)
    fetch(i.r1, s.r, 1)
    comm.work(1.0)

    def through(dst, src, w):
        def one(n, rows):
            value = dot_nt(src[...], w[rows, :])
            dst[:, rows] = value.astype(dst.dtype)

        tiles(4, 256)(one)

    through(s.up, branch, loaded(8))
    used(8)
    comm.work(1.6)
    have(4)
    gradient(8, lambda: s.ctx[...], lambda cut: branch[:, cut])
    have(5, 6, 7, 8)
    for group in range(4):
        attend_back_group(
            group,
            s.q,
            s.ck,
            s.cv,
            s.up,
            s.ctx,
            s.cbias,
            s.clse,
            s.stacked_q,
            s.stacked_g,
            s.total,
            s.dq,
            lambda: comm.work(1.8),
        )
    fetch(i.q, s.q, 5)
    fetch(i.ctx, s.ctx, 4)
    have(9, 10)
    gradient(9, lambda: s.nc[...], lambda cut: s.dq[:, cut])
    w_key, w_value = loaded(9), loaded(10)

    def text_part(n, rows):
        value = dot_nt(s.ck[...], w_key[rows, :]) + dot_nt(s.cv[...], w_value[rows, :])
        s.tpart[:, :, :, rows] = value.astype(BF16).reshape(2, 2, 16, 256)

    tiles(4, 256)(text_part)
    used(9)
    used(10)
    text_core = comm.copy(s.tpart.at[:, 1 - c], s.tcore, 17, 0, comm.to_c)
    comm.go(17, 0, text_core)
    through(g, s.dq, loaded(11))
    used(11)
    have(1)

    def back_one(b, rows):
        def put(grad):
            total = gr[rows, :] + grad
            gr[rows, :] = total
            branch[rows, :] = total.astype(BF16)

        norm_back(s.r[rows, :], g[rows, :], 1, put)

    tiles(5, 64)(back_one)
    comm.work(3.3)
    save_gr = pltpu.make_async_copy(gr, o.gr, s.fetch.at[16])
    save_gr.start()
    gradient(10, lambda: s.text[...], lambda cut: s.ck[:, cut])
    through(s.up, branch, loaded(12))
    used(12)
    comm.work(1.6)
    text_core.wait_recv()
    s.tsum[...] = s.tpart[:, c] + s.tcore[...]
    text_x = comm.copy(s.tsum.at[1 - x], o.tmine.at[1], 17, 1, comm.to_x)
    comm.go(17, 1, text_x)
    text_keep = pltpu.make_async_copy(s.tsum.at[x], o.tmine.at[0], s.keep.at[17])
    text_keep.start()
    have(4, 5, 11, 12, 13)
    todo = [
        lambda: gradient(11, lambda: s.text[...], lambda cut: s.cv[:, cut]),
        lambda: gradient(12, lambda: s.ctx[...], lambda cut: branch[:, cut]),
    ]
    for group in range(4):
        attend_back_group(
            group,
            s.q,
            s.k,
            s.v,
            s.up,
            s.ctx,
            s.bias,
            s.lse,
            s.stacked_q,
            s.stacked_g,
            s.total,
            s.dq,
            lambda: comm.work(7.0),
        )
        if group < len(todo):
            todo[group]()
    have(14)
    mine = pl.ds(pl.multiple_of(seq * 320, 64), 320)
    wq, wk, wv = loaded(13), loaded(14), loaded(15)
    comm.settle()
    fpart = s.big.at[0:1280].reshape(2, 2, 320, 1024)

    def frames_part(b, rows):
        block = pltpu.make_async_copy(i.frames.at[b // 2, b % 2], s.cot, s.fetch.at[15])
        block.start()

        def one(n, cut):
            g[:, cut] = dot_nt(s.k[rows, :], wk[cut, :]) + dot_nt(s.v[rows, :], wv[cut, :])

        tiles(4, 256)(one)

        @pl.when(b == seq)
        def _():
            def two(n, cut):
                g[:, cut] = g[:, cut] + dot_nt(s.dq[...], wq[cut, :])

            tiles(4, 256)(two)

        block.wait()

        def three(r, part):
            norm_back(s.cot[part, :].astype(F32), g[part, :], 0, None)
            fpart[b // 2, b % 2, part, :] = g[part, :].astype(BF16)

        tiles(5, 64)(three)

    gradient(13, lambda: s.normed[mine, :], lambda cut: s.dq[:, cut])
    for part_of in range(4):
        frames_part(part_of, pl.ds(part_of * 320, 320))
        comm.work(3.8)
    frames_core = comm.copy(fpart.at[:, 1 - c], s.fcore, 17, 2, comm.to_c)
    comm.go(17, 2, frames_core)
    gradient(14, lambda: s.normed[...], lambda cut: s.k[:, cut], 4.0)
    frames_core.wait_recv()

    def frames_sum(b, carry):
        rows = pl.ds(pl.multiple_of(lax.rem(b, 5) * 64, 64), 64)
        s.fcore[b // 5, rows] = s.fcore[b // 5, rows] + fpart[b // 5, c, rows]
        return carry

    lax.fori_loop(0, 10, frames_sum, 0)
    frames_x = comm.copy(s.fcore.at[1 - x], o.fmine.at[1], 17, 3, comm.to_x)
    comm.go(17, 3, frames_x)
    frames_keep = pltpu.make_async_copy(s.fcore.at[x], o.fmine.at[0], s.keep.at[18])
    frames_keep.start()
    gradient(15, lambda: s.normed[...], lambda cut: s.v[:, cut], 4.0)
    flat = jnp.concatenate([s.ng[...], jnp.zeros((120, 1024), F32)], axis=0).T
    s.nown[...] = flat.reshape(4, 2, 2, 2, 32, 128)
    comm.begin(16, s.nown, False)
    comm.finish()
    text_x.wait_recv()
    frames_x.wait_recv()
    text_keep.wait()
    frames_keep.wait()
    save_gr.wait()


def run_backward_kernel(args):
    S, V, D_SEM = jax.ShapeDtypeStruct, pltpu.VMEM, pltpu.SemaphoreType.DMA
    rows, block = (320, 1024), (32, 1024)
    shapes = dict(
        fin=S((16, 4) + block, BF16), nfin=S((4, 32, 128), F32), fmine=S((2,) + rows, BF16), tmine=S((2, 16, 1024), BF16), gr=S(rows, F32)
    )
    scratch = dict(
        send=D_SEM((18, 8)), recv=D_SEM((18, 8)), own=D_SEM((6,)), keep=D_SEM((19,)), fetch=D_SEM((17,)), load=D_SEM((3,)),
        free=pltpu.SemaphoreType.REGULAR,
        sum=V((4, 4, 2, 2) + block, BF16), core=V((4, 4, 2, 2) + block, BF16), xy=V((16, 4, 2) + block, BF16), cc=V((16, 4) + block, BF16), xw=V((2, 2, 16, 1024), BF16), yw=V((2, 2, 16, 1024), BF16),
        big=V((1792, 1024), BF16),
        nsum=V((4, 2, 2, 32, 128), F32), ncore=V((4, 2, 2, 32, 128), F32), nxy=V((4, 2, 32, 128), F32),
        ncc=V((4, 32, 128), F32), nown=V((4, 2, 2, 2, 32, 128), F32),
        gb=V((8, 1024), F32), r=V(rows, F32), g=V(rows, F32), cot=V(rows, BF16), ctx=V(rows, BF16), q=V(rows, BF16),
        ck=V((64, 1024), BF16), cv=V((64, 1024), BF16), clse=V((4, 1280), F32), nc=V(rows, BF16), text=V((64, 1024), BF16),
        k=V((1280, 1024), BF16), v=V((1280, 1024), BF16), lse=V((4, 1280), F32), normed=V((1280, 1024), BF16), w=V((3, 1024, 1024), BF16),
        bias=V((1280, 640), BF16), cbias=V((64, 640), BF16), ng=V((8, 1024), F32), gr=V(rows, F32), branch=V(rows, BF16),
        up=V(rows, BF16), dq=V(rows, BF16), stacked_q=V((1280, 256), BF16), stacked_g=V((1280, 256), BF16),
        total=V((256, 1280), F32), dw=V((2, 1024, 1024), BF16), tpart=V((2, 2, 16, 1024), BF16), tcore=V((2, 16, 1024), BF16),
        tsum=V((2, 16, 1024), BF16), fcore=V((2,) + rows, BF16),
    )
    apart = dict(seg=pltpu.VMEM, text_len=pltpu.SMEM)
    return pallas(backward_kernel, args, shapes, scratch, apart, dict(collective_id=1))


def finish_kernel(fin, nfin, fmine, tmine, gr, frames, gb, out, o_out, o_frames, o_text, o_gain, o_bias, o_sqkv, o_sout, o_cqkv, o_cout, o_up, o_down):
    def total(u):
        parts = [fin[u, k].astype(F32) for k in range(2 if u in WIDE else 4)]
        return sum(parts[1:], parts[0])

    for ref, first, count in ((o_sqkv, 13, 3), (o_sout, 12, 1), (o_cqkv, 9, 3), (o_cout, 8, 1)):
        for k in range(count):
            ref[:, k * 1024 : (k + 1) * 1024] = total(first + k)
    for k in range(4):
        o_down[k * 32 : (k + 1) * 32, :] = total(DOWN_UNITS[k])
    parts = [total(4 + j) for j in range(4)]

    def put(b, block):
        o_up[:, b * 128 : b * 128 + 128] = block

    shuffle_columns(lambda b: parts[b // 8][:, b % 8 * 128 : b % 8 * 128 + 128], put, True)
    n = ((nfin[0] + nfin[1]) + (nfin[2] + nfin[3])).T
    o_gain[...] = n[:3]
    o_bias[...] = n[3:6]
    o_text[...] = (tmine[0].astype(F32) + tmine[1].astype(F32)).astype(BF16)
    o_out[...] = out[...]
    gain = gb[0:1, :]

    def rows_of(b, rows):
        values = frames[rows, :].astype(F32)
        center = values - jnp.mean(values, axis=-1, keepdims=True)
        scale = lax.rsqrt(jnp.mean(center * center, axis=-1, keepdims=True) + 1e-05)
        hat = center * scale
        h = (fmine[0, rows, :].astype(F32) + fmine[1, rows, :].astype(F32)) * gain
        back = (h - jnp.mean(h, axis=-1, keepdims=True) - hat * jnp.mean(h * hat, axis=-1, keepdims=True)) * scale
        o_frames[rows, :] = (gr[rows, :] + back).astype(BF16)

    tiles(5, 64)(rows_of)


def run_finish_kernel(*args):
    S = jax.ShapeDtypeStruct
    return pl.pallas_call(
        finish_kernel,
        out_shape=[
            S((320, 1024), BF16),
            S((320, 1024), BF16),
            S((16, 1024), BF16),
            S((3, 32), F32),
            S((3, 32), F32),
            S((32, 3072), F32),
            S((32, 1024), F32),
            S((32, 3072), F32),
            S((32, 1024), F32),
            S((32, 4096), F32),
            S((128, 1024), F32),
        ],
        in_specs=[pl.BlockSpec(memory_space=pltpu.VMEM)] * len(args),
        out_specs=[pl.BlockSpec(memory_space=pltpu.VMEM)] * 11,
        compiler_params=pltpu.CompilerParams(vmem_limit_bytes=VMEM_BYTES),
    )(*args)


def fetch_all(norm_gain, norm_bias, self_qkv, self_out, cross_qkv, cross_out, ffn_up, ffn_down):
    first = (
        lax.all_gather(norm_gain, ("dp", "seq"), axis=0, tiled=True),
        lax.all_gather(norm_bias, ("dp", "seq"), axis=0, tiled=True),
        lax.all_gather(self_qkv, ("dp", "seq"), axis=0, tiled=True),
        lax.all_gather(self_out, ("dp", "seq"), axis=0, tiled=True),
    )
    second = (
        lax.all_gather(cross_qkv, ("dp", "seq"), axis=0, tiled=True),
        lax.all_gather(cross_out, ("dp", "seq"), axis=0, tiled=True),
    )
    third = (
        lax.all_gather(ffn_up, ("dp", "seq"), axis=0, tiled=True),
        lax.all_gather(ffn_down, ("dp", "seq"), axis=0, tiled=True),
    )
    return tuple(first) + tuple(second) + tuple(third)


def run_forward(frames, local_seg, frame_seg, text_seg, text_states, offset, weights):
    norm_gain, norm_bias, self_qkv, self_out, cross_qkv, cross_out, ffn_up, ffn_down = weights
    gains = norm_gain.astype(jnp.float32)
    biases = norm_bias.astype(jnp.float32)
    inputs = frames.astype(jnp.float32)
    normed_self = layer_norm(inputs, gains[:, 0], biases[:, 0]).astype(jnp.bfloat16)
    queries = jnp.dot(normed_self, self_qkv[:, :D], preferred_element_type=jnp.float32).astype(
        jnp.bfloat16
    )
    pair_weights = self_qkv[:, D:].reshape(D, 2, D)
    key_value = jnp.einsum(
        "rcd,dje->jrce", normed_self, pair_weights, preferred_element_type=jnp.float32
    ).astype(jnp.bfloat16)
    gathered = lax.all_gather(key_value, "seq", axis=2, tiled=True)
    self_context, self_logsum = lax.map(
        lambda record: attend(
            record[0], record[1], record[2], self_allowed(record[3], record[4], offset)
        ),
        (queries, gathered[0], gathered[1], local_seg, frame_seg),
    )
    self_context = self_context.astype(jnp.bfloat16)
    resid_one = inputs + jnp.dot(self_context, self_out, preferred_element_type=jnp.float32)
    normed_cross = layer_norm(resid_one, gains[:, 1], biases[:, 1]).astype(jnp.bfloat16)
    cross_queries = jnp.dot(
        normed_cross, cross_qkv[:, :D], preferred_element_type=jnp.float32
    ).astype(jnp.bfloat16)
    text_weights = cross_qkv[:, D:].reshape(D, 2, D)
    text_pair = jnp.einsum(
        "rtd,dje->jrte", text_states, text_weights, preferred_element_type=jnp.float32
    ).astype(jnp.bfloat16)
    cross_context, cross_logsum = lax.map(
        lambda record: attend(
            record[0], record[1], record[2], record[3][:, None] == record[4][None, :]
        ),
        (cross_queries, text_pair[0], text_pair[1], local_seg, text_seg),
    )
    cross_context = cross_context.astype(jnp.bfloat16)
    resid_two = resid_one + jnp.dot(cross_context, cross_out, preferred_element_type=jnp.float32)
    normed_ffn = layer_norm(resid_two, gains[:, 2], biases[:, 2]).astype(jnp.bfloat16)
    hidden_pre = jnp.dot(normed_ffn, ffn_up, preferred_element_type=jnp.float32)
    activated = exact_gelu(hidden_pre).astype(jnp.bfloat16)
    outcome = resid_two + jnp.dot(activated, ffn_down, preferred_element_type=jnp.float32)
    saved = (
        inputs,
        normed_self,
        queries,
        gathered,
        self_context,
        self_logsum,
        resid_one,
        normed_cross,
        cross_queries,
        text_pair,
        cross_context,
        cross_logsum,
        resid_two,
        normed_ffn,
        hidden_pre,
        activated,
    )
    return (outcome, saved)


def generic_body(
    frames,
    frame_seg,
    text_states,
    text_len,
    norm_gain,
    norm_bias,
    self_qkv,
    self_out,
    cross_qkv,
    cross_out,
    ffn_up,
    ffn_down,
    cotangent,
):
    width = frames.shape[1]
    offset = lax.axis_index("seq") * width
    local_seg = lax.dynamic_slice_in_dim(frame_seg, offset, width, 1)
    text_seg = text_segments(text_len)
    shards = (norm_gain, norm_bias, self_qkv, self_out, cross_qkv, cross_out, ffn_up, ffn_down)
    weights = fetch_all(*shards)
    outcome, saved = run_forward(
        frames, local_seg, frame_seg, text_seg, text_states, offset, weights
    )
    frames_out = outcome.astype(jnp.bfloat16)
    (
        inputs,
        normed_self,
        queries,
        gathered,
        self_context,
        self_logsum,
        resid_one,
        normed_cross,
        cross_queries,
        text_pair,
        cross_context,
        cross_logsum,
        resid_two,
        normed_ffn,
        hidden_pre,
        activated,
    ) = saved
    gain_full, bias_full, self_full, self_proj, cross_full, cross_proj, up_full, down_full = weights
    gains = gain_full.astype(jnp.float32)
    biases = bias_full.astype(jnp.float32)
    upstream = cotangent.astype(jnp.float32)
    down_grad = jnp.einsum("rcf,rcd->fd", activated, cotangent, preferred_element_type=jnp.float32)
    grad_act = jnp.einsum("rcd,fd->rcf", cotangent, down_full, preferred_element_type=jnp.float32)
    unused_value, gelu_pull = jax.vjp(exact_gelu, hidden_pre)
    grad_pre = gelu_pull(grad_act)[0].astype(jnp.bfloat16)
    up_grad = jnp.einsum("rcd,rcf->df", normed_ffn, grad_pre, preferred_element_type=jnp.float32)
    grad_normed = jnp.einsum("rcf,df->rcd", grad_pre, up_full, preferred_element_type=jnp.float32)
    grad_back, gain_two, bias_two = norm_back(resid_two, gains[:, 2], biases[:, 2], grad_normed)
    grad_resid_two = upstream + grad_back
    ffn_shares = (
        lax.psum_scatter(up_grad, ("dp", "seq"), scatter_dimension=0, tiled=True),
        lax.psum_scatter(down_grad, ("dp", "seq"), scatter_dimension=0, tiled=True),
    )
    branch_two = grad_resid_two.astype(jnp.bfloat16)
    cross_out_grad = jnp.einsum(
        "rcd,rce->de", cross_context, branch_two, preferred_element_type=jnp.float32
    )
    grad_context = jnp.einsum(
        "rce,de->rcd", branch_two, cross_proj, preferred_element_type=jnp.float32
    ).astype(jnp.bfloat16)
    grad_cross_q, grad_cross_k, grad_cross_v = lax.map(
        lambda record: attend_back(
            record[0],
            record[1],
            record[2],
            record[3][:, None] == record[4][None, :],
            record[5],
            record[6],
        ),
        (
            cross_queries,
            text_pair[0],
            text_pair[1],
            local_seg,
            text_seg,
            cross_logsum,
            grad_context,
        ),
    )
    text_joined = jnp.transpose(jnp.concatenate([grad_cross_k, grad_cross_v], axis=2), (1, 0, 2))
    text_summed = lax.psum_scatter(
        text_joined.astype(jnp.bfloat16), "seq", scatter_dimension=0, tiled=True
    ).astype(jnp.float32)
    text_shares = jnp.transpose(text_summed, (1, 0, 2)).astype(jnp.bfloat16)
    share = text_shares.shape[1]
    text_part = lax.dynamic_slice_in_dim(text_states, lax.axis_index("seq") * share, share, 1)
    text_kv_grad = jnp.einsum(
        "rtd,rte->de", text_part, text_shares, preferred_element_type=jnp.float32
    )
    text_grad = jnp.einsum(
        "rte,de->rtd", text_shares, cross_full[:, D:], preferred_element_type=jnp.float32
    ).astype(jnp.bfloat16)
    grad_cross_q = grad_cross_q.astype(jnp.bfloat16)
    cross_q_grad = jnp.einsum(
        "rcd,rce->de", normed_cross, grad_cross_q, preferred_element_type=jnp.float32
    )
    cross_qkv_grad = jnp.concatenate([cross_q_grad, text_kv_grad], axis=1)
    grad_normed = jnp.einsum(
        "rce,de->rcd", grad_cross_q, cross_full[:, :D], preferred_element_type=jnp.float32
    )
    grad_back, gain_one, bias_one = norm_back(resid_one, gains[:, 1], biases[:, 1], grad_normed)
    grad_resid_one = grad_resid_two + grad_back
    cross_shares = (
        lax.psum_scatter(cross_qkv_grad, ("dp", "seq"), scatter_dimension=0, tiled=True),
        lax.psum_scatter(cross_out_grad, ("dp", "seq"), scatter_dimension=0, tiled=True),
    )
    branch_one = grad_resid_one.astype(jnp.bfloat16)
    self_out_grad = jnp.einsum(
        "rcd,rce->de", self_context, branch_one, preferred_element_type=jnp.float32
    )
    grad_context = jnp.einsum(
        "rce,de->rcd", branch_one, self_proj, preferred_element_type=jnp.float32
    ).astype(jnp.bfloat16)
    grad_self_q, grad_self_k, grad_self_v = lax.map(
        lambda record: attend_back(
            record[0],
            record[1],
            record[2],
            self_allowed(record[3], record[4], offset),
            record[5],
            record[6],
        ),
        (queries, gathered[0], gathered[1], local_seg, frame_seg, self_logsum, grad_context),
    )
    joined = jnp.concatenate([grad_self_k, grad_self_v], axis=2)
    summed = lax.psum_scatter(
        jnp.transpose(joined, (1, 0, 2)).astype(jnp.bfloat16),
        "seq",
        scatter_dimension=0,
        tiled=True,
    ).astype(jnp.float32)
    key_shares = jnp.transpose(summed, (1, 0, 2)).astype(jnp.bfloat16)
    all_grads = jnp.concatenate([grad_self_q.astype(jnp.bfloat16), key_shares], axis=2)
    self_qkv_grad = jnp.einsum(
        "rcd,rce->de", normed_self, all_grads, preferred_element_type=jnp.float32
    )
    grad_normed = jnp.einsum(
        "rce,de->rcd", all_grads, self_full, preferred_element_type=jnp.float32
    )
    grad_back, gain_zero, bias_zero = norm_back(inputs, gains[:, 0], biases[:, 0], grad_normed)
    frames_grad = (grad_resid_one + grad_back).astype(jnp.bfloat16)
    gain_grad = jnp.stack([gain_zero, gain_one, gain_two], axis=1)
    bias_grad = jnp.stack([bias_zero, bias_one, bias_two], axis=1)
    self_shares = (
        lax.psum_scatter(gain_grad, ("dp", "seq"), scatter_dimension=0, tiled=True),
        lax.psum_scatter(bias_grad, ("dp", "seq"), scatter_dimension=0, tiled=True),
        lax.psum_scatter(self_qkv_grad, ("dp", "seq"), scatter_dimension=0, tiled=True),
        lax.psum_scatter(self_out_grad, ("dp", "seq"), scatter_dimension=0, tiled=True),
    )
    return (
        frames_out,
        frames_grad,
        text_grad,
        self_shares[0],
        self_shares[1],
        self_shares[2],
        self_shares[3],
        cross_shares[0],
        cross_shares[1],
        ffn_shares[0],
        ffn_shares[1],
    )


def fast_body(
    frames,
    frame_seg,
    text_states,
    text_len,
    norm_gain,
    norm_bias,
    self_qkv,
    self_out,
    cross_qkv,
    cross_out,
    ffn_up,
    ffn_down,
    cotangent,
):
    args = dict(
        frames=frames[0],
        gain=norm_gain.T,
        shift=norm_bias.T,
        sqkv=self_qkv,
        sout=self_out,
        cqkv=cross_qkv,
        cout=cross_out,
        up=ffn_up,
        down=ffn_down.reshape(4, 32, D),
        cot=cotangent[0],
        text=text_states[0],
        seg=frame_seg,
        text_len=text_len,
    )
    f = types.SimpleNamespace(**run_forward_kernel(args))
    a = types.SimpleNamespace(**args)
    units = (4, 4, 2, 2, 2, 32, D)
    back = run_backward_kernel(
        dict(
            ddown=f.ddown.reshape(units),
            slope=f.slope,
            nf=f.nf,
            down=f.down,
            up=f.up,
            cot=a.cot,
            gb=f.gb,
            r2=f.r2,
            r1=f.r1,
            cctx=f.cctx,
            ctx=f.ctx,
            cq=f.cq,
            ck=f.ck,
            cv=f.cv,
            clse=f.clse,
            nc=f.nc,
            text=a.text,
            q=f.q,
            k=f.k,
            v=f.v,
            lse=f.lse,
            normed=f.normed,
            frames=f.frames,
            cout=f.cout,
            cqkv=f.cqkv,
            sout=f.sout,
            sqkv=f.sqkv,
            seg=a.seg,
            text_len=a.text_len,
        )
    )
    b = types.SimpleNamespace(**back)
    outs = run_finish_kernel(b.fin, b.nfin, b.fmine, b.tmine, b.gr, frames[0], f.gb, f.out)
    return (outs[0][None], outs[1][None], outs[2][None], outs[3].T, outs[4].T) + tuple(outs[5:])


def solution(mesh):
    return jax.shard_map(
        fast_body if dict(mesh.shape) == {"dp": 8, "seq": 4} else generic_body,
        mesh=mesh,
        in_specs=(
            P("dp", "seq", None),
            P("dp", None),
            P("dp", None, None),
            P("dp", None),
            P(("dp", "seq"), None),
            P(("dp", "seq"), None),
            P(("dp", "seq"), None),
            P(("dp", "seq"), None),
            P(("dp", "seq"), None),
            P(("dp", "seq"), None),
            P(("dp", "seq"), None),
            P(("dp", "seq"), None),
            P("dp", "seq", None),
        ),
        out_specs=(
            P("dp", "seq", None),
            P("dp", "seq", None),
            P("dp", "seq", None),
            P(("dp", "seq"), None),
            P(("dp", "seq"), None),
            P(("dp", "seq"), None),
            P(("dp", "seq"), None),
            P(("dp", "seq"), None),
            P(("dp", "seq"), None),
            P(("dp", "seq"), None),
            P(("dp", "seq"), None),
        ),
        check_vma=False,
    )
```

```python
import types

import jax
import jax.numpy as jnp
from jax import lax
from jax.experimental import pallas as pl
from jax.experimental.pallas import tpu as pltpu
from jax.sharding import PartitionSpec as P

D = 1024
HEADS = 16
HEAD_DIM = 64
TEXT_LEN = 64


def layer_norm(values, gain, bias):
    center = values - jnp.mean(values, axis=-1, keepdims=True)
    spread = jnp.mean(center * center, axis=-1, keepdims=True)
    return center * lax.rsqrt(spread + 1e-05) * gain + bias


def norm_back(values, gain, bias, upstream):
    unused_value, pullback = jax.vjp(layer_norm, values, gain, bias)
    return pullback(upstream)


def exact_gelu(values):
    return jax.nn.gelu(values, approximate=False)


def split_heads(values):
    return values.reshape(values.shape[0], HEADS, HEAD_DIM)


def text_segments(text_len):
    bounds = jnp.cumsum(text_len, axis=1)
    positions = jnp.arange(TEXT_LEN, dtype=jnp.int32)
    return jnp.sum((positions[None, :, None] >= bounds[:, None, :]).astype(jnp.int32), axis=2)


def self_allowed(local_seg, full_seg, offset):
    row_pos = offset + jnp.arange(local_seg.shape[0], dtype=jnp.int32)
    col_pos = jnp.arange(full_seg.shape[0], dtype=jnp.int32)
    return (row_pos[:, None] >= col_pos[None, :]) & (local_seg[:, None] == full_seg[None, :])


def masked_scores(queries, keys_in, allowed):
    factor = HEAD_DIM ** (-0.5)
    scores = (
        jnp.einsum(
            "qhe,khe->hqk",
            split_heads(queries),
            split_heads(keys_in),
            preferred_element_type=jnp.float32,
        )
        * factor
    )
    return jnp.where(allowed[None], scores, -1e30)


def attend(queries, keys_in, values, allowed):
    scores = masked_scores(queries, keys_in, allowed)
    highest = jnp.max(scores, axis=-1, keepdims=True)
    powered = jnp.exp(scores - highest)
    totals = jnp.sum(powered, axis=-1, keepdims=True)
    weights = (powered / totals).astype(jnp.bfloat16)
    context = jnp.einsum(
        "hqk,khe->qhe", weights, split_heads(values), preferred_element_type=jnp.float32
    )
    return (context.reshape(queries.shape[0], -1), highest + jnp.log(totals))


def attend_back(queries, keys_in, values, allowed, logsum, upstream):
    factor = HEAD_DIM ** (-0.5)
    probs_full = jnp.exp(masked_scores(queries, keys_in, allowed) - logsum)
    grad_heads = split_heads(upstream)
    grad_probs = jnp.einsum(
        "qhe,khe->hqk", grad_heads, split_heads(values), preferred_element_type=jnp.float32
    )
    row_inner = jnp.sum(probs_full * grad_probs, axis=-1, keepdims=True)
    grad_scores = (probs_full * (grad_probs - row_inner)).astype(jnp.bfloat16)
    grad_queries = (
        jnp.einsum(
            "hqk,khe->qhe", grad_scores, split_heads(keys_in), preferred_element_type=jnp.float32
        )
        * factor
    )
    grad_keys = (
        jnp.einsum(
            "hqk,qhe->khe", grad_scores, split_heads(queries), preferred_element_type=jnp.float32
        )
        * factor
    )
    grad_values = jnp.einsum(
        "hqk,qhe->khe",
        probs_full.astype(jnp.bfloat16),
        grad_heads,
        preferred_element_type=jnp.float32,
    )
    return (
        grad_queries.reshape(queries.shape[0], -1),
        grad_keys.reshape(keys_in.shape[0], -1),
        grad_values.reshape(values.shape[0], -1),
    )


F32, BF16 = jnp.float32, jnp.bfloat16
MESH = pl.DeviceIdType.MESH
VMEM_BYTES = 64 * 2**20
BLOCK = 256
LEAD = 6
PACE_FORWARD = 3.5
PACE_BACKWARD = 3.5


def place():
    dp, seq = lax.axis_index("dp"), lax.axis_index("seq")
    return dp // 2, lax.rem(dp, 2), seq // 2, lax.rem(seq, 2)


def device(z, y, x, c):
    return (z * 2 + y, x * 2 + c)


def greet(z, y, x, c):
    barrier = pltpu.get_barrier_semaphore()
    others = [device(lax.rem(z + k, 4), y, x, c) for k in (1, 2, 3)]
    others += [device(z, 1 - y, x, c), device(z, y, 1 - x, c), device(z, y, x, 1 - c)]
    for other in others:
        pl.semaphore_signal(barrier, inc=1, device_id=other, device_id_type=MESH)
    pl.semaphore_wait(barrier, len(others))


def dot_nn(a, b):
    return jnp.dot(a, b, preferred_element_type=F32)


def dot_nt(a, b):
    return lax.dot_general(a, b, (((1,), (1,)), ((), ())), preferred_element_type=F32)


def dot_tn(a, b):
    return lax.dot_general(a, b, (((0,), (0,)), ((), ())), preferred_element_type=F32)


def tiles(count, size):
    def run(step):
        def one(i, carry):
            step(i, pl.ds(pl.multiple_of(i * size, size), size))
            return carry

        lax.fori_loop(0, count, one, 0)

    return run


def normalize(block, gain, bias):
    center = block - jnp.mean(block, axis=-1, keepdims=True)
    spread = jnp.mean(center * center, axis=-1, keepdims=True)
    return center * lax.rsqrt(spread + 1e-05) * gain + bias


def stack_heads(dst, src, group, factor):
    rows = src.shape[0]
    part = src[:, group * 256 : group * 256 + 256]
    if factor != 1.0:
        part = part * jnp.asarray(factor, part.dtype)
    head = lax.broadcasted_iota(jnp.int32, part.shape, 1) // HEAD_DIM
    for h in range(4):
        dst[h * rows : (h + 1) * rows, :] = jnp.where(head == h, part, jnp.zeros_like(part))


def unstack_heads(wide, rows):
    parts = [wide[h * 64 : (h + 1) * 64, h * rows : (h + 1) * rows] for h in range(4)]
    return jnp.concatenate(parts, axis=0).T


def attend_group(group, q, k, v, bias, stacked, scores, total, context, logsum, between):
    rows, keys = q.shape[0], k.shape[0]
    size = min(BLOCK, keys)
    cols = slice(group * 256, group * 256 + 256)
    stack_heads(stacked, q, group, HEAD_DIM**-0.5)

    def score(i, highest):
        at = pl.ds(pl.multiple_of(i * size, size), size)
        s = dot_nt(k[at, cols], stacked[...]) + bias[at, :].astype(F32)
        scores[at, :] = s
        return jnp.maximum(highest, jnp.max(s, axis=0, keepdims=True))

    highest = lax.fori_loop(0, keys // size, score, jnp.full((1, 4 * rows), -3e38, F32))
    between()
    total[...] = jnp.zeros_like(total)

    def weigh(i, summed):
        at = pl.ds(pl.multiple_of(i * size, size), size)
        p = jnp.exp(scores[at, :] - highest)
        total[...] += dot_tn(v[at, cols], p.astype(BF16))
        return summed + jnp.sum(p, axis=0, keepdims=True)

    summed = lax.fori_loop(0, keys // size, weigh, jnp.zeros((1, 4 * rows), F32))
    logsum[group : group + 1, :] = highest + jnp.log(summed)
    context[:, cols] = unstack_heads(total[...] / summed, rows).astype(BF16)


class Gathering:
    def __init__(self, at, units, over_y, wide, send_sem, recv_sem, own_sem):
        self.at, self.units, self.n = at, units, len(units)
        self.over_y, self.wide = over_y, wide
        self.order = [u for u in range(self.n) if u not in wide]
        self.send_sem, self.recv_sem, self.own_sem = send_sem, recv_sem, own_sem
        self.sent, self.step, self.spreads, self.since = [], 0, False, 0.0
        z, y, x, c = at
        self.to_x, self.to_y, self.to_c = device(z, y, 1 - x, c), device(z, 1 - y, x, c), device(z, y, x, 1 - c)

    def copy(self, src, dst, u, k, dev):
        return pltpu.make_async_remote_copy(
            src_ref=src,
            dst_ref=dst,
            send_sem=self.send_sem.at[u, k],
            recv_sem=self.recv_sem.at[u, k],
            device_id=dev,
            device_id_type=MESH,
        )

    def go(self, copy):
        copy.start()
        self.sent.append(copy)

    def same(self, u, k, dev, *spot):
        view = self.units[u][1](*spot)
        return self.copy(view, view, u, k, dev)

    def across(self, u, k):
        z, y, x, c = self.at
        src, dst = self.units[u][0], self.units[u][1](z, y, x, c)
        return self.copy(src, dst, u, k - 1, device(lax.rem(z + k, 4), y, x, c))

    def own(self, u):
        return pltpu.make_async_copy(self.units[u][0], self.units[u][1](*self.at), self.own_sem.at[u])

    def first(self, p):
        if p < len(self.order):
            u = self.order[p]
            self.own(u).start()
            for k in (1, 2, 3):
                self.go(self.across(u, k))

    def cuts(self, u):
        if u in self.over_y:
            return pl.ds(0, 4), None
        return pl.ds(0, 2), pl.ds(2, 2)

    def spread(self, p):
        z, y, x, c = self.at
        every, u, same, go = pl.ds(0, 4), self.order[p], self.same, self.go
        for k in (1, 2, 3):
            self.across(u, k).wait_recv()
        self.own(u).wait()
        go(same(u, 3, self.to_x, every, y, x, c))
        go(same(u, 4, self.to_y, every, y, x, c))
        go(same(u, 5, self.to_c, every, y, x, c))
        self.first(p + LEAD)

    def work(self, us):
        self.since += us
        if self.since >= PACE_FORWARD:
            self.pump()

    def pump(self):
        z, y, x, c = self.at
        every = pl.ds(0, 4)
        self.since = 0.0
        t, n, same, go = self.step, len(self.order), self.same, self.go
        if t >= n + 2:
            return
        if not self.spreads:
            self.spreads = True
            if t < n:
                self.spread(t)
            return
        self.spreads = False
        self.step += 1
        if 0 <= t - 1 < n:
            u = self.order[t - 1]
            low, high = self.cuts(u)
            same(u, 3, self.to_x, every, y, 1 - x, c).wait_recv()
            go(same(u, 6, self.to_y, low, y, 1 - x, c))
            go(same(u, 7, self.to_c, every, y, 1 - x, c))
            same(u, 4, self.to_y, every, 1 - y, x, c).wait_recv()
            if high is not None:
                go(same(u, 8, self.to_x, high, 1 - y, x, c))
            go(same(u, 9, self.to_c, every, 1 - y, x, c))
        if 0 <= t - 2 < n:
            u = self.order[t - 2]
            low, high = self.cuts(u)
            same(u, 6, self.to_y, low, 1 - y, 1 - x, c).wait_recv()
            go(same(u, 10, self.to_c, low, 1 - y, 1 - x, c))
            if high is not None:
                same(u, 8, self.to_x, high, 1 - y, 1 - x, c).wait_recv()
                go(same(u, 11, self.to_c, high, 1 - y, 1 - x, c))
        for u, steps in self.wide.items():
            for stage in range(4):
                if steps[stage] == t:
                    self.widen(u, stage)

    def half(self, u, k, dev, h, *spot):
        view = self.units[u][1](*spot).at[h * 16 : h * 16 + 16]
        return self.copy(view, view, u, k, dev)

    def plane(self, u, k, dev, zz, cc):
        return self.same(u, k, dev, zz, pl.ds(0, 2), pl.ds(0, 2), cc)

    def widen(self, u, stage):
        z, y, x, c = self.at
        go = self.go
        if stage == 0:
            self.own(u).start()
            src, dst = self.units[u][0], self.units[u][1](z, y, x, c)
            go(self.copy(src, dst, u, 0, self.to_x))
            go(self.copy(src, dst, u, 1, self.to_y))
        elif stage == 1:
            self.same(u, 0, self.to_x, z, y, 1 - x, c).wait_recv()
            go(self.half(u, 2, self.to_y, 0, z, y, 1 - x, c))
            self.same(u, 1, self.to_y, z, 1 - y, x, c).wait_recv()
            go(self.half(u, 3, self.to_x, 1, z, 1 - y, x, c))
        elif stage == 2:
            self.own(u).wait()
            self.half(u, 2, self.to_y, 0, z, 1 - y, 1 - x, c).wait_recv()
            self.half(u, 3, self.to_x, 1, z, 1 - y, 1 - x, c).wait_recv()
            for k in (1, 2, 3):
                go(self.plane(u, 3 + k, device(lax.rem(z + k, 4), y, x, c), z, c))
            go(self.plane(u, 7, self.to_c, z, c))
        else:
            for k in (1, 2, 3):
                other = lax.rem(z + 4 - k, 4)
                self.plane(u, 3 + k, self.to_c, other, c).wait_recv()
                go(self.plane(u, 7 + k, self.to_c, other, c))

    def need(self, u):
        z, y, x, c = self.at
        every = pl.ds(0, 4)
        if u in self.wide:
            while self.step <= self.wide[u][3]:
                self.pump()
            self.plane(u, 7, self.to_c, z, 1 - c).wait_recv()
            for k in (1, 2, 3):
                self.plane(u, 7 + k, self.to_c, lax.rem(z + 4 - k, 4), 1 - c).wait_recv()
            return
        while self.step <= self.order.index(u) + 2:
            self.pump()
        low, high = self.cuts(u)
        self.same(u, 5, self.to_c, every, y, x, 1 - c).wait_recv()
        self.same(u, 7, self.to_c, every, y, 1 - x, 1 - c).wait_recv()
        self.same(u, 9, self.to_c, every, 1 - y, x, 1 - c).wait_recv()
        self.same(u, 10, self.to_c, low, 1 - y, 1 - x, 1 - c).wait_recv()
        if high is not None:
            self.same(u, 11, self.to_c, high, 1 - y, 1 - x, 1 - c).wait_recv()


def same_clip(seg, seq):
    own = seg[:, 0:320]
    for k in range(1, 4):
        own = jnp.where(seq == k, seg[:, k * 320 : (k + 1) * 320], own)

    def down(b):
        part = seg[:, pl.ds(pl.multiple_of(b * 128, 128), 128)]
        return jnp.broadcast_to(part, (128, 128)).T[:, :1]

    return own, down


def set_masks(i, seq, bias, text_bias, copies):
    own, down = same_clip(i.seg, seq)

    def mask(b, rows):
        key = lax.broadcasted_iota(jnp.int32, (128, 320), 0) + b * 128
        query = lax.broadcasted_iota(jnp.int32, (128, 320), 1) + seq * 320
        seen = (key <= query) & (down(b) == own)
        block = jnp.where(seen, 0.0, -1e30).astype(F32)
        bias[rows, :] = jnp.concatenate([block] * copies, axis=1).astype(BF16)

    tiles(10, 128)(mask)
    slot = lax.broadcasted_iota(jnp.int32, (TEXT_LEN, 320), 0)
    clip = jnp.zeros((TEXT_LEN, 320), jnp.int32)
    bound = jnp.int32(0)
    for k in range(4):
        bound = bound + i.text_len[0, k]
        clip = clip + (slot >= bound).astype(jnp.int32)
    block = jnp.where(clip == own, 0.0, -1e30).astype(F32)
    text_bias[...] = jnp.concatenate([block] * copies, axis=1).astype(BF16)


def shuffle_columns(part, put, back):
    lane = lax.broadcasted_iota(jnp.int32, (32, 128), 1) // 32
    for b in range(32):
        block = jnp.zeros((32, 128), F32)
        for q in range(4):
            source, quarter = (q * 8 + b // 4, b % 4) if back else (b % 8 * 4 + q, b // 8)
            chunk = part(source)
            moved = pltpu.roll(chunk, (q - quarter) % 4 * 32, 1) if q != quarter else chunk
            block = jnp.where(lane == q, moved, block)
        put(b, block)


def forward_kernel(i, o, s):
    at = place()
    z, y, x, c = at
    seq = x * 2 + c
    units = [(s.nin, lambda zz, yy, xx, cc: o.norms.at[zz, yy, xx, cc])]

    def columns(shard, full, count):
        for k in range(count):
            cut = pl.ds(k * 1024, 1024)
            units.append(
                (shard.at[:, cut], lambda zz, yy, xx, cc, cut=cut: full.at[zz, yy, xx, cc, :, cut])
            )

    columns(i.sqkv, o.sqkv, 3)
    columns(i.sout, o.sout, 1)
    columns(i.cqkv, o.cqkv, 3)
    columns(i.cout, o.cout, 1)
    columns(s.upin, o.up, 4)
    for k in range(4):
        units.append(
            (i.down.at[k], lambda zz, yy, xx, cc, k=k: o.down.at[zz, yy, xx, cc, k])
        )
        wide = {12: (0, 1, 2, 10), 16: (6, 7, 8, 16)}
    comm = Gathering(at, units, (1, 2), wide, s.send, s.recv, s.own)
    up_copy = pltpu.make_async_copy(i.up, s.upraw, s.own.at[comm.n + 3])
    up_copy.start()
    s.flat[...] = jnp.zeros_like(s.flat)
    s.flat[0:3, 0:32] = i.gain[...].astype(F32)
    s.flat[3:6, 0:32] = i.shift[...].astype(F32)
    s.nin[...] = s.flat[...].T[:32].astype(BF16)
    greet(*at)
    fr = s.frames
    f = comm.n

    def share(k, dev, xx, cc):
        view = fr.at[xx, cc]
        return comm.copy(view, view, f, k, dev)

    own_frames = pltpu.make_async_copy(i.frames, fr.at[x, c], s.own.at[f])
    own_frames.start()
    cot_copy = pltpu.make_async_copy(i.cot, s.cot, s.own.at[f + 1])
    cot_copy.start()
    text_copy = pltpu.make_async_copy(i.text, s.text, s.own.at[f + 2])
    text_copy.start()
    for u in range(LEAD):
        comm.first(u)
    own_frames.wait()
    comm.go(share(0, comm.to_x, x, c))
    comm.go(share(1, comm.to_c, x, c))
    up_copy.wait()

    def put_up(b, block):
        s.upin[:, b * 128 : b * 128 + 128] = block.astype(BF16)

    shuffle_columns(lambda b: s.upraw[:, b * 128 : b * 128 + 128].astype(F32), put_up, False)

    saves = []

    def save(src, dst):
        copy = pltpu.make_async_copy(src, dst, s.save.at[len(saves)])
        copy.start()
        saves.append(copy)

    set_masks(i, seq, s.bias, s.cbias, 4)

    def weight(u, where):
        comm.need(u)
        src = units[u][1](pl.ds(0, 4), pl.ds(0, 2), pl.ds(0, 2), pl.ds(0, 2))
        dst = s.w.at[where]
        copy = pltpu.make_async_copy(src, dst.reshape(4, 2, 2, 2, 32, 1024), s.load.at[u])
        copy.start()
        copy.wait()
        return dst

    def norm(dst, src_block, k, count):
        gain, bias = s.gb[k : k + 1, :], s.gb[3 + k : 4 + k, :]

        def one(b, rows):
            dst[rows, :] = normalize(src_block(b, rows), gain, bias).astype(BF16)

        tiles(count, 64)(one)

    share(0, comm.to_x, 1 - x, c).wait_recv()
    comm.go(share(2, comm.to_c, 1 - x, c))
    comm.need(0)
    copy = pltpu.make_async_copy(o.norms, s.norms.reshape(4, 2, 2, 2, 32, 128), s.load.at[0])
    copy.start()
    copy.wait()
    s.gb[...] = s.norms[...].astype(F32).T[:8]
    share(1, comm.to_c, x, 1 - c).wait_recv()
    share(2, comm.to_c, 1 - x, 1 - c).wait_recv()
    normed = s.normed

    def frame_block(b, rows):
        return fr[b // 10, lax.rem(b // 5, 2), pl.ds(pl.multiple_of(lax.rem(b, 5) * 64, 64), 64), :].astype(F32)

    norm(normed, frame_block, 0, 20)
    comm.work(4.0)
    save(s.gb, o.gb)
    save(fr, o.frames)
    save(normed, o.normed)

    mine = pl.ds(pl.multiple_of(seq * 320, 64), 320)

    def project(dst, src, w, rows):
        def one(n, cut):
            dst[:, cut] = dot_nn(src[rows, :], w[:, cut]).astype(BF16)

        tiles(4, 256)(one)

    def project_all(dst, w):
        def one(b, rows):
            def two(n, cut):
                dst[rows, cut] = dot_nn(normed[rows, :], w[:, cut]).astype(BF16)

            tiles(4, 256)(two)

        for b in range(4):
            one(b, pl.ds(b * 320, 320))
            comm.work(1.8)

    every_row = pl.ds(0, 320)
    q, k, v = s.q, s.k, s.v
    project(q, normed, weight(1, 0), mine)
    project_all(k, weight(2, 1))
    project_all(v, weight(3, 2))
    save(q, o.q)
    save(k, o.k)
    save(v, o.v)
    for g in range(4):
        attend_group(
            g, q, k, v, s.bias, s.stacked, s.scores, s.total, s.ctx, s.lse, lambda: comm.work(2.0)
        )
        comm.work(2.0)
    save(s.ctx, o.ctx)
    save(s.lse, o.lse)

    def add_project(dst, base, src, w):
        def one(n, cut):
            dst[:, cut] = base(cut) + dot_nn(src[...], w[:, cut])

        tiles(4, 256)(one)

    add_project(s.r1, lambda cut: fr[x, c, :, cut].astype(F32), s.ctx, weight(4, 0))
    save(s.r1, o.r1)
    norm(s.nc, lambda b, rows: s.r1[rows, :], 1, 5)
    save(s.nc, o.nc)
    project(s.cq, s.nc, weight(5, 1), every_row)
    save(s.cq, o.cq)
    text_copy.wait()
    text_rows = pl.ds(0, TEXT_LEN)
    project(s.ck, s.text, weight(6, 2), text_rows)
    project(s.cv, s.text, weight(7, 0), text_rows)
    save(s.ck, o.ck)
    save(s.cv, o.cv)
    for g in range(4):
        attend_group(
            g,
            s.cq,
            s.ck,
            s.cv,
            s.cbias,
            s.stacked,
            s.scores,
            s.total,
            s.cctx,
            s.clse,
            lambda: None,
        )
        comm.work(0.6)
    save(s.cctx, o.cctx)
    save(s.clse, o.clse)
    add_project(s.r2, lambda cut: s.r1[:, cut], s.cctx, weight(8, 1))
    save(s.r2, o.r2)
    norm(s.nf, lambda b, rows: s.r2[rows, :], 2, 5)
    cot_copy.wait()
    act, slope, nf, cot = s.act, s.slope, s.nf, s.cot
    save(nf, o.nf)
    grads = []

    def gradient(dst, left, right):
        m = len(grads)
        if m >= 2:
            grads[m - 2].wait()
        stage = s.stage.at[m % 2]

        def one(n, cut):
            stage[:, cut] = dot_tn(left(), right(cut)).astype(BF16)

        tiles(4, 256)(one)
        copy = pltpu.make_async_copy(stage, dst, s.grad.at[m])
        copy.start()
        grads.append(copy)

    for j in range(4):
        w = weight(9 + j, j % 3)

        def one(n, cut):
            h = dot_nn(nf[...], w[:, cut])
            below = 0.5 * (1.0 + lax.erf(h * 0.7071067811865476))
            act[j, :, cut] = (h * below).astype(BF16)
            slope[j * 320 : (j + 1) * 320, cut] = (
                below + h * jnp.exp(-0.5 * h * h) * 0.3989422804014327
            ).astype(BF16)

        one(0, pl.ds(0, 512))
        comm.work(1.75)
        one(1, pl.ds(512, 512))
        comm.work(1.75)
        gradient(o.ddown.at[j], lambda: act[j], lambda cut: cot[:, cut])
        comm.work(2.0)
    save(slope, o.slope)
    for copy in saves:
        copy.wait()
    for j in range(4):
        w = weight(13 + j, j % 3)

        def onward(n, cut):
            s.r2[:, cut] = s.r2[:, cut] + dot_nn(act[j], w[:, cut])

        tiles(4, 256)(onward)
    s.out[...] = s.r2[...].astype(BF16)
    copy = pltpu.make_async_copy(s.out, o.out, s.save.at[len(saves)])
    copy.start()
    copy.wait()
    for copy in grads[-2:]:
        copy.wait()
    for copy in comm.sent:
        copy.wait_send()


def pallas(kernel, args, shapes, scratch, apart, params):
    def named(*refs):
        a, b = len(args), len(args) + len(shapes)
        kernel(
            types.SimpleNamespace(**dict(zip(args, refs[:a]))),
            types.SimpleNamespace(**dict(zip(shapes, refs[a:b]))),
            types.SimpleNamespace(**dict(zip(scratch, refs[b:]))),
        )

    outs = pl.pallas_call(
        named,
        out_shape=list(shapes.values()),
        in_specs=[pl.BlockSpec(memory_space=apart.get(n, pl.ANY)) for n in args],
        out_specs=[pl.BlockSpec(memory_space=pl.ANY)] * len(shapes),
        scratch_shapes=list(scratch.values()),
        compiler_params=pltpu.CompilerParams(
            has_side_effects=True, vmem_limit_bytes=VMEM_BYTES, **params
        ),
    )(*args.values())
    return dict(zip(shapes, outs))


def run_forward_kernel(args):
    S, V, D_SEM = jax.ShapeDtypeStruct, pltpu.VMEM, pltpu.SemaphoreType.DMA
    a = types.SimpleNamespace(**args)
    rows = (320, 1024)
    scratch = dict(
        send=D_SEM((18, 12)), recv=D_SEM((18, 12)), own=D_SEM((21,)), save=D_SEM((24,)), load=D_SEM((17,)), grad=D_SEM((4,)),
        frames=V((2, 2, 320, 1024), BF16), cot=V(rows, BF16), text=V((64, 1024), BF16), norms=V((1024, 128), BF16), gb=V((8, 1024), F32),
        bias=V((1280, 1280), BF16), cbias=V((64, 1280), BF16), w=V((3, 1024, 1024), BF16), normed=V((1280, 1024), BF16),
        q=V(rows, BF16), k=V((1280, 1024), BF16), v=V((1280, 1024), BF16), stacked=V((1280, 256), BF16), scores=V((1280, 1280), F32),
        total=V((256, 1280), F32), ctx=V(rows, BF16), lse=V((4, 1280), F32), r1=V(rows, F32), nc=V(rows, BF16), cq=V(rows, BF16),
        ck=V((64, 1024), BF16), cv=V((64, 1024), BF16), cctx=V(rows, BF16), clse=V((4, 1280), F32), r2=V(rows, F32), nf=V(rows, BF16),
        act=V((4, 320, 1024), BF16), slope=V((1280, 1024), BF16), out=V(rows, BF16), nin=V((32, 128), BF16), flat=V((128, 128), F32),
        upraw=V((32, 4096), BF16), upin=V((32, 4096), BF16), stage=V((2, 1024, 1024), BF16),
    )
    m = types.SimpleNamespace(**scratch)
    shapes = dict(norms=m.nin, sqkv=a.sqkv, sout=a.sout, cqkv=a.cqkv, cout=a.cout, up=a.up, down=a.down)
    shapes = {n: S((4, 2, 2, 2) + v.shape, BF16) for n, v in shapes.items()}
    saved = dict(
        gb=m.gb, frames=m.frames, normed=m.normed, q=m.q, k=m.k, v=m.v, ctx=m.ctx, lse=m.lse, r1=m.r1, nc=m.nc, cq=m.cq, ck=m.ck,
        cv=m.cv, cctx=m.cctx, clse=m.clse, r2=m.r2, out=m.out, nf=m.nf, slope=m.slope,
    )
    shapes.update({n: S(v.shape, v.dtype) for n, v in saved.items()})
    shapes.update(ddown=S((4, 1024, 1024), BF16))
    apart = dict(seg=pltpu.VMEM, gain=pltpu.VMEM, shift=pltpu.VMEM, text_len=pltpu.SMEM)
    return pallas(forward_kernel, args, shapes, scratch, apart, dict(collective_id=0))


def attend_back_group(group, q, k, v, up, context, bias, logsum, stacked_q, stacked_g, total, grad_q, between):
    rows, keys = q.shape[0], k.shape[0]
    size = min(BLOCK, keys)
    cols = slice(group * 256, group * 256 + 256)
    stack_heads(stacked_q, q, group, HEAD_DIM**-0.5)
    stack_heads(stacked_g, up, group, 1.0)
    four = jnp.concatenate([context[:, cols].astype(F32)] * 4, axis=0)
    inner = lax.dot_general(
        jnp.ones((8, 256), F32),
        stacked_g[...].astype(F32) * four,
        (((1,), (1,)), ((), ())),
        precision=lax.Precision.HIGHEST,
        preferred_element_type=F32,
    )[:1]
    shift = logsum[group : group + 1, :]
    total[...] = jnp.zeros_like(total)

    def step(i, carry):
        at = pl.ds(pl.multiple_of(i * size, size), size)
        key, value = k[at, cols], v[at, cols]
        half = bias[at, :].astype(F32)
        s = dot_nt(key, stacked_q[...]) + jnp.concatenate([half, half], axis=1)
        p = jnp.exp(s - shift)
        ds = (p * (dot_nt(value, stacked_g[...]) - inner)).astype(BF16)
        v[at, cols] = dot_nn(p.astype(BF16), stacked_g[...]).astype(BF16)
        k[at, cols] = dot_nn(ds, stacked_q[...]).astype(BF16)
        total[...] += dot_tn(key, ds)
        return carry

    count = keys // size
    if count == 1:
        step(0, 0)
        between()
    else:
        for start in range(0, count, 2):
            lax.fori_loop(start, min(start + 2, count), step, 0)
            between()
    grad_q[:, cols] = (unstack_heads(total[...], rows) * HEAD_DIM**-0.5).astype(BF16)


DOWN_UNITS = (1, 3, 0, 2)
WIDE = {1: (8, 9), 3: (10, 11)}


class Scattering:
    def __init__(self, at, i, o, s, n, last, wide, over_y):
        self.at, self.o, self.s, self.n, self.last = at, o, s, n, last
        self.wide, self.over_y = wide, over_y
        self.begun, self.done1, self.step = 0, 0, 0
        self.fresh, self.queue2, self.queue3, self.finished, self.odd = [], [], [], [], False
        self.sent, self.source, self.since = {}, {}, 0.0
        z, y, x, c = at
        self.to_x, self.to_y, self.to_c = device(z, y, 1 - x, c), device(z, 1 - y, x, c), device(z, y, x, 1 - c)

    def copy(self, src, dst, u, k, dev):
        return pltpu.make_async_remote_copy(
            src_ref=src,
            dst_ref=dst,
            send_sem=self.s.send.at[u, k],
            recv_sem=self.s.recv.at[u, k],
            device_id=dev,
            device_id_type=MESH,
        )

    def go(self, u, k, copy):
        copy.start()
        self.sent[u, k] = copy

    def left(self, u, k):
        copy = self.sent.pop((u, k), None)
        if copy is not None:
            copy.wait_send()

    def buffer(self, main, last, u, slots=16):
        return last if u == self.last else main.at[u % slots]

    def total(self, u):
        if u in self.wide:
            m = list(self.wide).index(u)
            return self.s.big.at[m * 512 : m * 512 + 512].reshape(4, 2, 2, 32, 1024)
        return self.buffer(self.s.sum, self.s.nsum, u, 4)

    def xr(self, u):
        return self.buffer(self.s.xy, self.s.nxy, u).at[0 : self.cut(u)]

    def yr(self, u):
        return self.buffer(self.s.xy, self.s.nxy, u).at[self.cut(u) : 4]

    def cc(self, u):
        return self.buffer(self.s.cc, self.s.ncc, u)

    def from_core(self, u):
        src = self.source[u].at[:, :, :, 1 - self.at[3]]
        return self.copy(src, self.buffer(self.s.core, self.s.ncore, u, 4), u, 0, self.to_c)

    def cut(self, u):
        return 0 if u in self.over_y else 2

    def first_x(self, u):
        n = self.cut(u)
        return self.copy(self.total(u).at[0:n, :, 1 - self.at[2]], self.xr(u), u, 1, self.to_x)

    def first_y(self, u):
        n = self.cut(u)
        return self.copy(self.total(u).at[n:4, 1 - self.at[1]], self.yr(u), u, 2, self.to_y)

    def second_y(self, u):
        n = self.cut(u)
        return self.copy(self.xr(u).at[:, 1 - self.at[1]], self.cc(u).at[0:n], u, 3, self.to_y)

    def second_x(self, u):
        n = self.cut(u)
        return self.copy(self.yr(u).at[:, 1 - self.at[2]], self.cc(u).at[n:4], u, 4, self.to_x)

    def final(self, u):
        return self.o.nfin if u == self.last else self.o.fin.at[u]

    def across(self, u, k):
        z, y, x, c = self.at
        to = lax.rem(z + k, 4)
        return self.copy(self.cc(u).at[to], self.final(u).at[k - 1], u, 4 + k, device(to, y, x, c))

    def keep(self, u):
        return pltpu.make_async_copy(self.cc(u).at[self.at[0]], self.final(u).at[3], self.s.keep.at[u])

    def load(self, u):
        return pltpu.make_async_copy(self.source[u].at[:, :, :, self.at[3]], self.total(u), self.s.own.at[u])

    def begin(self, u, source, in_hbm):
        while self.done1 < u - 3:
            self.pump()
        self.begun += 1
        self.source[u] = source
        if 4 <= u < self.last:
            pl.semaphore_wait(self.s.free, 1)
        if in_hbm:
            self.load(u).start()
        self.go(u, 0, self.from_core(u))

    def work(self, us):
        self.since += us
        if self.since >= PACE_BACKWARD:
            self.pump()

    def pump(self):
        self.since = 0.0
        self.odd = not self.odd
        if self.odd:
            self.queue2 += self.fresh
            self.fresh = []
            if self.done1 < self.begun:
                new = self.done1
                self.done1 += 1
                self.stage1(new)
                if new not in self.wide:
                    self.fresh = [new]
            return
        seconds, self.queue2 = self.queue2[:1], self.queue2[1:]
        thirds, self.queue3 = self.queue3[:1], self.queue3[1:] + seconds
        for u in seconds:
            self.stage2(u)
        for u in thirds:
            self.stage3(u)
        for u, steps in self.wide.items():
            for stage in range(2):
                if steps[stage] == self.step:
                    (self.wide_plane, self.wide_last)[stage](u)
                    self.finished.append((u, stage))
        self.step += 1

    def stage1(self, u):
        z, y, x, c = self.at
        total, got, source = self.total(u), self.buffer(self.s.core, self.s.ncore, u, 4), self.source[u]
        in_hbm = u < 4
        if in_hbm:
            self.load(u).wait()
        else:
            self.left(u - 4, 1)
            self.left(u - 4, 2)
        self.from_core(u).wait_recv()

        def add(j, carry):
            at = (j // 4, lax.rem(j // 2, 2), lax.rem(j, 2))
            own = total[at] if in_hbm else source[at + (c,)]
            total[at] = own + got[at]
            return carry

        lax.fori_loop(0, 16, add, 0)
        if u + 4 < self.last:
            pl.semaphore_signal(self.s.free, inc=1, device_id=self.to_c, device_id_type=MESH)
        if u in self.wide:
            for k in (1, 2, 3):
                self.go(u, 4 + k, self.wide_across(u, k))
            return
        if self.cut(u):
            self.go(u, 1, self.first_x(u))
        self.go(u, 2, self.first_y(u))

    def stage2(self, u):
        z, y, x, c = self.at
        total, yr, n = self.total(u), self.yr(u), self.cut(u)
        if n:
            xr = self.xr(u)
            self.first_x(u).wait_recv()

            def add_x(j, carry):
                a, b = j // 2, lax.rem(j, 2)
                xr[a, b] = xr[a, b] + total[a, b, x]
                return carry

            lax.fori_loop(0, 2 * n, add_x, 0)
            self.go(u, 3, self.second_y(u))
        self.first_y(u).wait_recv()

        def add_y(j, carry):
            a, b = j // 2, lax.rem(j, 2)
            yr[a, b] = yr[a, b] + total[n + a, y, b]
            return carry

        lax.fori_loop(0, 8 - 2 * n, add_y, 0)
        self.go(u, 4, self.second_x(u))

    def stage3(self, u):
        z, y, x, c = self.at
        yr, cc, n = self.yr(u), self.cc(u), self.cut(u)
        if n:
            xr = self.xr(u)
            self.second_y(u).wait_recv()
            for a in range(n):
                cc[a] = cc[a] + xr[a, y]
        self.second_x(u).wait_recv()
        for a in range(4 - n):
            cc[n + a] = cc[n + a] + yr[a, x]
        for k in (1, 2, 3):
            self.go(u, 4 + k, self.across(u, k))
        self.keep(u).start()

    def wide_got(self, u, k):
        m = list(self.wide).index(u)
        at = 1024 + (m * 3 + k - 1) * 128
        return self.s.big.at[at : at + 128].reshape(2, 2, 32, 1024)

    def wide_across(self, u, k):
        z, y, x, c = self.at
        to = lax.rem(z + k, 4)
        return self.copy(self.total(u).at[to], self.wide_got(u, k), u, 4 + k, device(to, y, x, c))

    def wide_copy(self, u, which):
        z, y, x, c = self.at
        m, total = list(self.wide).index(u), self.total(u)
        xw, yw, top, low = self.s.xw.at[m], self.s.yw.at[m], pl.ds(0, 16), pl.ds(16, 16)
        if which == 0:
            return self.copy(total.at[z, :, 1 - x, top], xw, u, 1, self.to_x)
        if which == 1:
            return self.copy(total.at[z, 1 - y, :, low], yw, u, 2, self.to_y)
        if which == 2:
            return self.copy(xw.at[1 - y], self.o.fin.at[u, 1, top], u, 3, self.to_y)
        if which == 3:
            return self.copy(yw.at[1 - x], self.o.fin.at[u, 1, low], u, 4, self.to_x)
        if which == 4:
            return pltpu.make_async_copy(xw.at[y], self.o.fin.at[u, 0, top], self.s.keep.at[u])
        return pltpu.make_async_copy(yw.at[x], self.o.fin.at[u, 0, low], self.s.own.at[4 + m])

    def wide_plane(self, u):
        z, y, x, c = self.at
        total, got = self.total(u), [self.wide_got(u, k) for k in (1, 2, 3)]
        for k in (1, 2, 3):
            self.wide_across(u, k).wait_recv()

        def add(j, carry):
            a, b = j // 2, lax.rem(j, 2)
            own = total[z, a, b].astype(F32) + got[0][a, b].astype(F32)
            more = got[1][a, b].astype(F32) + got[2][a, b].astype(F32)
            total[z, a, b] = (own + more).astype(BF16)
            return carry

        lax.fori_loop(0, 4, add, 0)
        self.go(u, 1, self.wide_copy(u, 0))
        self.go(u, 2, self.wide_copy(u, 1))

    def wide_last(self, u):
        z, y, x, c = self.at
        m, total = list(self.wide).index(u), self.total(u)
        xw, yw = self.s.xw.at[m], self.s.yw.at[m]
        self.wide_copy(u, 0).wait_recv()
        for a in range(2):
            xw[a] = xw[a] + total[z, a, x, 0:16]
        self.go(u, 3, self.wide_copy(u, 2))
        self.wide_copy(u, 4).start()
        self.wide_copy(u, 1).wait_recv()
        for a in range(2):
            yw[a] = yw[a] + total[z, y, a, 16:32]
        self.go(u, 4, self.wide_copy(u, 3))
        self.wide_copy(u, 5).start()

    def settle(self):
        while len(self.finished) < 2 * len(self.wide):
            self.pump()
        for u in self.wide:
            for k in (1, 2, 5, 6, 7):
                self.left(u, k)

    def finish(self):
        while self.fresh or self.queue2 or self.queue3 or self.done1 < self.begun:
            self.pump()
        for u in range(self.n):
            if u in self.wide:
                for which in (2, 3):
                    self.wide_copy(u, which).wait_recv()
                for which in (4, 5):
                    self.wide_copy(u, which).wait()
                continue
            for k in (1, 2, 3):
                self.across(u, k).wait_recv()
            self.keep(u).wait()
        for key in list(self.sent):
            self.left(*key)


def backward_kernel(i, o, s):
    at = place()
    z, y, x, c = at
    seq = x * 2 + c
    comm = Scattering(at, i, o, s, 17, 16, WIDE, ())
    greet(*at)
    six = (4, 2, 2, 2, 32, 1024)
    for u in range(4):
        comm.begin(u, i.ddown.at[DOWN_UNITS.index(u)], True)
    waits = {}

    def fetch(src, dst, slot):
        copy = pltpu.make_async_copy(src, dst, s.fetch.at[slot])
        copy.start()
        waits[slot] = copy

    def have(*slots):
        for slot in slots:
            waits.pop(slot).wait()

    def block(full, k):
        return full.at[:, :, :, :, :, pl.ds(k * 1024, 1024)]

    stream = []
    for j in range(4):
        stream += [i.down.at[:, :, :, :, j], block(i.up, j)]
    stream += [block(i.cout, 0), block(i.cqkv, 1), block(i.cqkv, 2), block(i.cqkv, 0), block(i.sout, 0)]
    stream += [block(i.sqkv, k) for k in range(3)]

    def weight(n):
        dst = s.w.at[n % 3]
        return pltpu.make_async_copy(stream[n], dst.reshape(*six), s.load.at[n % 3])

    def loaded(n):
        weight(n).wait()
        return s.w.at[n % 3]

    def used(n):
        if n + 3 < len(stream):
            weight(n + 3).start()

    for n in range(3):
        weight(n).start()
    fetch(i.cot, s.cot, 3)
    fetch(i.slope, s.k, 11)
    fetch(i.nf, s.up, 5)
    fetch(i.gb, s.gb, 0)
    fetch(i.r2, s.r, 1)
    fetch(i.cctx, s.ctx, 4)
    fetch(i.ck, s.ck, 6)
    fetch(i.cv, s.cv, 7)
    fetch(i.clse, s.clse, 8)
    fetch(i.nc, s.nc, 9)
    fetch(i.text, s.text, 10)
    fetch(i.v, s.v, 12)
    fetch(i.lse, s.lse, 13)
    fetch(i.normed, s.normed, 14)
    comm.pump()
    comm.pump()
    set_masks(i, seq, s.bias, s.cbias, 2)
    s.ng[...] = jnp.zeros_like(s.ng)
    have(0)

    def norm_back(values, upstream, k, put):
        gain = s.gb[k : k + 1, :]
        center = values - jnp.mean(values, axis=-1, keepdims=True)
        scale = lax.rsqrt(jnp.mean(center * center, axis=-1, keepdims=True) + 1e-05)
        hat = center * scale
        s.ng[k : k + 1, :] += jnp.sum(upstream * hat, axis=0, keepdims=True)
        s.ng[3 + k : 4 + k, :] += jnp.sum(upstream, axis=0, keepdims=True)
        if put is not None:
            h = upstream * gain
            put((h - jnp.mean(h, axis=-1, keepdims=True) - hat * jnp.mean(h * hat, axis=-1, keepdims=True)) * scale)

    def gradient(u, left, right, cost=2.2):
        while u > 5 and comm.done1 < u - 1:
            comm.pump()
        comm.left(u - 2, 0)
        dw = s.dw.at[u % 2]

        def one(n, cut):
            dw[:, cut] = dot_tn(left(), right(cut)).astype(BF16)

        tiles(4, 256)(one)
        comm.begin(u, dw.reshape(*six), False)
        comm.work(cost)

    gr, branch, g = s.gr, s.branch, s.g
    for j in range(4):
        w, w_up = loaded(2 * j), None
        if j == 0:
            have(3, 5, 11)

        def back(n, rows):
            slope = s.k[j * 320 : (j + 1) * 320, rows].astype(F32)
            branch[:, rows] = (dot_nt(s.cot[...], w[rows, :]) * slope).astype(BF16)

        tiles(4, 256)(back)
        used(2 * j)
        comm.work(1.6)
        gradient(4 + j, lambda: s.up[...], lambda cut: branch[:, cut])
        w_up = loaded(2 * j + 1)

        def onward(n, rows):
            more = dot_nt(branch[...], w_up[rows, :])
            g[:, rows] = more if j == 0 else g[:, rows] + more

        tiles(4, 256)(onward)
        used(2 * j + 1)
        comm.work(1.6)
    fetch(i.k, s.k, 11)
    fetch(i.cq, s.q, 5)
    have(1)

    def back_two(b, rows):
        def put(grad):
            total = s.cot[rows, :].astype(F32) + grad
            gr[rows, :] = total
            branch[rows, :] = total.astype(BF16)

        norm_back(s.r[rows, :], g[rows, :], 2, put)

    tiles(5, 64)(back_two)
    fetch(i.r1, s.r, 1)
    comm.work(1.0)

    def through(dst, src, w):
        def one(n, rows):
            value = dot_nt(src[...], w[rows, :])
            dst[:, rows] = value.astype(dst.dtype)

        tiles(4, 256)(one)

    through(s.up, branch, loaded(8))
    used(8)
    comm.work(1.6)
    have(4)
    gradient(8, lambda: s.ctx[...], lambda cut: branch[:, cut])
    have(5, 6, 7, 8)
    for group in range(4):
        attend_back_group(
            group,
            s.q,
            s.ck,
            s.cv,
            s.up,
            s.ctx,
            s.cbias,
            s.clse,
            s.stacked_q,
            s.stacked_g,
            s.total,
            s.dq,
            lambda: comm.work(1.8),
        )
    fetch(i.q, s.q, 5)
    fetch(i.ctx, s.ctx, 4)
    have(9, 10)
    gradient(9, lambda: s.nc[...], lambda cut: s.dq[:, cut])
    w_key, w_value = loaded(9), loaded(10)

    def text_part(n, rows):
        value = dot_nt(s.ck[...], w_key[rows, :]) + dot_nt(s.cv[...], w_value[rows, :])
        s.tpart[:, :, :, rows] = value.astype(BF16).reshape(2, 2, 16, 256)

    tiles(4, 256)(text_part)
    used(9)
    used(10)
    text_core = comm.copy(s.tpart.at[:, 1 - c], s.tcore, 17, 0, comm.to_c)
    comm.go(17, 0, text_core)
    comm.work(0.8)
    through(g, s.dq, loaded(11))
    used(11)
    comm.work(1.6)
    have(1)

    def back_one(b, rows):
        def put(grad):
            total = gr[rows, :] + grad
            gr[rows, :] = total
            branch[rows, :] = total.astype(BF16)

        norm_back(s.r[rows, :], g[rows, :], 1, put)

    tiles(5, 64)(back_one)
    comm.work(1.0)
    save_gr = pltpu.make_async_copy(gr, o.gr, s.fetch.at[16])
    save_gr.start()
    gradient(10, lambda: s.text[...], lambda cut: s.ck[:, cut])
    through(s.up, branch, loaded(12))
    used(12)
    comm.work(1.6)
    text_core.wait_recv()
    s.tsum[...] = s.tpart[:, c] + s.tcore[...]
    text_x = comm.copy(s.tsum.at[1 - x], o.tmine.at[1], 17, 1, comm.to_x)
    comm.go(17, 1, text_x)
    text_keep = pltpu.make_async_copy(s.tsum.at[x], o.tmine.at[0], s.keep.at[17])
    text_keep.start()
    have(4, 5, 11, 12, 13)
    todo = [
        lambda: gradient(11, lambda: s.text[...], lambda cut: s.cv[:, cut]),
        lambda: gradient(12, lambda: s.ctx[...], lambda cut: branch[:, cut]),
    ]
    for group in range(4):
        attend_back_group(
            group,
            s.q,
            s.k,
            s.v,
            s.up,
            s.ctx,
            s.bias,
            s.lse,
            s.stacked_q,
            s.stacked_g,
            s.total,
            s.dq,
            lambda: comm.work(2.6),
        )
        if group < len(todo):
            todo[group]()
    have(14)
    mine = pl.ds(pl.multiple_of(seq * 320, 64), 320)
    wq, wk, wv = loaded(13), loaded(14), loaded(15)
    comm.settle()
    fpart = s.big.at[0:1280].reshape(2, 2, 320, 1024)

    def frames_part(b, rows):
        block = pltpu.make_async_copy(i.frames.at[b // 2, b % 2], s.cot, s.fetch.at[15])
        block.start()

        def one(n, cut):
            g[:, cut] = dot_nt(s.k[rows, :], wk[cut, :]) + dot_nt(s.v[rows, :], wv[cut, :])

        tiles(4, 256)(one)

        @pl.when(b == seq)
        def _():
            def two(n, cut):
                g[:, cut] = g[:, cut] + dot_nt(s.dq[...], wq[cut, :])

            tiles(4, 256)(two)

        block.wait()

        def three(r, part):
            norm_back(s.cot[part, :].astype(F32), g[part, :], 0, None)
            fpart[b // 2, b % 2, part, :] = g[part, :].astype(BF16)

        tiles(5, 64)(three)

    gradient(13, lambda: s.normed[mine, :], lambda cut: s.dq[:, cut])
    for part_of in range(4):
        frames_part(part_of, pl.ds(part_of * 320, 320))
        comm.work(3.8)
    frames_core = comm.copy(fpart.at[:, 1 - c], s.fcore, 17, 2, comm.to_c)
    comm.go(17, 2, frames_core)
    gradient(14, lambda: s.normed[...], lambda cut: s.k[:, cut], 4.0)
    frames_core.wait_recv()

    def frames_sum(b, carry):
        rows = pl.ds(pl.multiple_of(lax.rem(b, 5) * 64, 64), 64)
        s.fcore[b // 5, rows] = s.fcore[b // 5, rows] + fpart[b // 5, c, rows]
        return carry

    lax.fori_loop(0, 10, frames_sum, 0)
    frames_x = comm.copy(s.fcore.at[1 - x], o.fmine.at[1], 17, 3, comm.to_x)
    comm.go(17, 3, frames_x)
    frames_keep = pltpu.make_async_copy(s.fcore.at[x], o.fmine.at[0], s.keep.at[18])
    frames_keep.start()
    gradient(15, lambda: s.normed[...], lambda cut: s.v[:, cut], 4.0)
    flat = jnp.concatenate([s.ng[...], jnp.zeros((120, 1024), F32)], axis=0).T
    s.nown[...] = flat.reshape(4, 2, 2, 2, 32, 128)
    comm.begin(16, s.nown, False)
    comm.finish()
    text_x.wait_recv()
    frames_x.wait_recv()
    text_keep.wait()
    frames_keep.wait()
    save_gr.wait()


def run_backward_kernel(args):
    S, V, D_SEM = jax.ShapeDtypeStruct, pltpu.VMEM, pltpu.SemaphoreType.DMA
    rows, block = (320, 1024), (32, 1024)
    shapes = dict(
        fin=S((16, 4) + block, BF16), nfin=S((4, 32, 128), F32), fmine=S((2,) + rows, BF16), tmine=S((2, 16, 1024), BF16), gr=S(rows, F32)
    )
    scratch = dict(
        send=D_SEM((18, 8)), recv=D_SEM((18, 8)), own=D_SEM((6,)), keep=D_SEM((19,)), fetch=D_SEM((17,)), load=D_SEM((3,)),
        free=pltpu.SemaphoreType.REGULAR,
        sum=V((4, 4, 2, 2) + block, BF16), core=V((4, 4, 2, 2) + block, BF16), xy=V((16, 4, 2) + block, BF16), cc=V((16, 4) + block, BF16), xw=V((2, 2, 16, 1024), BF16), yw=V((2, 2, 16, 1024), BF16),
        big=V((1792, 1024), BF16),
        nsum=V((4, 2, 2, 32, 128), F32), ncore=V((4, 2, 2, 32, 128), F32), nxy=V((4, 2, 32, 128), F32),
        ncc=V((4, 32, 128), F32), nown=V((4, 2, 2, 2, 32, 128), F32),
        gb=V((8, 1024), F32), r=V(rows, F32), g=V(rows, F32), cot=V(rows, BF16), ctx=V(rows, BF16), q=V(rows, BF16),
        ck=V((64, 1024), BF16), cv=V((64, 1024), BF16), clse=V((4, 1280), F32), nc=V(rows, BF16), text=V((64, 1024), BF16),
        k=V((1280, 1024), BF16), v=V((1280, 1024), BF16), lse=V((4, 1280), F32), normed=V((1280, 1024), BF16), w=V((3, 1024, 1024), BF16),
        bias=V((1280, 640), BF16), cbias=V((64, 640), BF16), ng=V((8, 1024), F32), gr=V(rows, F32), branch=V(rows, BF16),
        up=V(rows, BF16), dq=V(rows, BF16), stacked_q=V((1280, 256), BF16), stacked_g=V((1280, 256), BF16),
        total=V((256, 1280), F32), dw=V((2, 1024, 1024), BF16), tpart=V((2, 2, 16, 1024), BF16), tcore=V((2, 16, 1024), BF16),
        tsum=V((2, 16, 1024), BF16), fcore=V((2,) + rows, BF16),
    )
    apart = dict(seg=pltpu.VMEM, text_len=pltpu.SMEM)
    return pallas(backward_kernel, args, shapes, scratch, apart, dict(collective_id=1))


def finish_kernel(i, o, s):
    coming = []

    def fetch(src, dst):
        copy = pltpu.make_async_copy(src, dst, s.fetch.at[len(coming)])
        copy.start()
        coming.append(copy)
        return copy

    fetch(i.out, s.out)
    fetch(i.frames, s.frames)
    fetch(i.gr, s.gr)
    fetch(i.fmine, s.fmine)
    parts = [fetch(i.fin.at[u, 0 : 2 if u in WIDE else 4], s.fin.at[u, 0 : 2 if u in WIDE else 4]) for u in range(16)]
    going = []

    def put(src, dst):
        copy = pltpu.make_async_copy(src, dst, s.put.at[len(going)])
        copy.start()
        going.append(copy)

    coming[0].wait()
    put(s.out, o.out)
    for copy in coming[1:4]:
        copy.wait()
    gain = i.gb[0:1, :]

    def rows_of(b, rows):
        values = s.frames[rows, :].astype(F32)
        center = values - jnp.mean(values, axis=-1, keepdims=True)
        scale = lax.rsqrt(jnp.mean(center * center, axis=-1, keepdims=True) + 1e-05)
        hat = center * scale
        h = (s.fmine[0, rows, :].astype(F32) + s.fmine[1, rows, :].astype(F32)) * gain
        back = (h - jnp.mean(h, axis=-1, keepdims=True) - hat * jnp.mean(h * hat, axis=-1, keepdims=True)) * scale
        s.frames[rows, :] = (s.gr[rows, :] + back).astype(BF16)

    tiles(5, 64)(rows_of)
    put(s.frames, o.frames)

    def total(u):
        parts[u].wait()
        terms = [s.fin[u, k].astype(F32) for k in range(2 if u in WIDE else 4)]
        return sum(terms[1:], terms[0])

    for k in range(4):
        s.down[k * 32 : (k + 1) * 32, :] = total(DOWN_UNITS[k])
    put(s.down, o.down)
    for j in range(4):
        s.upraw[:, j * 1024 : (j + 1) * 1024] = total(4 + j)

    def put_up(b, block):
        s.up[:, b * 128 : b * 128 + 128] = block

    shuffle_columns(lambda b: s.upraw[:, b * 128 : b * 128 + 128], put_up, True)
    put(s.up, o.up)
    for src, dst, first, count in (
        (s.cout, o.cout, 8, 1),
        (s.cqkv, o.cqkv, 9, 3),
        (s.sout, o.sout, 12, 1),
        (s.sqkv, o.sqkv, 13, 3),
    ):
        for k in range(count):
            src[:, k * 1024 : (k + 1) * 1024] = total(first + k)
        put(src, dst)
    n = ((i.nfin[0] + i.nfin[1]) + (i.nfin[2] + i.nfin[3])).T
    s.gain[...] = n[:3]
    s.shift[...] = n[3:6]
    s.text[...] = (i.tmine[0].astype(F32) + i.tmine[1].astype(F32)).astype(BF16)
    put(s.gain, o.gain)
    put(s.shift, o.shift)
    put(s.text, o.text)
    for copy in going:
        copy.wait()


def run_finish_kernel(args):
    S, V, D_SEM = jax.ShapeDtypeStruct, pltpu.VMEM, pltpu.SemaphoreType.DMA
    rows = (320, 1024)
    shapes = dict(
        out=S(rows, BF16), frames=S(rows, BF16), text=S((16, 1024), BF16), gain=S((3, 32), F32), shift=S((3, 32), F32),
        sqkv=S((32, 3072), F32), sout=S((32, 1024), F32), cqkv=S((32, 3072), F32), cout=S((32, 1024), F32), up=S((32, 4096), F32),
        down=S((128, 1024), F32),
    )
    scratch = {n: V(v.shape, v.dtype) for n, v in shapes.items()}
    scratch.update(
        fin=V((16, 4, 32, 1024), BF16), fmine=V((2,) + rows, BF16), gr=V(rows, F32), upraw=V((32, 4096), F32), fetch=D_SEM((20,)),
        put=D_SEM((11,)),
    )
    apart = dict(nfin=pltpu.VMEM, tmine=pltpu.VMEM, gb=pltpu.VMEM)
    return pallas(finish_kernel, args, shapes, scratch, apart, dict())


def fetch_all(norm_gain, norm_bias, self_qkv, self_out, cross_qkv, cross_out, ffn_up, ffn_down):
    first = (
        lax.all_gather(norm_gain, ("dp", "seq"), axis=0, tiled=True),
        lax.all_gather(norm_bias, ("dp", "seq"), axis=0, tiled=True),
        lax.all_gather(self_qkv, ("dp", "seq"), axis=0, tiled=True),
        lax.all_gather(self_out, ("dp", "seq"), axis=0, tiled=True),
    )
    second = (
        lax.all_gather(cross_qkv, ("dp", "seq"), axis=0, tiled=True),
        lax.all_gather(cross_out, ("dp", "seq"), axis=0, tiled=True),
    )
    third = (
        lax.all_gather(ffn_up, ("dp", "seq"), axis=0, tiled=True),
        lax.all_gather(ffn_down, ("dp", "seq"), axis=0, tiled=True),
    )
    return tuple(first) + tuple(second) + tuple(third)


def run_forward(frames, local_seg, frame_seg, text_seg, text_states, offset, weights):
    norm_gain, norm_bias, self_qkv, self_out, cross_qkv, cross_out, ffn_up, ffn_down = weights
    gains = norm_gain.astype(jnp.float32)
    biases = norm_bias.astype(jnp.float32)
    inputs = frames.astype(jnp.float32)
    normed_self = layer_norm(inputs, gains[:, 0], biases[:, 0]).astype(jnp.bfloat16)
    queries = jnp.dot(normed_self, self_qkv[:, :D], preferred_element_type=jnp.float32).astype(
        jnp.bfloat16
    )
    pair_weights = self_qkv[:, D:].reshape(D, 2, D)
    key_value = jnp.einsum(
        "rcd,dje->jrce", normed_self, pair_weights, preferred_element_type=jnp.float32
    ).astype(jnp.bfloat16)
    gathered = lax.all_gather(key_value, "seq", axis=2, tiled=True)
    self_context, self_logsum = lax.map(
        lambda record: attend(
            record[0], record[1], record[2], self_allowed(record[3], record[4], offset)
        ),
        (queries, gathered[0], gathered[1], local_seg, frame_seg),
    )
    self_context = self_context.astype(jnp.bfloat16)
    resid_one = inputs + jnp.dot(self_context, self_out, preferred_element_type=jnp.float32)
    normed_cross = layer_norm(resid_one, gains[:, 1], biases[:, 1]).astype(jnp.bfloat16)
    cross_queries = jnp.dot(
        normed_cross, cross_qkv[:, :D], preferred_element_type=jnp.float32
    ).astype(jnp.bfloat16)
    text_weights = cross_qkv[:, D:].reshape(D, 2, D)
    text_pair = jnp.einsum(
        "rtd,dje->jrte", text_states, text_weights, preferred_element_type=jnp.float32
    ).astype(jnp.bfloat16)
    cross_context, cross_logsum = lax.map(
        lambda record: attend(
            record[0], record[1], record[2], record[3][:, None] == record[4][None, :]
        ),
        (cross_queries, text_pair[0], text_pair[1], local_seg, text_seg),
    )
    cross_context = cross_context.astype(jnp.bfloat16)
    resid_two = resid_one + jnp.dot(cross_context, cross_out, preferred_element_type=jnp.float32)
    normed_ffn = layer_norm(resid_two, gains[:, 2], biases[:, 2]).astype(jnp.bfloat16)
    hidden_pre = jnp.dot(normed_ffn, ffn_up, preferred_element_type=jnp.float32)
    activated = exact_gelu(hidden_pre).astype(jnp.bfloat16)
    outcome = resid_two + jnp.dot(activated, ffn_down, preferred_element_type=jnp.float32)
    saved = (
        inputs,
        normed_self,
        queries,
        gathered,
        self_context,
        self_logsum,
        resid_one,
        normed_cross,
        cross_queries,
        text_pair,
        cross_context,
        cross_logsum,
        resid_two,
        normed_ffn,
        hidden_pre,
        activated,
    )
    return (outcome, saved)


def generic_body(
    frames,
    frame_seg,
    text_states,
    text_len,
    norm_gain,
    norm_bias,
    self_qkv,
    self_out,
    cross_qkv,
    cross_out,
    ffn_up,
    ffn_down,
    cotangent,
):
    width = frames.shape[1]
    offset = lax.axis_index("seq") * width
    local_seg = lax.dynamic_slice_in_dim(frame_seg, offset, width, 1)
    text_seg = text_segments(text_len)
    shards = (norm_gain, norm_bias, self_qkv, self_out, cross_qkv, cross_out, ffn_up, ffn_down)
    weights = fetch_all(*shards)
    outcome, saved = run_forward(
        frames, local_seg, frame_seg, text_seg, text_states, offset, weights
    )
    frames_out = outcome.astype(jnp.bfloat16)
    (
        inputs,
        normed_self,
        queries,
        gathered,
        self_context,
        self_logsum,
        resid_one,
        normed_cross,
        cross_queries,
        text_pair,
        cross_context,
        cross_logsum,
        resid_two,
        normed_ffn,
        hidden_pre,
        activated,
    ) = saved
    gain_full, bias_full, self_full, self_proj, cross_full, cross_proj, up_full, down_full = weights
    gains = gain_full.astype(jnp.float32)
    biases = bias_full.astype(jnp.float32)
    upstream = cotangent.astype(jnp.float32)
    down_grad = jnp.einsum("rcf,rcd->fd", activated, cotangent, preferred_element_type=jnp.float32)
    grad_act = jnp.einsum("rcd,fd->rcf", cotangent, down_full, preferred_element_type=jnp.float32)
    unused_value, gelu_pull = jax.vjp(exact_gelu, hidden_pre)
    grad_pre = gelu_pull(grad_act)[0].astype(jnp.bfloat16)
    up_grad = jnp.einsum("rcd,rcf->df", normed_ffn, grad_pre, preferred_element_type=jnp.float32)
    grad_normed = jnp.einsum("rcf,df->rcd", grad_pre, up_full, preferred_element_type=jnp.float32)
    grad_back, gain_two, bias_two = norm_back(resid_two, gains[:, 2], biases[:, 2], grad_normed)
    grad_resid_two = upstream + grad_back
    ffn_shares = (
        lax.psum_scatter(up_grad, ("dp", "seq"), scatter_dimension=0, tiled=True),
        lax.psum_scatter(down_grad, ("dp", "seq"), scatter_dimension=0, tiled=True),
    )
    branch_two = grad_resid_two.astype(jnp.bfloat16)
    cross_out_grad = jnp.einsum(
        "rcd,rce->de", cross_context, branch_two, preferred_element_type=jnp.float32
    )
    grad_context = jnp.einsum(
        "rce,de->rcd", branch_two, cross_proj, preferred_element_type=jnp.float32
    ).astype(jnp.bfloat16)
    grad_cross_q, grad_cross_k, grad_cross_v = lax.map(
        lambda record: attend_back(
            record[0],
            record[1],
            record[2],
            record[3][:, None] == record[4][None, :],
            record[5],
            record[6],
        ),
        (
            cross_queries,
            text_pair[0],
            text_pair[1],
            local_seg,
            text_seg,
            cross_logsum,
            grad_context,
        ),
    )
    text_joined = jnp.transpose(jnp.concatenate([grad_cross_k, grad_cross_v], axis=2), (1, 0, 2))
    text_summed = lax.psum_scatter(
        text_joined.astype(jnp.bfloat16), "seq", scatter_dimension=0, tiled=True
    ).astype(jnp.float32)
    text_shares = jnp.transpose(text_summed, (1, 0, 2)).astype(jnp.bfloat16)
    share = text_shares.shape[1]
    text_part = lax.dynamic_slice_in_dim(text_states, lax.axis_index("seq") * share, share, 1)
    text_kv_grad = jnp.einsum(
        "rtd,rte->de", text_part, text_shares, preferred_element_type=jnp.float32
    )
    text_grad = jnp.einsum(
        "rte,de->rtd", text_shares, cross_full[:, D:], preferred_element_type=jnp.float32
    ).astype(jnp.bfloat16)
    grad_cross_q = grad_cross_q.astype(jnp.bfloat16)
    cross_q_grad = jnp.einsum(
        "rcd,rce->de", normed_cross, grad_cross_q, preferred_element_type=jnp.float32
    )
    cross_qkv_grad = jnp.concatenate([cross_q_grad, text_kv_grad], axis=1)
    grad_normed = jnp.einsum(
        "rce,de->rcd", grad_cross_q, cross_full[:, :D], preferred_element_type=jnp.float32
    )
    grad_back, gain_one, bias_one = norm_back(resid_one, gains[:, 1], biases[:, 1], grad_normed)
    grad_resid_one = grad_resid_two + grad_back
    cross_shares = (
        lax.psum_scatter(cross_qkv_grad, ("dp", "seq"), scatter_dimension=0, tiled=True),
        lax.psum_scatter(cross_out_grad, ("dp", "seq"), scatter_dimension=0, tiled=True),
    )
    branch_one = grad_resid_one.astype(jnp.bfloat16)
    self_out_grad = jnp.einsum(
        "rcd,rce->de", self_context, branch_one, preferred_element_type=jnp.float32
    )
    grad_context = jnp.einsum(
        "rce,de->rcd", branch_one, self_proj, preferred_element_type=jnp.float32
    ).astype(jnp.bfloat16)
    grad_self_q, grad_self_k, grad_self_v = lax.map(
        lambda record: attend_back(
            record[0],
            record[1],
            record[2],
            self_allowed(record[3], record[4], offset),
            record[5],
            record[6],
        ),
        (queries, gathered[0], gathered[1], local_seg, frame_seg, self_logsum, grad_context),
    )
    joined = jnp.concatenate([grad_self_k, grad_self_v], axis=2)
    summed = lax.psum_scatter(
        jnp.transpose(joined, (1, 0, 2)).astype(jnp.bfloat16),
        "seq",
        scatter_dimension=0,
        tiled=True,
    ).astype(jnp.float32)
    key_shares = jnp.transpose(summed, (1, 0, 2)).astype(jnp.bfloat16)
    all_grads = jnp.concatenate([grad_self_q.astype(jnp.bfloat16), key_shares], axis=2)
    self_qkv_grad = jnp.einsum(
        "rcd,rce->de", normed_self, all_grads, preferred_element_type=jnp.float32
    )
    grad_normed = jnp.einsum(
        "rce,de->rcd", all_grads, self_full, preferred_element_type=jnp.float32
    )
    grad_back, gain_zero, bias_zero = norm_back(inputs, gains[:, 0], biases[:, 0], grad_normed)
    frames_grad = (grad_resid_one + grad_back).astype(jnp.bfloat16)
    gain_grad = jnp.stack([gain_zero, gain_one, gain_two], axis=1)
    bias_grad = jnp.stack([bias_zero, bias_one, bias_two], axis=1)
    self_shares = (
        lax.psum_scatter(gain_grad, ("dp", "seq"), scatter_dimension=0, tiled=True),
        lax.psum_scatter(bias_grad, ("dp", "seq"), scatter_dimension=0, tiled=True),
        lax.psum_scatter(self_qkv_grad, ("dp", "seq"), scatter_dimension=0, tiled=True),
        lax.psum_scatter(self_out_grad, ("dp", "seq"), scatter_dimension=0, tiled=True),
    )
    return (
        frames_out,
        frames_grad,
        text_grad,
        self_shares[0],
        self_shares[1],
        self_shares[2],
        self_shares[3],
        cross_shares[0],
        cross_shares[1],
        ffn_shares[0],
        ffn_shares[1],
    )


def fast_body(
    frames,
    frame_seg,
    text_states,
    text_len,
    norm_gain,
    norm_bias,
    self_qkv,
    self_out,
    cross_qkv,
    cross_out,
    ffn_up,
    ffn_down,
    cotangent,
):
    args = dict(
        frames=frames[0],
        gain=norm_gain.T,
        shift=norm_bias.T,
        sqkv=self_qkv,
        sout=self_out,
        cqkv=cross_qkv,
        cout=cross_out,
        up=ffn_up,
        down=ffn_down.reshape(4, 32, D),
        cot=cotangent[0],
        text=text_states[0],
        seg=frame_seg,
        text_len=text_len,
    )
    f = types.SimpleNamespace(**run_forward_kernel(args))
    a = types.SimpleNamespace(**args)
    units = (4, 4, 2, 2, 2, 32, D)
    back = run_backward_kernel(
        dict(
            ddown=f.ddown.reshape(units),
            slope=f.slope,
            nf=f.nf,
            down=f.down,
            up=f.up,
            cot=a.cot,
            gb=f.gb,
            r2=f.r2,
            r1=f.r1,
            cctx=f.cctx,
            ctx=f.ctx,
            cq=f.cq,
            ck=f.ck,
            cv=f.cv,
            clse=f.clse,
            nc=f.nc,
            text=a.text,
            q=f.q,
            k=f.k,
            v=f.v,
            lse=f.lse,
            normed=f.normed,
            frames=f.frames,
            cout=f.cout,
            cqkv=f.cqkv,
            sout=f.sout,
            sqkv=f.sqkv,
            seg=a.seg,
            text_len=a.text_len,
        )
    )
    b = types.SimpleNamespace(**back)
    outs = run_finish_kernel(
        dict(
            fin=b.fin, nfin=b.nfin, fmine=b.fmine, tmine=b.tmine, gr=b.gr, frames=a.frames, gb=f.gb, out=f.out
        )
    )
    n = types.SimpleNamespace(**outs)
    return (
        n.out[None],
        n.frames[None],
        n.text[None],
        n.gain.T,
        n.shift.T,
        n.sqkv,
        n.sout,
        n.cqkv,
        n.cout,
        n.up,
        n.down,
    )


def solution(mesh):
    return jax.shard_map(
        fast_body if dict(mesh.shape) == {"dp": 8, "seq": 4} else generic_body,
        mesh=mesh,
        in_specs=(
            P("dp", "seq", None),
            P("dp", None),
            P("dp", None, None),
            P("dp", None),
            P(("dp", "seq"), None),
            P(("dp", "seq"), None),
            P(("dp", "seq"), None),
            P(("dp", "seq"), None),
            P(("dp", "seq"), None),
            P(("dp", "seq"), None),
            P(("dp", "seq"), None),
            P(("dp", "seq"), None),
            P("dp", "seq", None),
        ),
        out_specs=(
            P("dp", "seq", None),
            P("dp", "seq", None),
            P("dp", "seq", None),
            P(("dp", "seq"), None),
            P(("dp", "seq"), None),
            P(("dp", "seq"), None),
            P(("dp", "seq"), None),
            P(("dp", "seq"), None),
            P(("dp", "seq"), None),
            P(("dp", "seq"), None),
            P(("dp", "seq"), None),
        ),
        check_vma=False,
    )
```

```python
import types

import jax
import jax.numpy as jnp
from jax import lax
from jax.experimental import pallas as pl
from jax.experimental.pallas import tpu as pltpu
from jax.sharding import PartitionSpec as P

D = 1024
HEADS = 16
HEAD_DIM = 64
TEXT_LEN = 64


def layer_norm(values, gain, bias):
    center = values - jnp.mean(values, axis=-1, keepdims=True)
    spread = jnp.mean(center * center, axis=-1, keepdims=True)
    return center * lax.rsqrt(spread + 1e-05) * gain + bias


def norm_back(values, gain, bias, upstream):
    unused_value, pullback = jax.vjp(layer_norm, values, gain, bias)
    return pullback(upstream)


def exact_gelu(values):
    return jax.nn.gelu(values, approximate=False)


def split_heads(values):
    return values.reshape(values.shape[0], HEADS, HEAD_DIM)


def text_segments(text_len):
    bounds = jnp.cumsum(text_len, axis=1)
    positions = jnp.arange(TEXT_LEN, dtype=jnp.int32)
    return jnp.sum((positions[None, :, None] >= bounds[:, None, :]).astype(jnp.int32), axis=2)


def self_allowed(local_seg, full_seg, offset):
    row_pos = offset + jnp.arange(local_seg.shape[0], dtype=jnp.int32)
    col_pos = jnp.arange(full_seg.shape[0], dtype=jnp.int32)
    return (row_pos[:, None] >= col_pos[None, :]) & (local_seg[:, None] == full_seg[None, :])


def masked_scores(queries, keys_in, allowed):
    factor = HEAD_DIM ** (-0.5)
    scores = (
        jnp.einsum(
            "qhe,khe->hqk",
            split_heads(queries),
            split_heads(keys_in),
            preferred_element_type=jnp.float32,
        )
        * factor
    )
    return jnp.where(allowed[None], scores, -1e30)


def attend(queries, keys_in, values, allowed):
    scores = masked_scores(queries, keys_in, allowed)
    highest = jnp.max(scores, axis=-1, keepdims=True)
    powered = jnp.exp(scores - highest)
    totals = jnp.sum(powered, axis=-1, keepdims=True)
    weights = (powered / totals).astype(jnp.bfloat16)
    context = jnp.einsum(
        "hqk,khe->qhe", weights, split_heads(values), preferred_element_type=jnp.float32
    )
    return (context.reshape(queries.shape[0], -1), highest + jnp.log(totals))


def attend_back(queries, keys_in, values, allowed, logsum, upstream):
    factor = HEAD_DIM ** (-0.5)
    probs_full = jnp.exp(masked_scores(queries, keys_in, allowed) - logsum)
    grad_heads = split_heads(upstream)
    grad_probs = jnp.einsum(
        "qhe,khe->hqk", grad_heads, split_heads(values), preferred_element_type=jnp.float32
    )
    row_inner = jnp.sum(probs_full * grad_probs, axis=-1, keepdims=True)
    grad_scores = (probs_full * (grad_probs - row_inner)).astype(jnp.bfloat16)
    grad_queries = (
        jnp.einsum(
            "hqk,khe->qhe", grad_scores, split_heads(keys_in), preferred_element_type=jnp.float32
        )
        * factor
    )
    grad_keys = (
        jnp.einsum(
            "hqk,qhe->khe", grad_scores, split_heads(queries), preferred_element_type=jnp.float32
        )
        * factor
    )
    grad_values = jnp.einsum(
        "hqk,qhe->khe",
        probs_full.astype(jnp.bfloat16),
        grad_heads,
        preferred_element_type=jnp.float32,
    )
    return (
        grad_queries.reshape(queries.shape[0], -1),
        grad_keys.reshape(keys_in.shape[0], -1),
        grad_values.reshape(values.shape[0], -1),
    )


F32, BF16 = jnp.float32, jnp.bfloat16
MESH = pl.DeviceIdType.MESH
VMEM_BYTES = 64 * 2**20
BLOCK = 256
LEAD = 6
PACE_FORWARD = 3.5
PACE_BACKWARD = 3.1


def place():
    dp, seq = lax.axis_index("dp"), lax.axis_index("seq")
    return dp // 2, lax.rem(dp, 2), seq // 2, lax.rem(seq, 2)


def device(z, y, x, c):
    return (z * 2 + y, x * 2 + c)


def greet(z, y, x, c):
    barrier = pltpu.get_barrier_semaphore()
    others = [device(lax.rem(z + k, 4), y, x, c) for k in (1, 2, 3)]
    others += [device(z, 1 - y, x, c), device(z, y, 1 - x, c), device(z, y, x, 1 - c)]
    for other in others:
        pl.semaphore_signal(barrier, inc=1, device_id=other, device_id_type=MESH)
    pl.semaphore_wait(barrier, len(others))


def dot_nn(a, b):
    return jnp.dot(a, b, preferred_element_type=F32)


def dot_nt(a, b):
    return lax.dot_general(a, b, (((1,), (1,)), ((), ())), preferred_element_type=F32)


def dot_tn(a, b):
    return lax.dot_general(a, b, (((0,), (0,)), ((), ())), preferred_element_type=F32)


def tiles(count, size):
    def run(step):
        def one(i, carry):
            step(i, pl.ds(pl.multiple_of(i * size, size), size))
            return carry

        lax.fori_loop(0, count, one, 0)

    return run


def normalize(block, gain, bias):
    center = block - jnp.mean(block, axis=-1, keepdims=True)
    spread = jnp.mean(center * center, axis=-1, keepdims=True)
    return center * lax.rsqrt(spread + 1e-05) * gain + bias


def stack_heads(dst, src, group, factor):
    rows = src.shape[0]
    part = src[:, group * 256 : group * 256 + 256]
    if factor != 1.0:
        part = part * jnp.asarray(factor, part.dtype)
    head = lax.broadcasted_iota(jnp.int32, part.shape, 1) // HEAD_DIM
    for h in range(4):
        dst[h * rows : (h + 1) * rows, :] = jnp.where(head == h, part, jnp.zeros_like(part))


def unstack_heads(wide, rows):
    parts = [wide[h * 64 : (h + 1) * 64, h * rows : (h + 1) * rows] for h in range(4)]
    return jnp.concatenate(parts, axis=0).T


def attend_group(group, q, k, v, bias, stacked, scores, total, context, logsum, between):
    rows, keys = q.shape[0], k.shape[0]
    size = min(BLOCK, keys)
    cols = slice(group * 256, group * 256 + 256)
    stack_heads(stacked, q, group, HEAD_DIM**-0.5)

    def score(i, highest):
        at = pl.ds(pl.multiple_of(i * size, size), size)
        s = dot_nt(k[at, cols], stacked[...]) + bias[at, :].astype(F32)
        scores[at, :] = s
        return jnp.maximum(highest, jnp.max(s, axis=0, keepdims=True))

    highest = lax.fori_loop(0, keys // size, score, jnp.full((1, 4 * rows), -3e38, F32))
    between()
    total[...] = jnp.zeros_like(total)

    def weigh(i, summed):
        at = pl.ds(pl.multiple_of(i * size, size), size)
        p = jnp.exp(scores[at, :] - highest)
        total[...] += dot_tn(v[at, cols], p.astype(BF16))
        return summed + jnp.sum(p, axis=0, keepdims=True)

    summed = lax.fori_loop(0, keys // size, weigh, jnp.zeros((1, 4 * rows), F32))
    logsum[group : group + 1, :] = highest + jnp.log(summed)
    context[:, cols] = unstack_heads(total[...] / summed, rows).astype(BF16)


class Gathering:
    def __init__(self, at, units, over_y, wide, send_sem, recv_sem, own_sem):
        self.at, self.units, self.n = at, units, len(units)
        self.over_y, self.wide = over_y, wide
        self.order = [u for u in range(self.n) if u not in wide]
        self.send_sem, self.recv_sem, self.own_sem = send_sem, recv_sem, own_sem
        self.sent, self.step, self.spreads, self.since = [], 0, False, 0.0
        z, y, x, c = at
        self.to_x, self.to_y, self.to_c = device(z, y, 1 - x, c), device(z, 1 - y, x, c), device(z, y, x, 1 - c)

    def copy(self, src, dst, u, k, dev):
        return pltpu.make_async_remote_copy(
            src_ref=src,
            dst_ref=dst,
            send_sem=self.send_sem.at[u, k],
            recv_sem=self.recv_sem.at[u, k],
            device_id=dev,
            device_id_type=MESH,
        )

    def go(self, copy):
        copy.start()
        self.sent.append(copy)

    def same(self, u, k, dev, *spot):
        view = self.units[u][1](*spot)
        return self.copy(view, view, u, k, dev)

    def across(self, u, k):
        z, y, x, c = self.at
        src, dst = self.units[u][0], self.units[u][1](z, y, x, c)
        return self.copy(src, dst, u, k - 1, device(lax.rem(z + k, 4), y, x, c))

    def own(self, u):
        return pltpu.make_async_copy(self.units[u][0], self.units[u][1](*self.at), self.own_sem.at[u])

    def first(self, p):
        if p < len(self.order):
            u = self.order[p]
            self.own(u).start()
            for k in (1, 2, 3):
                self.go(self.across(u, k))

    def cuts(self, u):
        if u in self.over_y:
            return pl.ds(0, 4), None
        return pl.ds(0, 2), pl.ds(2, 2)

    def spread(self, p):
        z, y, x, c = self.at
        every, u, same, go = pl.ds(0, 4), self.order[p], self.same, self.go
        for k in (1, 2, 3):
            self.across(u, k).wait_recv()
        self.own(u).wait()
        go(same(u, 3, self.to_x, every, y, x, c))
        go(same(u, 4, self.to_y, every, y, x, c))
        go(same(u, 5, self.to_c, every, y, x, c))
        self.first(p + LEAD)

    def work(self, us):
        self.since += us
        if self.since >= PACE_FORWARD:
            self.pump()

    def pump(self):
        z, y, x, c = self.at
        every = pl.ds(0, 4)
        self.since = 0.0
        t, n, same, go = self.step, len(self.order), self.same, self.go
        if t >= n + 2:
            return
        if not self.spreads:
            self.spreads = True
            if t < n:
                self.spread(t)
            return
        self.spreads = False
        self.step += 1
        if 0 <= t - 1 < n:
            u = self.order[t - 1]
            low, high = self.cuts(u)
            same(u, 3, self.to_x, every, y, 1 - x, c).wait_recv()
            go(same(u, 6, self.to_y, low, y, 1 - x, c))
            go(same(u, 7, self.to_c, every, y, 1 - x, c))
            same(u, 4, self.to_y, every, 1 - y, x, c).wait_recv()
            if high is not None:
                go(same(u, 8, self.to_x, high, 1 - y, x, c))
            go(same(u, 9, self.to_c, every, 1 - y, x, c))
        if 0 <= t - 2 < n:
            u = self.order[t - 2]
            low, high = self.cuts(u)
            same(u, 6, self.to_y, low, 1 - y, 1 - x, c).wait_recv()
            go(same(u, 10, self.to_c, low, 1 - y, 1 - x, c))
            if high is not None:
                same(u, 8, self.to_x, high, 1 - y, 1 - x, c).wait_recv()
                go(same(u, 11, self.to_c, high, 1 - y, 1 - x, c))
        for u, steps in self.wide.items():
            for stage in range(4):
                if steps[stage] == t:
                    self.widen(u, stage)

    def half(self, u, k, dev, h, *spot):
        view = self.units[u][1](*spot).at[h * 16 : h * 16 + 16]
        return self.copy(view, view, u, k, dev)

    def plane(self, u, k, dev, zz, cc):
        return self.same(u, k, dev, zz, pl.ds(0, 2), pl.ds(0, 2), cc)

    def widen(self, u, stage):
        z, y, x, c = self.at
        go = self.go
        if stage == 0:
            self.own(u).start()
            src, dst = self.units[u][0], self.units[u][1](z, y, x, c)
            go(self.copy(src, dst, u, 0, self.to_x))
            go(self.copy(src, dst, u, 1, self.to_y))
        elif stage == 1:
            self.same(u, 0, self.to_x, z, y, 1 - x, c).wait_recv()
            go(self.half(u, 2, self.to_y, 0, z, y, 1 - x, c))
            self.same(u, 1, self.to_y, z, 1 - y, x, c).wait_recv()
            go(self.half(u, 3, self.to_x, 1, z, 1 - y, x, c))
        elif stage == 2:
            self.own(u).wait()
            self.half(u, 2, self.to_y, 0, z, 1 - y, 1 - x, c).wait_recv()
            self.half(u, 3, self.to_x, 1, z, 1 - y, 1 - x, c).wait_recv()
            for k in (1, 2, 3):
                go(self.plane(u, 3 + k, device(lax.rem(z + k, 4), y, x, c), z, c))
            go(self.plane(u, 7, self.to_c, z, c))
        else:
            for k in (1, 2, 3):
                other = lax.rem(z + 4 - k, 4)
                self.plane(u, 3 + k, self.to_c, other, c).wait_recv()
                go(self.plane(u, 7 + k, self.to_c, other, c))

    def need(self, u):
        z, y, x, c = self.at
        every = pl.ds(0, 4)
        if u in self.wide:
            while self.step <= self.wide[u][3]:
                self.pump()
            self.plane(u, 7, self.to_c, z, 1 - c).wait_recv()
            for k in (1, 2, 3):
                self.plane(u, 7 + k, self.to_c, lax.rem(z + 4 - k, 4), 1 - c).wait_recv()
            return
        while self.step <= self.order.index(u) + 2:
            self.pump()
        low, high = self.cuts(u)
        self.same(u, 5, self.to_c, every, y, x, 1 - c).wait_recv()
        self.same(u, 7, self.to_c, every, y, 1 - x, 1 - c).wait_recv()
        self.same(u, 9, self.to_c, every, 1 - y, x, 1 - c).wait_recv()
        self.same(u, 10, self.to_c, low, 1 - y, 1 - x, 1 - c).wait_recv()
        if high is not None:
            self.same(u, 11, self.to_c, high, 1 - y, 1 - x, 1 - c).wait_recv()


def same_clip(seg, seq):
    own = seg[:, 0:320]
    for k in range(1, 4):
        own = jnp.where(seq == k, seg[:, k * 320 : (k + 1) * 320], own)

    def down(b):
        part = seg[:, pl.ds(pl.multiple_of(b * 128, 128), 128)]
        return jnp.broadcast_to(part, (128, 128)).T[:, :1]

    return own, down


def set_masks(i, seq, bias, text_bias, copies):
    own, down = same_clip(i.seg, seq)

    def mask(b, rows):
        key = lax.broadcasted_iota(jnp.int32, (128, 320), 0) + b * 128
        query = lax.broadcasted_iota(jnp.int32, (128, 320), 1) + seq * 320
        seen = (key <= query) & (down(b) == own)
        block = jnp.where(seen, 0.0, -1e30).astype(F32)
        bias[rows, :] = jnp.concatenate([block] * copies, axis=1).astype(BF16)

    tiles(10, 128)(mask)
    slot = lax.broadcasted_iota(jnp.int32, (TEXT_LEN, 320), 0)
    clip = jnp.zeros((TEXT_LEN, 320), jnp.int32)
    bound = jnp.int32(0)
    for k in range(4):
        bound = bound + i.text_len[0, k]
        clip = clip + (slot >= bound).astype(jnp.int32)
    block = jnp.where(clip == own, 0.0, -1e30).astype(F32)
    text_bias[...] = jnp.concatenate([block] * copies, axis=1).astype(BF16)


def shuffle_columns(part, put, back):
    lane = lax.broadcasted_iota(jnp.int32, (32, 128), 1) // 32
    for b in range(32):
        block = jnp.zeros((32, 128), F32)
        for q in range(4):
            source, quarter = (q * 8 + b // 4, b % 4) if back else (b % 8 * 4 + q, b // 8)
            chunk = part(source)
            moved = pltpu.roll(chunk, (q - quarter) % 4 * 32, 1) if q != quarter else chunk
            block = jnp.where(lane == q, moved, block)
        put(b, block)


def forward_kernel(i, o, s):
    at = place()
    z, y, x, c = at
    seq = x * 2 + c
    units = [(s.nin, lambda zz, yy, xx, cc: o.norms.at[zz, yy, xx, cc])]

    def columns(shard, full, count):
        for k in range(count):
            cut = pl.ds(k * 1024, 1024)
            units.append(
                (shard.at[:, cut], lambda zz, yy, xx, cc, cut=cut: full.at[zz, yy, xx, cc, :, cut])
            )

    columns(i.sqkv, o.sqkv, 3)
    columns(i.sout, o.sout, 1)
    columns(i.cqkv, o.cqkv, 3)
    columns(i.cout, o.cout, 1)
    columns(s.upin, o.up, 4)
    for k in range(4):
        units.append(
            (i.down.at[k], lambda zz, yy, xx, cc, k=k: o.down.at[zz, yy, xx, cc, k])
        )
        wide = {12: (0, 1, 2, 10), 16: (6, 7, 8, 16)}
    comm = Gathering(at, units, (1, 2), wide, s.send, s.recv, s.own)
    up_copy = pltpu.make_async_copy(i.up, s.upraw, s.own.at[comm.n + 3])
    up_copy.start()
    s.flat[...] = jnp.zeros_like(s.flat)
    s.flat[0:3, 0:32] = i.gain[...].astype(F32)
    s.flat[3:6, 0:32] = i.shift[...].astype(F32)
    s.nin[...] = s.flat[...].T[:32].astype(BF16)
    greet(*at)
    fr = s.frames
    f = comm.n

    def share(k, dev, xx, cc):
        view = fr.at[xx, cc]
        return comm.copy(view, view, f, k, dev)

    own_frames = pltpu.make_async_copy(i.frames, fr.at[x, c], s.own.at[f])
    own_frames.start()
    cot_copy = pltpu.make_async_copy(i.cot, s.cot, s.own.at[f + 1])
    cot_copy.start()
    text_copy = pltpu.make_async_copy(i.text, s.text, s.own.at[f + 2])
    text_copy.start()
    for u in range(LEAD):
        comm.first(u)
    own_frames.wait()
    comm.go(share(0, comm.to_x, x, c))
    comm.go(share(1, comm.to_c, x, c))
    up_copy.wait()

    def put_up(b, block):
        s.upin[:, b * 128 : b * 128 + 128] = block.astype(BF16)

    shuffle_columns(lambda b: s.upraw[:, b * 128 : b * 128 + 128].astype(F32), put_up, False)

    saves = []

    def save(src, dst):
        copy = pltpu.make_async_copy(src, dst, s.save.at[len(saves)])
        copy.start()
        saves.append(copy)

    set_masks(i, seq, s.bias, s.cbias, 4)

    def weight(u, where):
        comm.need(u)
        src = units[u][1](pl.ds(0, 4), pl.ds(0, 2), pl.ds(0, 2), pl.ds(0, 2))
        dst = s.w.at[where]
        copy = pltpu.make_async_copy(src, dst.reshape(4, 2, 2, 2, 32, 1024), s.load.at[u])
        copy.start()
        copy.wait()
        return dst

    def norm(dst, src_block, k, count):
        gain, bias = s.gb[k : k + 1, :], s.gb[3 + k : 4 + k, :]

        def one(b, rows):
            dst[rows, :] = normalize(src_block(b, rows), gain, bias).astype(BF16)

        tiles(count, 64)(one)

    share(0, comm.to_x, 1 - x, c).wait_recv()
    comm.go(share(2, comm.to_c, 1 - x, c))
    comm.need(0)
    copy = pltpu.make_async_copy(o.norms, s.norms.reshape(4, 2, 2, 2, 32, 128), s.load.at[0])
    copy.start()
    copy.wait()
    s.gb[...] = s.norms[...].astype(F32).T[:8]
    share(1, comm.to_c, x, 1 - c).wait_recv()
    share(2, comm.to_c, 1 - x, 1 - c).wait_recv()
    normed = s.normed

    def frame_block(b, rows):
        return fr[b // 10, lax.rem(b // 5, 2), pl.ds(pl.multiple_of(lax.rem(b, 5) * 64, 64), 64), :].astype(F32)

    norm(normed, frame_block, 0, 20)
    comm.work(4.0)
    save(s.gb, o.gb)
    save(fr, o.frames)
    save(normed, o.normed)

    mine = pl.ds(pl.multiple_of(seq * 320, 64), 320)

    def project(dst, src, w, rows):
        def one(n, cut):
            dst[:, cut] = dot_nn(src[rows, :], w[:, cut]).astype(BF16)

        tiles(4, 256)(one)

    def project_all(dst, w):
        def one(b, rows):
            def two(n, cut):
                dst[rows, cut] = dot_nn(normed[rows, :], w[:, cut]).astype(BF16)

            tiles(4, 256)(two)

        for b in range(4):
            one(b, pl.ds(b * 320, 320))
            comm.work(1.8)

    every_row = pl.ds(0, 320)
    q, k, v = s.q, s.k, s.v
    project(q, normed, weight(1, 0), mine)
    project_all(k, weight(2, 1))
    project_all(v, weight(3, 2))
    save(q, o.q)
    save(k, o.k)
    save(v, o.v)
    for g in range(4):
        attend_group(
            g, q, k, v, s.bias, s.stacked, s.scores, s.total, s.ctx, s.lse, lambda: comm.work(2.0)
        )
        comm.work(2.0)
    save(s.ctx, o.ctx)
    save(s.lse, o.lse)

    def add_project(dst, base, src, w):
        def one(n, cut):
            dst[:, cut] = base(cut) + dot_nn(src[...], w[:, cut])

        tiles(4, 256)(one)

    add_project(s.r1, lambda cut: fr[x, c, :, cut].astype(F32), s.ctx, weight(4, 0))
    save(s.r1, o.r1)
    norm(s.nc, lambda b, rows: s.r1[rows, :], 1, 5)
    save(s.nc, o.nc)
    project(s.cq, s.nc, weight(5, 1), every_row)
    save(s.cq, o.cq)
    text_copy.wait()
    text_rows = pl.ds(0, TEXT_LEN)
    project(s.ck, s.text, weight(6, 2), text_rows)
    project(s.cv, s.text, weight(7, 0), text_rows)
    save(s.ck, o.ck)
    save(s.cv, o.cv)
    for g in range(4):
        attend_group(
            g,
            s.cq,
            s.ck,
            s.cv,
            s.cbias,
            s.stacked,
            s.scores,
            s.total,
            s.cctx,
            s.clse,
            lambda: None,
        )
        comm.work(0.6)
    save(s.cctx, o.cctx)
    save(s.clse, o.clse)
    add_project(s.r2, lambda cut: s.r1[:, cut], s.cctx, weight(8, 1))
    save(s.r2, o.r2)
    norm(s.nf, lambda b, rows: s.r2[rows, :], 2, 5)
    cot_copy.wait()
    act, slope, nf, cot = s.act, s.slope, s.nf, s.cot
    save(nf, o.nf)
    grads = []

    def gradient(dst, left, right):
        m = len(grads)
        if m >= 2:
            grads[m - 2].wait()
        stage = s.stage.at[m % 2]

        def one(n, cut):
            stage[:, cut] = dot_tn(left(), right(cut)).astype(BF16)

        tiles(4, 256)(one)
        copy = pltpu.make_async_copy(stage, dst, s.grad.at[m])
        copy.start()
        grads.append(copy)

    for j in range(4):
        w = weight(9 + j, j % 3)

        def one(n, cut):
            h = dot_nn(nf[...], w[:, cut])
            below = 0.5 * (1.0 + lax.erf(h * 0.7071067811865476))
            act[j, :, cut] = (h * below).astype(BF16)
            slope[j * 320 : (j + 1) * 320, cut] = (
                below + h * jnp.exp(-0.5 * h * h) * 0.3989422804014327
            ).astype(BF16)

        one(0, pl.ds(0, 512))
        comm.work(1.75)
        one(1, pl.ds(512, 512))
        comm.work(1.75)
        gradient(o.ddown.at[j], lambda: act[j], lambda cut: cot[:, cut])
        comm.work(2.0)
    save(slope, o.slope)
    for copy in saves:
        copy.wait()
    for j in range(4):
        w = weight(13 + j, j % 3)

        def onward(n, cut):
            s.r2[:, cut] = s.r2[:, cut] + dot_nn(act[j], w[:, cut])

        tiles(4, 256)(onward)
    s.out[...] = s.r2[...].astype(BF16)
    copy = pltpu.make_async_copy(s.out, o.out, s.save.at[len(saves)])
    copy.start()
    copy.wait()
    for copy in grads[-2:]:
        copy.wait()
    for copy in comm.sent:
        copy.wait_send()


def pallas(kernel, args, shapes, scratch, apart, params):
    def named(*refs):
        a, b = len(args), len(args) + len(shapes)
        kernel(
            types.SimpleNamespace(**dict(zip(args, refs[:a]))),
            types.SimpleNamespace(**dict(zip(shapes, refs[a:b]))),
            types.SimpleNamespace(**dict(zip(scratch, refs[b:]))),
        )

    outs = pl.pallas_call(
        named,
        out_shape=list(shapes.values()),
        in_specs=[pl.BlockSpec(memory_space=apart.get(n, pl.ANY)) for n in args],
        out_specs=[pl.BlockSpec(memory_space=pl.ANY)] * len(shapes),
        scratch_shapes=list(scratch.values()),
        compiler_params=pltpu.CompilerParams(
            has_side_effects=True, vmem_limit_bytes=VMEM_BYTES, **params
        ),
    )(*args.values())
    return dict(zip(shapes, outs))


def run_forward_kernel(args):
    S, V, D_SEM = jax.ShapeDtypeStruct, pltpu.VMEM, pltpu.SemaphoreType.DMA
    a = types.SimpleNamespace(**args)
    rows = (320, 1024)
    scratch = dict(
        send=D_SEM((18, 12)), recv=D_SEM((18, 12)), own=D_SEM((21,)), save=D_SEM((24,)), load=D_SEM((17,)), grad=D_SEM((4,)),
        frames=V((2, 2, 320, 1024), BF16), cot=V(rows, BF16), text=V((64, 1024), BF16), norms=V((1024, 128), BF16), gb=V((8, 1024), F32),
        bias=V((1280, 1280), BF16), cbias=V((64, 1280), BF16), w=V((3, 1024, 1024), BF16), normed=V((1280, 1024), BF16),
        q=V(rows, BF16), k=V((1280, 1024), BF16), v=V((1280, 1024), BF16), stacked=V((1280, 256), BF16), scores=V((1280, 1280), F32),
        total=V((256, 1280), F32), ctx=V(rows, BF16), lse=V((4, 1280), F32), r1=V(rows, F32), nc=V(rows, BF16), cq=V(rows, BF16),
        ck=V((64, 1024), BF16), cv=V((64, 1024), BF16), cctx=V(rows, BF16), clse=V((4, 1280), F32), r2=V(rows, F32), nf=V(rows, BF16),
        act=V((4, 320, 1024), BF16), slope=V((1280, 1024), BF16), out=V(rows, BF16), nin=V((32, 128), BF16), flat=V((128, 128), F32),
        upraw=V((32, 4096), BF16), upin=V((32, 4096), BF16), stage=V((2, 1024, 1024), BF16),
    )
    m = types.SimpleNamespace(**scratch)
    shapes = dict(norms=m.nin, sqkv=a.sqkv, sout=a.sout, cqkv=a.cqkv, cout=a.cout, up=a.up, down=a.down)
    shapes = {n: S((4, 2, 2, 2) + v.shape, BF16) for n, v in shapes.items()}
    saved = dict(
        gb=m.gb, frames=m.frames, normed=m.normed, q=m.q, k=m.k, v=m.v, ctx=m.ctx, lse=m.lse, r1=m.r1, nc=m.nc, cq=m.cq, ck=m.ck,
        cv=m.cv, cctx=m.cctx, clse=m.clse, r2=m.r2, out=m.out, nf=m.nf, slope=m.slope,
    )
    shapes.update({n: S(v.shape, v.dtype) for n, v in saved.items()})
    shapes.update(ddown=S((4, 1024, 1024), BF16))
    apart = dict(seg=pltpu.VMEM, gain=pltpu.VMEM, shift=pltpu.VMEM, text_len=pltpu.SMEM)
    return pallas(forward_kernel, args, shapes, scratch, apart, dict(collective_id=0))


def attend_back_group(group, q, k, v, up, context, bias, logsum, stacked_q, stacked_g, total, grad_q, between):
    rows, keys = q.shape[0], k.shape[0]
    size = min(BLOCK, keys)
    cols = slice(group * 256, group * 256 + 256)
    stack_heads(stacked_q, q, group, HEAD_DIM**-0.5)
    stack_heads(stacked_g, up, group, 1.0)
    four = jnp.concatenate([context[:, cols].astype(F32)] * 4, axis=0)
    inner = lax.dot_general(
        jnp.ones((8, 256), F32),
        stacked_g[...].astype(F32) * four,
        (((1,), (1,)), ((), ())),
        precision=lax.Precision.HIGHEST,
        preferred_element_type=F32,
    )[:1]
    shift = logsum[group : group + 1, :]
    total[...] = jnp.zeros_like(total)

    def step(i, carry):
        at = pl.ds(pl.multiple_of(i * size, size), size)
        key, value = k[at, cols], v[at, cols]
        half = bias[at, :].astype(F32)
        s = dot_nt(key, stacked_q[...]) + jnp.concatenate([half, half], axis=1)
        p = jnp.exp(s - shift)
        ds = (p * (dot_nt(value, stacked_g[...]) - inner)).astype(BF16)
        v[at, cols] = dot_nn(p.astype(BF16), stacked_g[...]).astype(BF16)
        k[at, cols] = dot_nn(ds, stacked_q[...]).astype(BF16)
        total[...] += dot_tn(key, ds)
        return carry

    count = keys // size
    if count == 1:
        step(0, 0)
        between()
    else:
        for start in range(0, count, 2):
            lax.fori_loop(start, min(start + 2, count), step, 0)
            between()
    grad_q[:, cols] = (unstack_heads(total[...], rows) * HEAD_DIM**-0.5).astype(BF16)


DOWN_UNITS = (1, 3, 0, 2)
WIDE = {1: (8, 9), 3: (10, 11)}


class Scattering:
    def __init__(self, at, i, o, s, n, last, wide, over_y):
        self.at, self.o, self.s, self.n, self.last = at, o, s, n, last
        self.wide, self.over_y = wide, over_y
        self.begun, self.done1, self.step = 0, 0, 0
        self.fresh, self.queue2, self.queue3, self.finished, self.odd = [], [], [], [], False
        self.sent, self.source, self.since = {}, {}, 0.0
        z, y, x, c = at
        self.to_x, self.to_y, self.to_c = device(z, y, 1 - x, c), device(z, 1 - y, x, c), device(z, y, x, 1 - c)

    def copy(self, src, dst, u, k, dev):
        return pltpu.make_async_remote_copy(
            src_ref=src,
            dst_ref=dst,
            send_sem=self.s.send.at[u, k],
            recv_sem=self.s.recv.at[u, k],
            device_id=dev,
            device_id_type=MESH,
        )

    def go(self, u, k, copy):
        copy.start()
        self.sent[u, k] = copy

    def left(self, u, k):
        copy = self.sent.pop((u, k), None)
        if copy is not None:
            copy.wait_send()

    def buffer(self, main, last, u, slots=16):
        return last if u == self.last else main.at[u % slots]

    def total(self, u):
        if u in self.wide:
            m = list(self.wide).index(u)
            return self.s.big.at[m * 512 : m * 512 + 512].reshape(4, 2, 2, 32, 1024)
        return self.buffer(self.s.sum, self.s.nsum, u, 4)

    def xr(self, u):
        return self.buffer(self.s.xy, self.s.nxy, u).at[0 : self.cut(u)]

    def yr(self, u):
        return self.buffer(self.s.xy, self.s.nxy, u).at[self.cut(u) : 4]

    def cc(self, u):
        return self.buffer(self.s.cc, self.s.ncc, u)

    def from_core(self, u):
        src = self.source[u].at[:, :, :, 1 - self.at[3]]
        return self.copy(src, self.buffer(self.s.core, self.s.ncore, u, 4), u, 0, self.to_c)

    def cut(self, u):
        return 1 if u in self.over_y else 2

    def first_x(self, u):
        n = self.cut(u)
        return self.copy(self.total(u).at[0:n, :, 1 - self.at[2]], self.xr(u), u, 1, self.to_x)

    def first_y(self, u):
        n = self.cut(u)
        return self.copy(self.total(u).at[n:4, 1 - self.at[1]], self.yr(u), u, 2, self.to_y)

    def second_y(self, u):
        n = self.cut(u)
        return self.copy(self.xr(u).at[:, 1 - self.at[1]], self.cc(u).at[0:n], u, 3, self.to_y)

    def second_x(self, u):
        n = self.cut(u)
        return self.copy(self.yr(u).at[:, 1 - self.at[2]], self.cc(u).at[n:4], u, 4, self.to_x)

    def final(self, u):
        return self.o.nfin if u == self.last else self.o.fin.at[u]

    def across(self, u, k):
        z, y, x, c = self.at
        to = lax.rem(z + k, 4)
        return self.copy(self.cc(u).at[to], self.final(u).at[k - 1], u, 4 + k, device(to, y, x, c))

    def keep(self, u):
        return pltpu.make_async_copy(self.cc(u).at[self.at[0]], self.final(u).at[3], self.s.keep.at[u])

    def load(self, u):
        return pltpu.make_async_copy(self.source[u].at[:, :, :, self.at[3]], self.total(u), self.s.own.at[u])

    def begin(self, u, source, in_hbm):
        while self.done1 < u - 3:
            self.pump()
        self.begun += 1
        self.source[u] = source
        if 4 <= u < self.last:
            pl.semaphore_wait(self.s.free, 1)
        if in_hbm:
            self.load(u).start()
        self.go(u, 0, self.from_core(u))

    def work(self, us):
        self.since += us
        if self.since >= PACE_BACKWARD:
            self.pump()

    def pump(self):
        self.since = 0.0
        self.odd = not self.odd
        if self.odd:
            self.queue2 += self.fresh
            self.fresh = []
            if self.done1 < self.begun:
                new = self.done1
                self.done1 += 1
                self.stage1(new)
                if new not in self.wide:
                    self.fresh = [new]
            return
        seconds, self.queue2 = self.queue2[:1], self.queue2[1:]
        thirds, self.queue3 = self.queue3[:1], self.queue3[1:] + seconds
        for u in seconds:
            self.stage2(u)
        for u in thirds:
            self.stage3(u)
        for u, steps in self.wide.items():
            for stage in range(2):
                if steps[stage] == self.step:
                    (self.wide_plane, self.wide_last)[stage](u)
                    self.finished.append((u, stage))
        self.step += 1

    def stage1(self, u):
        z, y, x, c = self.at
        total, got, source = self.total(u), self.buffer(self.s.core, self.s.ncore, u, 4), self.source[u]
        in_hbm = u < 4
        if in_hbm:
            self.load(u).wait()
        else:
            self.left(u - 4, 1)
            self.left(u - 4, 2)
        self.from_core(u).wait_recv()

        def add(j, carry):
            at = (j // 4, lax.rem(j // 2, 2), lax.rem(j, 2))
            own = total[at] if in_hbm else source[at + (c,)]
            total[at] = own + got[at]
            return carry

        lax.fori_loop(0, 16, add, 0)
        if u + 4 < self.last:
            pl.semaphore_signal(self.s.free, inc=1, device_id=self.to_c, device_id_type=MESH)
        if u in self.wide:
            for k in (1, 2, 3):
                self.go(u, 4 + k, self.wide_across(u, k))
            return
        if self.cut(u):
            self.go(u, 1, self.first_x(u))
        self.go(u, 2, self.first_y(u))

    def stage2(self, u):
        z, y, x, c = self.at
        total, yr, n = self.total(u), self.yr(u), self.cut(u)
        if n:
            xr = self.xr(u)
            self.first_x(u).wait_recv()

            def add_x(j, carry):
                a, b = j // 2, lax.rem(j, 2)
                xr[a, b] = xr[a, b] + total[a, b, x]
                return carry

            lax.fori_loop(0, 2 * n, add_x, 0)
            self.go(u, 3, self.second_y(u))
        self.first_y(u).wait_recv()

        def add_y(j, carry):
            a, b = j // 2, lax.rem(j, 2)
            yr[a, b] = yr[a, b] + total[n + a, y, b]
            return carry

        lax.fori_loop(0, 8 - 2 * n, add_y, 0)
        self.go(u, 4, self.second_x(u))

    def stage3(self, u):
        z, y, x, c = self.at
        yr, cc, n = self.yr(u), self.cc(u), self.cut(u)
        if n:
            xr = self.xr(u)
            self.second_y(u).wait_recv()
            for a in range(n):
                cc[a] = cc[a] + xr[a, y]
        self.second_x(u).wait_recv()
        for a in range(4 - n):
            cc[n + a] = cc[n + a] + yr[a, x]
        for k in (1, 2, 3):
            self.go(u, 4 + k, self.across(u, k))
        self.keep(u).start()

    def wide_got(self, u, k):
        m = list(self.wide).index(u)
        at = 1024 + (m * 3 + k - 1) * 128
        return self.s.big.at[at : at + 128].reshape(2, 2, 32, 1024)

    def wide_across(self, u, k):
        z, y, x, c = self.at
        to = lax.rem(z + k, 4)
        return self.copy(self.total(u).at[to], self.wide_got(u, k), u, 4 + k, device(to, y, x, c))

    def wide_copy(self, u, which):
        z, y, x, c = self.at
        m, total = list(self.wide).index(u), self.total(u)
        xw, yw, top, low = self.s.xw.at[m], self.s.yw.at[m], pl.ds(0, 16), pl.ds(16, 16)
        if which == 0:
            return self.copy(total.at[z, :, 1 - x, top], xw, u, 1, self.to_x)
        if which == 1:
            return self.copy(total.at[z, 1 - y, :, low], yw, u, 2, self.to_y)
        if which == 2:
            return self.copy(xw.at[1 - y], self.o.fin.at[u, 1, top], u, 3, self.to_y)
        if which == 3:
            return self.copy(yw.at[1 - x], self.o.fin.at[u, 1, low], u, 4, self.to_x)
        if which == 4:
            return pltpu.make_async_copy(xw.at[y], self.o.fin.at[u, 0, top], self.s.keep.at[u])
        return pltpu.make_async_copy(yw.at[x], self.o.fin.at[u, 0, low], self.s.own.at[4 + m])

    def wide_plane(self, u):
        z, y, x, c = self.at
        total, got = self.total(u), [self.wide_got(u, k) for k in (1, 2, 3)]
        for k in (1, 2, 3):
            self.wide_across(u, k).wait_recv()

        def add(j, carry):
            a, b = j // 2, lax.rem(j, 2)
            own = total[z, a, b].astype(F32) + got[0][a, b].astype(F32)
            more = got[1][a, b].astype(F32) + got[2][a, b].astype(F32)
            total[z, a, b] = (own + more).astype(BF16)
            return carry

        lax.fori_loop(0, 4, add, 0)
        self.go(u, 1, self.wide_copy(u, 0))
        self.go(u, 2, self.wide_copy(u, 1))

    def wide_last(self, u):
        z, y, x, c = self.at
        m, total = list(self.wide).index(u), self.total(u)
        xw, yw = self.s.xw.at[m], self.s.yw.at[m]
        self.wide_copy(u, 0).wait_recv()
        for a in range(2):
            xw[a] = xw[a] + total[z, a, x, 0:16]
        self.go(u, 3, self.wide_copy(u, 2))
        self.wide_copy(u, 4).start()
        self.wide_copy(u, 1).wait_recv()
        for a in range(2):
            yw[a] = yw[a] + total[z, y, a, 16:32]
        self.go(u, 4, self.wide_copy(u, 3))
        self.wide_copy(u, 5).start()

    def settle(self):
        while len(self.finished) < 2 * len(self.wide):
            self.pump()
        for u in self.wide:
            for k in (1, 2, 5, 6, 7):
                self.left(u, k)

    def finish(self):
        while self.fresh or self.queue2 or self.queue3 or self.done1 < self.begun:
            self.pump()
        for u in range(self.n):
            if u in self.wide:
                for which in (2, 3):
                    self.wide_copy(u, which).wait_recv()
                for which in (4, 5):
                    self.wide_copy(u, which).wait()
                continue
            for k in (1, 2, 3):
                self.across(u, k).wait_recv()
            self.keep(u).wait()
        for key in list(self.sent):
            self.left(*key)


def backward_kernel(i, o, s):
    at = place()
    z, y, x, c = at
    seq = x * 2 + c
    comm = Scattering(at, i, o, s, 17, 16, WIDE, (14, 15))
    greet(*at)
    six = (4, 2, 2, 2, 32, 1024)
    for u in range(4):
        comm.begin(u, i.ddown.at[DOWN_UNITS.index(u)], True)
    waits = {}

    def fetch(src, dst, slot):
        copy = pltpu.make_async_copy(src, dst, s.fetch.at[slot])
        copy.start()
        waits[slot] = copy

    def have(*slots):
        for slot in slots:
            waits.pop(slot).wait()

    def block(full, k):
        return full.at[:, :, :, :, :, pl.ds(k * 1024, 1024)]

    stream = []
    for j in range(4):
        stream += [i.down.at[:, :, :, :, j], block(i.up, j)]
    stream += [block(i.cout, 0), block(i.cqkv, 1), block(i.cqkv, 2), block(i.cqkv, 0), block(i.sout, 0)]
    stream += [block(i.sqkv, k) for k in range(3)]

    def weight(n):
        dst = s.w.at[n % 3]
        return pltpu.make_async_copy(stream[n], dst.reshape(*six), s.load.at[n % 3])

    def loaded(n):
        weight(n).wait()
        return s.w.at[n % 3]

    def used(n):
        if n + 3 < len(stream):
            weight(n + 3).start()

    for n in range(3):
        weight(n).start()
    fetch(i.cot, s.cot, 3)
    fetch(i.slope, s.k, 11)
    fetch(i.nf, s.up, 5)
    fetch(i.gb, s.gb, 0)
    fetch(i.r2, s.r, 1)
    fetch(i.cctx, s.ctx, 4)
    fetch(i.ck, s.ck, 6)
    fetch(i.cv, s.cv, 7)
    fetch(i.clse, s.clse, 8)
    fetch(i.nc, s.nc, 9)
    fetch(i.text, s.text, 10)
    fetch(i.v, s.v, 12)
    fetch(i.lse, s.lse, 13)
    fetch(i.normed, s.normed, 14)
    comm.pump()
    comm.pump()
    set_masks(i, seq, s.bias, s.cbias, 2)
    s.ng[...] = jnp.zeros_like(s.ng)
    have(0)

    def norm_back(values, upstream, k, put):
        gain = s.gb[k : k + 1, :]
        center = values - jnp.mean(values, axis=-1, keepdims=True)
        scale = lax.rsqrt(jnp.mean(center * center, axis=-1, keepdims=True) + 1e-05)
        hat = center * scale
        s.ng[k : k + 1, :] += jnp.sum(upstream * hat, axis=0, keepdims=True)
        s.ng[3 + k : 4 + k, :] += jnp.sum(upstream, axis=0, keepdims=True)
        if put is not None:
            h = upstream * gain
            put((h - jnp.mean(h, axis=-1, keepdims=True) - hat * jnp.mean(h * hat, axis=-1, keepdims=True)) * scale)

    def gradient(u, left, right, cost=2.2):
        while u > 5 and comm.done1 < u - 1:
            comm.pump()
        comm.left(u - 2, 0)
        dw = s.dw.at[u % 2]

        def one(n, cut):
            dw[:, cut] = dot_tn(left(), right(cut)).astype(BF16)

        tiles(4, 256)(one)
        comm.begin(u, dw.reshape(*six), False)
        comm.work(cost)

    gr, branch, g = s.gr, s.branch, s.g
    for j in range(4):
        w, w_up = loaded(2 * j), None
        if j == 0:
            have(3, 5, 11)

        def back(n, rows):
            slope = s.k[j * 320 : (j + 1) * 320, rows].astype(F32)
            branch[:, rows] = (dot_nt(s.cot[...], w[rows, :]) * slope).astype(BF16)

        tiles(4, 256)(back)
        used(2 * j)
        comm.work(1.6)
        gradient(4 + j, lambda: s.up[...], lambda cut: branch[:, cut])
        w_up = loaded(2 * j + 1)

        def onward(n, rows):
            more = dot_nt(branch[...], w_up[rows, :])
            g[:, rows] = more if j == 0 else g[:, rows] + more

        tiles(4, 256)(onward)
        used(2 * j + 1)
        comm.work(1.6)
    fetch(i.k, s.k, 11)
    fetch(i.cq, s.q, 5)
    have(1)

    def back_two(b, rows):
        def put(grad):
            total = s.cot[rows, :].astype(F32) + grad
            gr[rows, :] = total
            branch[rows, :] = total.astype(BF16)

        norm_back(s.r[rows, :], g[rows, :], 2, put)

    tiles(5, 64)(back_two)
    fetch(i.r1, s.r, 1)
    comm.work(1.0)

    def through(dst, src, w):
        def one(n, rows):
            value = dot_nt(src[...], w[rows, :])
            dst[:, rows] = value.astype(dst.dtype)

        tiles(4, 256)(one)

    through(s.up, branch, loaded(8))
    used(8)
    comm.work(1.6)
    have(4)
    gradient(8, lambda: s.ctx[...], lambda cut: branch[:, cut])
    have(5, 6, 7, 8)
    for group in range(4):
        attend_back_group(
            group,
            s.q,
            s.ck,
            s.cv,
            s.up,
            s.ctx,
            s.cbias,
            s.clse,
            s.stacked_q,
            s.stacked_g,
            s.total,
            s.dq,
            lambda: comm.work(1.8),
        )
    fetch(i.q, s.q, 5)
    fetch(i.ctx, s.ctx, 4)
    have(9, 10)
    gradient(9, lambda: s.nc[...], lambda cut: s.dq[:, cut])
    w_key, w_value = loaded(9), loaded(10)

    def text_part(n, rows):
        value = dot_nt(s.ck[...], w_key[rows, :]) + dot_nt(s.cv[...], w_value[rows, :])
        s.tpart[:, :, :, rows] = value.astype(BF16).reshape(2, 2, 16, 256)

    tiles(4, 256)(text_part)
    used(9)
    used(10)
    text_core = comm.copy(s.tpart.at[:, 1 - c], s.tcore, 17, 0, comm.to_c)
    comm.go(17, 0, text_core)
    comm.work(0.8)
    through(g, s.dq, loaded(11))
    used(11)
    comm.work(1.6)
    have(1)

    def back_one(b, rows):
        def put(grad):
            total = gr[rows, :] + grad
            gr[rows, :] = total
            branch[rows, :] = total.astype(BF16)

        norm_back(s.r[rows, :], g[rows, :], 1, put)

    tiles(5, 64)(back_one)
    comm.work(1.0)
    save_gr = pltpu.make_async_copy(gr, o.gr, s.fetch.at[16])
    save_gr.start()
    gradient(10, lambda: s.text[...], lambda cut: s.ck[:, cut])
    through(s.up, branch, loaded(12))
    used(12)
    comm.work(1.6)
    text_core.wait_recv()
    s.tsum[...] = s.tpart[:, c] + s.tcore[...]
    text_x = comm.copy(s.tsum.at[1 - x], o.tmine.at[1], 17, 1, comm.to_x)
    comm.go(17, 1, text_x)
    text_keep = pltpu.make_async_copy(s.tsum.at[x], o.tmine.at[0], s.keep.at[17])
    text_keep.start()
    have(4, 5, 11, 12, 13)
    todo = [
        lambda: gradient(11, lambda: s.text[...], lambda cut: s.cv[:, cut]),
        lambda: gradient(12, lambda: s.ctx[...], lambda cut: branch[:, cut]),
    ]
    for group in range(4):
        attend_back_group(
            group,
            s.q,
            s.k,
            s.v,
            s.up,
            s.ctx,
            s.bias,
            s.lse,
            s.stacked_q,
            s.stacked_g,
            s.total,
            s.dq,
            lambda: comm.work(2.6),
        )
        if group < len(todo):
            todo[group]()
    have(14)
    mine = pl.ds(pl.multiple_of(seq * 320, 64), 320)
    wq, wk, wv = loaded(13), loaded(14), loaded(15)
    comm.settle()
    fpart = s.big.at[0:1280].reshape(2, 2, 320, 1024)

    def frames_part(b, rows):
        block = pltpu.make_async_copy(i.frames.at[b // 2, b % 2], s.cot, s.fetch.at[15])
        block.start()

        def one(n, cut):
            g[:, cut] = dot_nt(s.k[rows, :], wk[cut, :]) + dot_nt(s.v[rows, :], wv[cut, :])

        tiles(4, 256)(one)

        @pl.when(b == seq)
        def _():
            def two(n, cut):
                g[:, cut] = g[:, cut] + dot_nt(s.dq[...], wq[cut, :])

            tiles(4, 256)(two)

        block.wait()

        def three(r, part):
            norm_back(s.cot[part, :].astype(F32), g[part, :], 0, None)
            fpart[b // 2, b % 2, part, :] = g[part, :].astype(BF16)

        tiles(5, 64)(three)

    gradient(13, lambda: s.normed[mine, :], lambda cut: s.dq[:, cut])
    for part_of in range(4):
        frames_part(part_of, pl.ds(part_of * 320, 320))
        comm.work(3.8)
    frames_core = comm.copy(fpart.at[:, 1 - c], s.fcore, 17, 2, comm.to_c)
    comm.go(17, 2, frames_core)
    flat = jnp.concatenate([s.ng[...], jnp.zeros((120, 1024), F32)], axis=0).T
    s.nown[...] = flat.reshape(4, 2, 2, 2, 32, 128)
    comm.source[16] = s.nown
    comm.go(16, 0, comm.from_core(16))
    gradient(14, lambda: s.normed[...], lambda cut: s.k[:, cut], 4.0)
    frames_core.wait_recv()

    def frames_sum(b, carry):
        rows = pl.ds(pl.multiple_of(lax.rem(b, 5) * 64, 64), 64)
        s.fcore[b // 5, rows] = s.fcore[b // 5, rows] + fpart[b // 5, c, rows]
        return carry

    lax.fori_loop(0, 10, frames_sum, 0)
    frames_x = comm.copy(s.fcore.at[1 - x], o.fmine.at[1], 17, 3, comm.to_x)
    comm.go(17, 3, frames_x)
    frames_keep = pltpu.make_async_copy(s.fcore.at[x], o.fmine.at[0], s.keep.at[18])
    frames_keep.start()
    comm.stage1(16)
    gradient(15, lambda: s.normed[...], lambda cut: s.v[:, cut], 4.0)
    comm.stage2(16)
    comm.pump()
    comm.stage3(16)
    comm.finish()
    text_x.wait_recv()
    frames_x.wait_recv()
    text_keep.wait()
    frames_keep.wait()
    save_gr.wait()


def run_backward_kernel(args):
    S, V, D_SEM = jax.ShapeDtypeStruct, pltpu.VMEM, pltpu.SemaphoreType.DMA
    rows, block = (320, 1024), (32, 1024)
    shapes = dict(
        fin=S((16, 4) + block, BF16), nfin=S((4, 32, 128), F32), fmine=S((2,) + rows, BF16), tmine=S((2, 16, 1024), BF16), gr=S(rows, F32)
    )
    scratch = dict(
        send=D_SEM((18, 8)), recv=D_SEM((18, 8)), own=D_SEM((6,)), keep=D_SEM((19,)), fetch=D_SEM((17,)), load=D_SEM((3,)),
        free=pltpu.SemaphoreType.REGULAR,
        sum=V((4, 4, 2, 2) + block, BF16), core=V((4, 4, 2, 2) + block, BF16), xy=V((16, 4, 2) + block, BF16), cc=V((16, 4) + block, BF16), xw=V((2, 2, 16, 1024), BF16), yw=V((2, 2, 16, 1024), BF16),
        big=V((1792, 1024), BF16),
        nsum=V((4, 2, 2, 32, 128), F32), ncore=V((4, 2, 2, 32, 128), F32), nxy=V((4, 2, 32, 128), F32),
        ncc=V((4, 32, 128), F32), nown=V((4, 2, 2, 2, 32, 128), F32),
        gb=V((8, 1024), F32), r=V(rows, F32), g=V(rows, F32), cot=V(rows, BF16), ctx=V(rows, BF16), q=V(rows, BF16),
        ck=V((64, 1024), BF16), cv=V((64, 1024), BF16), clse=V((4, 1280), F32), nc=V(rows, BF16), text=V((64, 1024), BF16),
        k=V((1280, 1024), BF16), v=V((1280, 1024), BF16), lse=V((4, 1280), F32), normed=V((1280, 1024), BF16), w=V((3, 1024, 1024), BF16),
        bias=V((1280, 640), BF16), cbias=V((64, 640), BF16), ng=V((8, 1024), F32), gr=V(rows, F32), branch=V(rows, BF16),
        up=V(rows, BF16), dq=V(rows, BF16), stacked_q=V((1280, 256), BF16), stacked_g=V((1280, 256), BF16),
        total=V((256, 1280), F32), dw=V((2, 1024, 1024), BF16), tpart=V((2, 2, 16, 1024), BF16), tcore=V((2, 16, 1024), BF16),
        tsum=V((2, 16, 1024), BF16), fcore=V((2,) + rows, BF16),
    )
    apart = dict(seg=pltpu.VMEM, text_len=pltpu.SMEM)
    return pallas(backward_kernel, args, shapes, scratch, apart, dict(collective_id=1))


def finish_kernel(i, o, s):
    coming = []

    def fetch(src, dst):
        copy = pltpu.make_async_copy(src, dst, s.fetch.at[len(coming)])
        copy.start()
        coming.append(copy)
        return copy

    fetch(i.out, s.out)
    fetch(i.frames, s.frames)
    fetch(i.gr, s.gr)
    fetch(i.fmine, s.fmine)
    parts = [fetch(i.fin.at[u, 0 : 2 if u in WIDE else 4], s.fin.at[u, 0 : 2 if u in WIDE else 4]) for u in range(16)]
    going = []

    def put(src, dst):
        copy = pltpu.make_async_copy(src, dst, s.put.at[len(going)])
        copy.start()
        going.append(copy)

    coming[0].wait()
    put(s.out, o.out)
    for copy in coming[1:4]:
        copy.wait()
    gain = i.gb[0:1, :]

    def rows_of(b, rows):
        values = s.frames[rows, :].astype(F32)
        center = values - jnp.mean(values, axis=-1, keepdims=True)
        scale = lax.rsqrt(jnp.mean(center * center, axis=-1, keepdims=True) + 1e-05)
        hat = center * scale
        h = (s.fmine[0, rows, :].astype(F32) + s.fmine[1, rows, :].astype(F32)) * gain
        back = (h - jnp.mean(h, axis=-1, keepdims=True) - hat * jnp.mean(h * hat, axis=-1, keepdims=True)) * scale
        s.frames[rows, :] = (s.gr[rows, :] + back).astype(BF16)

    tiles(5, 64)(rows_of)
    put(s.frames, o.frames)

    def total(u):
        parts[u].wait()
        terms = [s.fin[u, k].astype(F32) for k in range(2 if u in WIDE else 4)]
        return sum(terms[1:], terms[0])

    for k in range(4):
        s.down[k * 32 : (k + 1) * 32, :] = total(DOWN_UNITS[k])
    put(s.down, o.down)
    for j in range(4):
        s.upraw[:, j * 1024 : (j + 1) * 1024] = total(4 + j)

    def put_up(b, block):
        s.up[:, b * 128 : b * 128 + 128] = block

    shuffle_columns(lambda b: s.upraw[:, b * 128 : b * 128 + 128], put_up, True)
    put(s.up, o.up)
    for src, dst, first, count in (
        (s.cout, o.cout, 8, 1),
        (s.cqkv, o.cqkv, 9, 3),
        (s.sout, o.sout, 12, 1),
        (s.sqkv, o.sqkv, 13, 3),
    ):
        for k in range(count):
            src[:, k * 1024 : (k + 1) * 1024] = total(first + k)
        put(src, dst)
    n = ((i.nfin[0] + i.nfin[1]) + (i.nfin[2] + i.nfin[3])).T
    s.gain[...] = n[:3]
    s.shift[...] = n[3:6]
    s.text[...] = (i.tmine[0].astype(F32) + i.tmine[1].astype(F32)).astype(BF16)
    put(s.gain, o.gain)
    put(s.shift, o.shift)
    put(s.text, o.text)
    for copy in going:
        copy.wait()


def run_finish_kernel(args):
    S, V, D_SEM = jax.ShapeDtypeStruct, pltpu.VMEM, pltpu.SemaphoreType.DMA
    rows = (320, 1024)
    shapes = dict(
        out=S(rows, BF16), frames=S(rows, BF16), text=S((16, 1024), BF16), gain=S((3, 32), F32), shift=S((3, 32), F32),
        sqkv=S((32, 3072), F32), sout=S((32, 1024), F32), cqkv=S((32, 3072), F32), cout=S((32, 1024), F32), up=S((32, 4096), F32),
        down=S((128, 1024), F32),
    )
    scratch = {n: V(v.shape, v.dtype) for n, v in shapes.items()}
    scratch.update(
        fin=V((16, 4, 32, 1024), BF16), fmine=V((2,) + rows, BF16), gr=V(rows, F32), upraw=V((32, 4096), F32), fetch=D_SEM((20,)),
        put=D_SEM((11,)),
    )
    apart = dict(nfin=pltpu.VMEM, tmine=pltpu.VMEM, gb=pltpu.VMEM)
    return pallas(finish_kernel, args, shapes, scratch, apart, dict())


def fetch_all(norm_gain, norm_bias, self_qkv, self_out, cross_qkv, cross_out, ffn_up, ffn_down):
    first = (
        lax.all_gather(norm_gain, ("dp", "seq"), axis=0, tiled=True),
        lax.all_gather(norm_bias, ("dp", "seq"), axis=0, tiled=True),
        lax.all_gather(self_qkv, ("dp", "seq"), axis=0, tiled=True),
        lax.all_gather(self_out, ("dp", "seq"), axis=0, tiled=True),
    )
    second = (
        lax.all_gather(cross_qkv, ("dp", "seq"), axis=0, tiled=True),
        lax.all_gather(cross_out, ("dp", "seq"), axis=0, tiled=True),
    )
    third = (
        lax.all_gather(ffn_up, ("dp", "seq"), axis=0, tiled=True),
        lax.all_gather(ffn_down, ("dp", "seq"), axis=0, tiled=True),
    )
    return tuple(first) + tuple(second) + tuple(third)


def run_forward(frames, local_seg, frame_seg, text_seg, text_states, offset, weights):
    norm_gain, norm_bias, self_qkv, self_out, cross_qkv, cross_out, ffn_up, ffn_down = weights
    gains = norm_gain.astype(jnp.float32)
    biases = norm_bias.astype(jnp.float32)
    inputs = frames.astype(jnp.float32)
    normed_self = layer_norm(inputs, gains[:, 0], biases[:, 0]).astype(jnp.bfloat16)
    queries = jnp.dot(normed_self, self_qkv[:, :D], preferred_element_type=jnp.float32).astype(
        jnp.bfloat16
    )
    pair_weights = self_qkv[:, D:].reshape(D, 2, D)
    key_value = jnp.einsum(
        "rcd,dje->jrce", normed_self, pair_weights, preferred_element_type=jnp.float32
    ).astype(jnp.bfloat16)
    gathered = lax.all_gather(key_value, "seq", axis=2, tiled=True)
    self_context, self_logsum = lax.map(
        lambda record: attend(
            record[0], record[1], record[2], self_allowed(record[3], record[4], offset)
        ),
        (queries, gathered[0], gathered[1], local_seg, frame_seg),
    )
    self_context = self_context.astype(jnp.bfloat16)
    resid_one = inputs + jnp.dot(self_context, self_out, preferred_element_type=jnp.float32)
    normed_cross = layer_norm(resid_one, gains[:, 1], biases[:, 1]).astype(jnp.bfloat16)
    cross_queries = jnp.dot(
        normed_cross, cross_qkv[:, :D], preferred_element_type=jnp.float32
    ).astype(jnp.bfloat16)
    text_weights = cross_qkv[:, D:].reshape(D, 2, D)
    text_pair = jnp.einsum(
        "rtd,dje->jrte", text_states, text_weights, preferred_element_type=jnp.float32
    ).astype(jnp.bfloat16)
    cross_context, cross_logsum = lax.map(
        lambda record: attend(
            record[0], record[1], record[2], record[3][:, None] == record[4][None, :]
        ),
        (cross_queries, text_pair[0], text_pair[1], local_seg, text_seg),
    )
    cross_context = cross_context.astype(jnp.bfloat16)
    resid_two = resid_one + jnp.dot(cross_context, cross_out, preferred_element_type=jnp.float32)
    normed_ffn = layer_norm(resid_two, gains[:, 2], biases[:, 2]).astype(jnp.bfloat16)
    hidden_pre = jnp.dot(normed_ffn, ffn_up, preferred_element_type=jnp.float32)
    activated = exact_gelu(hidden_pre).astype(jnp.bfloat16)
    outcome = resid_two + jnp.dot(activated, ffn_down, preferred_element_type=jnp.float32)
    saved = (
        inputs,
        normed_self,
        queries,
        gathered,
        self_context,
        self_logsum,
        resid_one,
        normed_cross,
        cross_queries,
        text_pair,
        cross_context,
        cross_logsum,
        resid_two,
        normed_ffn,
        hidden_pre,
        activated,
    )
    return (outcome, saved)


def generic_body(
    frames,
    frame_seg,
    text_states,
    text_len,
    norm_gain,
    norm_bias,
    self_qkv,
    self_out,
    cross_qkv,
    cross_out,
    ffn_up,
    ffn_down,
    cotangent,
):
    width = frames.shape[1]
    offset = lax.axis_index("seq") * width
    local_seg = lax.dynamic_slice_in_dim(frame_seg, offset, width, 1)
    text_seg = text_segments(text_len)
    shards = (norm_gain, norm_bias, self_qkv, self_out, cross_qkv, cross_out, ffn_up, ffn_down)
    weights = fetch_all(*shards)
    outcome, saved = run_forward(
        frames, local_seg, frame_seg, text_seg, text_states, offset, weights
    )
    frames_out = outcome.astype(jnp.bfloat16)
    (
        inputs,
        normed_self,
        queries,
        gathered,
        self_context,
        self_logsum,
        resid_one,
        normed_cross,
        cross_queries,
        text_pair,
        cross_context,
        cross_logsum,
        resid_two,
        normed_ffn,
        hidden_pre,
        activated,
    ) = saved
    gain_full, bias_full, self_full, self_proj, cross_full, cross_proj, up_full, down_full = weights
    gains = gain_full.astype(jnp.float32)
    biases = bias_full.astype(jnp.float32)
    upstream = cotangent.astype(jnp.float32)
    down_grad = jnp.einsum("rcf,rcd->fd", activated, cotangent, preferred_element_type=jnp.float32)
    grad_act = jnp.einsum("rcd,fd->rcf", cotangent, down_full, preferred_element_type=jnp.float32)
    unused_value, gelu_pull = jax.vjp(exact_gelu, hidden_pre)
    grad_pre = gelu_pull(grad_act)[0].astype(jnp.bfloat16)
    up_grad = jnp.einsum("rcd,rcf->df", normed_ffn, grad_pre, preferred_element_type=jnp.float32)
    grad_normed = jnp.einsum("rcf,df->rcd", grad_pre, up_full, preferred_element_type=jnp.float32)
    grad_back, gain_two, bias_two = norm_back(resid_two, gains[:, 2], biases[:, 2], grad_normed)
    grad_resid_two = upstream + grad_back
    ffn_shares = (
        lax.psum_scatter(up_grad, ("dp", "seq"), scatter_dimension=0, tiled=True),
        lax.psum_scatter(down_grad, ("dp", "seq"), scatter_dimension=0, tiled=True),
    )
    branch_two = grad_resid_two.astype(jnp.bfloat16)
    cross_out_grad = jnp.einsum(
        "rcd,rce->de", cross_context, branch_two, preferred_element_type=jnp.float32
    )
    grad_context = jnp.einsum(
        "rce,de->rcd", branch_two, cross_proj, preferred_element_type=jnp.float32
    ).astype(jnp.bfloat16)
    grad_cross_q, grad_cross_k, grad_cross_v = lax.map(
        lambda record: attend_back(
            record[0],
            record[1],
            record[2],
            record[3][:, None] == record[4][None, :],
            record[5],
            record[6],
        ),
        (
            cross_queries,
            text_pair[0],
            text_pair[1],
            local_seg,
            text_seg,
            cross_logsum,
            grad_context,
        ),
    )
    text_joined = jnp.transpose(jnp.concatenate([grad_cross_k, grad_cross_v], axis=2), (1, 0, 2))
    text_summed = lax.psum_scatter(
        text_joined.astype(jnp.bfloat16), "seq", scatter_dimension=0, tiled=True
    ).astype(jnp.float32)
    text_shares = jnp.transpose(text_summed, (1, 0, 2)).astype(jnp.bfloat16)
    share = text_shares.shape[1]
    text_part = lax.dynamic_slice_in_dim(text_states, lax.axis_index("seq") * share, share, 1)
    text_kv_grad = jnp.einsum(
        "rtd,rte->de", text_part, text_shares, preferred_element_type=jnp.float32
    )
    text_grad = jnp.einsum(
        "rte,de->rtd", text_shares, cross_full[:, D:], preferred_element_type=jnp.float32
    ).astype(jnp.bfloat16)
    grad_cross_q = grad_cross_q.astype(jnp.bfloat16)
    cross_q_grad = jnp.einsum(
        "rcd,rce->de", normed_cross, grad_cross_q, preferred_element_type=jnp.float32
    )
    cross_qkv_grad = jnp.concatenate([cross_q_grad, text_kv_grad], axis=1)
    grad_normed = jnp.einsum(
        "rce,de->rcd", grad_cross_q, cross_full[:, :D], preferred_element_type=jnp.float32
    )
    grad_back, gain_one, bias_one = norm_back(resid_one, gains[:, 1], biases[:, 1], grad_normed)
    grad_resid_one = grad_resid_two + grad_back
    cross_shares = (
        lax.psum_scatter(cross_qkv_grad, ("dp", "seq"), scatter_dimension=0, tiled=True),
        lax.psum_scatter(cross_out_grad, ("dp", "seq"), scatter_dimension=0, tiled=True),
    )
    branch_one = grad_resid_one.astype(jnp.bfloat16)
    self_out_grad = jnp.einsum(
        "rcd,rce->de", self_context, branch_one, preferred_element_type=jnp.float32
    )
    grad_context = jnp.einsum(
        "rce,de->rcd", branch_one, self_proj, preferred_element_type=jnp.float32
    ).astype(jnp.bfloat16)
    grad_self_q, grad_self_k, grad_self_v = lax.map(
        lambda record: attend_back(
            record[0],
            record[1],
            record[2],
            self_allowed(record[3], record[4], offset),
            record[5],
            record[6],
        ),
        (queries, gathered[0], gathered[1], local_seg, frame_seg, self_logsum, grad_context),
    )
    joined = jnp.concatenate([grad_self_k, grad_self_v], axis=2)
    summed = lax.psum_scatter(
        jnp.transpose(joined, (1, 0, 2)).astype(jnp.bfloat16),
        "seq",
        scatter_dimension=0,
        tiled=True,
    ).astype(jnp.float32)
    key_shares = jnp.transpose(summed, (1, 0, 2)).astype(jnp.bfloat16)
    all_grads = jnp.concatenate([grad_self_q.astype(jnp.bfloat16), key_shares], axis=2)
    self_qkv_grad = jnp.einsum(
        "rcd,rce->de", normed_self, all_grads, preferred_element_type=jnp.float32
    )
    grad_normed = jnp.einsum(
        "rce,de->rcd", all_grads, self_full, preferred_element_type=jnp.float32
    )
    grad_back, gain_zero, bias_zero = norm_back(inputs, gains[:, 0], biases[:, 0], grad_normed)
    frames_grad = (grad_resid_one + grad_back).astype(jnp.bfloat16)
    gain_grad = jnp.stack([gain_zero, gain_one, gain_two], axis=1)
    bias_grad = jnp.stack([bias_zero, bias_one, bias_two], axis=1)
    self_shares = (
        lax.psum_scatter(gain_grad, ("dp", "seq"), scatter_dimension=0, tiled=True),
        lax.psum_scatter(bias_grad, ("dp", "seq"), scatter_dimension=0, tiled=True),
        lax.psum_scatter(self_qkv_grad, ("dp", "seq"), scatter_dimension=0, tiled=True),
        lax.psum_scatter(self_out_grad, ("dp", "seq"), scatter_dimension=0, tiled=True),
    )
    return (
        frames_out,
        frames_grad,
        text_grad,
        self_shares[0],
        self_shares[1],
        self_shares[2],
        self_shares[3],
        cross_shares[0],
        cross_shares[1],
        ffn_shares[0],
        ffn_shares[1],
    )


def fast_body(
    frames,
    frame_seg,
    text_states,
    text_len,
    norm_gain,
    norm_bias,
    self_qkv,
    self_out,
    cross_qkv,
    cross_out,
    ffn_up,
    ffn_down,
    cotangent,
):
    args = dict(
        frames=frames[0],
        gain=norm_gain.T,
        shift=norm_bias.T,
        sqkv=self_qkv,
        sout=self_out,
        cqkv=cross_qkv,
        cout=cross_out,
        up=ffn_up,
        down=ffn_down.reshape(4, 32, D),
        cot=cotangent[0],
        text=text_states[0],
        seg=frame_seg,
        text_len=text_len,
    )
    f = types.SimpleNamespace(**run_forward_kernel(args))
    a = types.SimpleNamespace(**args)
    units = (4, 4, 2, 2, 2, 32, D)
    back = run_backward_kernel(
        dict(
            ddown=f.ddown.reshape(units),
            slope=f.slope,
            nf=f.nf,
            down=f.down,
            up=f.up,
            cot=a.cot,
            gb=f.gb,
            r2=f.r2,
            r1=f.r1,
            cctx=f.cctx,
            ctx=f.ctx,
            cq=f.cq,
            ck=f.ck,
            cv=f.cv,
            clse=f.clse,
            nc=f.nc,
            text=a.text,
            q=f.q,
            k=f.k,
            v=f.v,
            lse=f.lse,
            normed=f.normed,
            frames=f.frames,
            cout=f.cout,
            cqkv=f.cqkv,
            sout=f.sout,
            sqkv=f.sqkv,
            seg=a.seg,
            text_len=a.text_len,
        )
    )
    b = types.SimpleNamespace(**back)
    outs = run_finish_kernel(
        dict(
            fin=b.fin, nfin=b.nfin, fmine=b.fmine, tmine=b.tmine, gr=b.gr, frames=a.frames, gb=f.gb, out=f.out
        )
    )
    n = types.SimpleNamespace(**outs)
    return (
        n.out[None],
        n.frames[None],
        n.text[None],
        n.gain.T,
        n.shift.T,
        n.sqkv,
        n.sout,
        n.cqkv,
        n.cout,
        n.up,
        n.down,
    )


def solution(mesh):
    return jax.shard_map(
        fast_body if dict(mesh.shape) == {"dp": 8, "seq": 4} else generic_body,
        mesh=mesh,
        in_specs=(
            P("dp", "seq", None),
            P("dp", None),
            P("dp", None, None),
            P("dp", None),
            P(("dp", "seq"), None),
            P(("dp", "seq"), None),
            P(("dp", "seq"), None),
            P(("dp", "seq"), None),
            P(("dp", "seq"), None),
            P(("dp", "seq"), None),
            P(("dp", "seq"), None),
            P(("dp", "seq"), None),
            P("dp", "seq", None),
        ),
        out_specs=(
            P("dp", "seq", None),
            P("dp", "seq", None),
            P("dp", "seq", None),
            P(("dp", "seq"), None),
            P(("dp", "seq"), None),
            P(("dp", "seq"), None),
            P(("dp", "seq"), None),
            P(("dp", "seq"), None),
            P(("dp", "seq"), None),
            P(("dp", "seq"), None),
            P(("dp", "seq"), None),
        ),
        check_vma=False,
    )
```

```python
import types

import jax
import jax.numpy as jnp
from jax import lax
from jax.experimental import pallas as pl
from jax.experimental.pallas import tpu as pltpu
from jax.sharding import PartitionSpec as P

D = 1024
HEADS = 16
HEAD_DIM = 64
TEXT_LEN = 64


def layer_norm(values, gain, bias):
    center = values - jnp.mean(values, axis=-1, keepdims=True)
    spread = jnp.mean(center * center, axis=-1, keepdims=True)
    return center * lax.rsqrt(spread + 1e-05) * gain + bias


def norm_back(values, gain, bias, upstream):
    unused_value, pullback = jax.vjp(layer_norm, values, gain, bias)
    return pullback(upstream)


def exact_gelu(values):
    return jax.nn.gelu(values, approximate=False)


def split_heads(values):
    return values.reshape(values.shape[0], HEADS, HEAD_DIM)


def text_segments(text_len):
    bounds = jnp.cumsum(text_len, axis=1)
    positions = jnp.arange(TEXT_LEN, dtype=jnp.int32)
    return jnp.sum((positions[None, :, None] >= bounds[:, None, :]).astype(jnp.int32), axis=2)


def self_allowed(local_seg, full_seg, offset):
    row_pos = offset + jnp.arange(local_seg.shape[0], dtype=jnp.int32)
    col_pos = jnp.arange(full_seg.shape[0], dtype=jnp.int32)
    return (row_pos[:, None] >= col_pos[None, :]) & (local_seg[:, None] == full_seg[None, :])


def masked_scores(queries, keys_in, allowed):
    factor = HEAD_DIM ** (-0.5)
    scores = (
        jnp.einsum(
            "qhe,khe->hqk",
            split_heads(queries),
            split_heads(keys_in),
            preferred_element_type=jnp.float32,
        )
        * factor
    )
    return jnp.where(allowed[None], scores, -1e30)


def attend(queries, keys_in, values, allowed):
    scores = masked_scores(queries, keys_in, allowed)
    highest = jnp.max(scores, axis=-1, keepdims=True)
    powered = jnp.exp(scores - highest)
    totals = jnp.sum(powered, axis=-1, keepdims=True)
    weights = (powered / totals).astype(jnp.bfloat16)
    context = jnp.einsum(
        "hqk,khe->qhe", weights, split_heads(values), preferred_element_type=jnp.float32
    )
    return (context.reshape(queries.shape[0], -1), highest + jnp.log(totals))


def attend_back(queries, keys_in, values, allowed, logsum, upstream):
    factor = HEAD_DIM ** (-0.5)
    probs_full = jnp.exp(masked_scores(queries, keys_in, allowed) - logsum)
    grad_heads = split_heads(upstream)
    grad_probs = jnp.einsum(
        "qhe,khe->hqk", grad_heads, split_heads(values), preferred_element_type=jnp.float32
    )
    row_inner = jnp.sum(probs_full * grad_probs, axis=-1, keepdims=True)
    grad_scores = (probs_full * (grad_probs - row_inner)).astype(jnp.bfloat16)
    grad_queries = (
        jnp.einsum(
            "hqk,khe->qhe", grad_scores, split_heads(keys_in), preferred_element_type=jnp.float32
        )
        * factor
    )
    grad_keys = (
        jnp.einsum(
            "hqk,qhe->khe", grad_scores, split_heads(queries), preferred_element_type=jnp.float32
        )
        * factor
    )
    grad_values = jnp.einsum(
        "hqk,qhe->khe",
        probs_full.astype(jnp.bfloat16),
        grad_heads,
        preferred_element_type=jnp.float32,
    )
    return (
        grad_queries.reshape(queries.shape[0], -1),
        grad_keys.reshape(keys_in.shape[0], -1),
        grad_values.reshape(values.shape[0], -1),
    )


F32, BF16 = jnp.float32, jnp.bfloat16
MESH = pl.DeviceIdType.MESH
VMEM_BYTES = 64 * 2**20
BLOCK = 256
LEAD = 6
PACE_FORWARD = 3.1
PACE_BACKWARD = 3.1


def place():
    dp, seq = lax.axis_index("dp"), lax.axis_index("seq")
    return dp // 2, lax.rem(dp, 2), seq // 2, lax.rem(seq, 2)


def device(z, y, x, c):
    return (z * 2 + y, x * 2 + c)


def greet(z, y, x, c):
    barrier = pltpu.get_barrier_semaphore()
    others = [device(lax.rem(z + k, 4), y, x, c) for k in (1, 2, 3)]
    others += [device(z, 1 - y, x, c), device(z, y, 1 - x, c), device(z, y, x, 1 - c)]
    for other in others:
        pl.semaphore_signal(barrier, inc=1, device_id=other, device_id_type=MESH)
    pl.semaphore_wait(barrier, len(others))


def dot_nn(a, b):
    return jnp.dot(a, b, preferred_element_type=F32)


def dot_nt(a, b):
    return lax.dot_general(a, b, (((1,), (1,)), ((), ())), preferred_element_type=F32)


def dot_tn(a, b):
    return lax.dot_general(a, b, (((0,), (0,)), ((), ())), preferred_element_type=F32)


def tiles(count, size):
    def run(step):
        def one(i, carry):
            step(i, pl.ds(pl.multiple_of(i * size, size), size))
            return carry

        lax.fori_loop(0, count, one, 0)

    return run


def normalize(block, gain, bias):
    center = block - jnp.mean(block, axis=-1, keepdims=True)
    spread = jnp.mean(center * center, axis=-1, keepdims=True)
    return center * lax.rsqrt(spread + 1e-05) * gain + bias


def stack_heads(dst, src, group, factor):
    rows = src.shape[0]
    part = src[:, group * 256 : group * 256 + 256]
    if factor != 1.0:
        part = part * jnp.asarray(factor, part.dtype)
    head = lax.broadcasted_iota(jnp.int32, part.shape, 1) // HEAD_DIM
    for h in range(4):
        dst[h * rows : (h + 1) * rows, :] = jnp.where(head == h, part, jnp.zeros_like(part))


def unstack_heads(wide, rows):
    parts = [wide[h * 64 : (h + 1) * 64, h * rows : (h + 1) * rows] for h in range(4)]
    return jnp.concatenate(parts, axis=0).T


def attend_group(group, q, k, v, bias, stacked, scores, total, context, logsum, between):
    rows, keys = q.shape[0], k.shape[0]
    size = min(BLOCK, keys)
    cols = slice(group * 256, group * 256 + 256)
    stack_heads(stacked, q, group, HEAD_DIM**-0.5)

    def score(i, highest):
        at = pl.ds(pl.multiple_of(i * size, size), size)
        s = dot_nt(k[at, cols], stacked[...]) + bias[at, :].astype(F32)
        scores[at, :] = s
        return jnp.maximum(highest, jnp.max(s, axis=0, keepdims=True))

    highest = lax.fori_loop(0, keys // size, score, jnp.full((1, 4 * rows), -3e38, F32))
    between()
    total[...] = jnp.zeros_like(total)

    def weigh(i, summed):
        at = pl.ds(pl.multiple_of(i * size, size), size)
        p = jnp.exp(scores[at, :] - highest)
        total[...] += dot_tn(v[at, cols], p.astype(BF16))
        return summed + jnp.sum(p, axis=0, keepdims=True)

    summed = lax.fori_loop(0, keys // size, weigh, jnp.zeros((1, 4 * rows), F32))
    logsum[group : group + 1, :] = highest + jnp.log(summed)
    context[:, cols] = unstack_heads(total[...] / summed, rows).astype(BF16)


class Gathering:
    def __init__(self, at, units, over_y, wide, send_sem, recv_sem, own_sem):
        self.at, self.units, self.n = at, units, len(units)
        self.over_y, self.wide = over_y, wide
        self.order = [u for u in range(self.n) if u not in wide]
        self.send_sem, self.recv_sem, self.own_sem = send_sem, recv_sem, own_sem
        self.sent, self.step, self.spreads, self.since = [], 0, False, 0.0
        z, y, x, c = at
        self.to_x, self.to_y, self.to_c = device(z, y, 1 - x, c), device(z, 1 - y, x, c), device(z, y, x, 1 - c)

    def copy(self, src, dst, u, k, dev):
        return pltpu.make_async_remote_copy(
            src_ref=src,
            dst_ref=dst,
            send_sem=self.send_sem.at[u, k],
            recv_sem=self.recv_sem.at[u, k],
            device_id=dev,
            device_id_type=MESH,
        )

    def go(self, copy):
        copy.start()
        self.sent.append(copy)

    def same(self, u, k, dev, *spot):
        view = self.units[u][1](*spot)
        return self.copy(view, view, u, k, dev)

    def across(self, u, k):
        z, y, x, c = self.at
        src, dst = self.units[u][0], self.units[u][1](z, y, x, c)
        return self.copy(src, dst, u, k - 1, device(lax.rem(z + k, 4), y, x, c))

    def own(self, u):
        return pltpu.make_async_copy(self.units[u][0], self.units[u][1](*self.at), self.own_sem.at[u])

    def first(self, p):
        if p < len(self.order):
            u = self.order[p]
            self.own(u).start()
            for k in (1, 2, 3):
                self.go(self.across(u, k))

    def cuts(self, u):
        if u in self.over_y:
            return pl.ds(0, 4), None
        return pl.ds(0, 2), pl.ds(2, 2)

    def spread(self, p):
        z, y, x, c = self.at
        every, u, same, go = pl.ds(0, 4), self.order[p], self.same, self.go
        for k in (1, 2, 3):
            self.across(u, k).wait_recv()
        self.own(u).wait()
        go(same(u, 3, self.to_x, every, y, x, c))
        go(same(u, 4, self.to_y, every, y, x, c))
        go(same(u, 5, self.to_c, every, y, x, c))
        self.first(p + LEAD)

    def work(self, us):
        self.since += us
        if self.since >= PACE_FORWARD:
            self.pump()

    def pump(self):
        z, y, x, c = self.at
        every = pl.ds(0, 4)
        self.since = 0.0
        t, n, same, go = self.step, len(self.order), self.same, self.go
        if t >= n + 2:
            return
        if not self.spreads:
            self.spreads = True
            if t < n:
                self.spread(t)
            return
        self.spreads = False
        self.step += 1
        if 0 <= t - 1 < n:
            u = self.order[t - 1]
            low, high = self.cuts(u)
            same(u, 3, self.to_x, every, y, 1 - x, c).wait_recv()
            go(same(u, 6, self.to_y, low, y, 1 - x, c))
            go(same(u, 7, self.to_c, every, y, 1 - x, c))
            same(u, 4, self.to_y, every, 1 - y, x, c).wait_recv()
            if high is not None:
                go(same(u, 8, self.to_x, high, 1 - y, x, c))
            go(same(u, 9, self.to_c, every, 1 - y, x, c))
        if 0 <= t - 2 < n:
            u = self.order[t - 2]
            low, high = self.cuts(u)
            same(u, 6, self.to_y, low, 1 - y, 1 - x, c).wait_recv()
            go(same(u, 10, self.to_c, low, 1 - y, 1 - x, c))
            if high is not None:
                same(u, 8, self.to_x, high, 1 - y, 1 - x, c).wait_recv()
                go(same(u, 11, self.to_c, high, 1 - y, 1 - x, c))
        for u, steps in self.wide.items():
            for stage in range(4):
                if steps[stage] == t:
                    self.widen(u, stage)

    def half(self, u, k, dev, h, *spot):
        view = self.units[u][1](*spot).at[h * 16 : h * 16 + 16]
        return self.copy(view, view, u, k, dev)

    def plane(self, u, k, dev, zz, cc):
        return self.same(u, k, dev, zz, pl.ds(0, 2), pl.ds(0, 2), cc)

    def widen(self, u, stage):
        z, y, x, c = self.at
        go = self.go
        if stage == 0:
            self.own(u).start()
            src, dst = self.units[u][0], self.units[u][1](z, y, x, c)
            go(self.copy(src, dst, u, 0, self.to_x))
            go(self.copy(src, dst, u, 1, self.to_y))
        elif stage == 1:
            self.same(u, 0, self.to_x, z, y, 1 - x, c).wait_recv()
            go(self.half(u, 2, self.to_y, 0, z, y, 1 - x, c))
            self.same(u, 1, self.to_y, z, 1 - y, x, c).wait_recv()
            go(self.half(u, 3, self.to_x, 1, z, 1 - y, x, c))
        elif stage == 2:
            self.own(u).wait()
            self.half(u, 2, self.to_y, 0, z, 1 - y, 1 - x, c).wait_recv()
            self.half(u, 3, self.to_x, 1, z, 1 - y, 1 - x, c).wait_recv()
            for k in (1, 2, 3):
                go(self.plane(u, 3 + k, device(lax.rem(z + k, 4), y, x, c), z, c))
            go(self.plane(u, 7, self.to_c, z, c))
        else:
            for k in (1, 2, 3):
                other = lax.rem(z + 4 - k, 4)
                self.plane(u, 3 + k, self.to_c, other, c).wait_recv()
                go(self.plane(u, 7 + k, self.to_c, other, c))

    def need(self, u):
        z, y, x, c = self.at
        every = pl.ds(0, 4)
        if u in self.wide:
            while self.step <= self.wide[u][3]:
                self.pump()
            self.plane(u, 7, self.to_c, z, 1 - c).wait_recv()
            for k in (1, 2, 3):
                self.plane(u, 7 + k, self.to_c, lax.rem(z + 4 - k, 4), 1 - c).wait_recv()
            return
        while self.step <= self.order.index(u) + 2:
            self.pump()
        low, high = self.cuts(u)
        self.same(u, 5, self.to_c, every, y, x, 1 - c).wait_recv()
        self.same(u, 7, self.to_c, every, y, 1 - x, 1 - c).wait_recv()
        self.same(u, 9, self.to_c, every, 1 - y, x, 1 - c).wait_recv()
        self.same(u, 10, self.to_c, low, 1 - y, 1 - x, 1 - c).wait_recv()
        if high is not None:
            self.same(u, 11, self.to_c, high, 1 - y, 1 - x, 1 - c).wait_recv()


def same_clip(seg, seq):
    own = seg[:, 0:320]
    for k in range(1, 4):
        own = jnp.where(seq == k, seg[:, k * 320 : (k + 1) * 320], own)

    def down(b):
        part = seg[:, pl.ds(pl.multiple_of(b * 128, 128), 128)]
        return jnp.broadcast_to(part, (128, 128)).T[:, :1]

    return own, down


def set_masks(i, seq, bias, text_bias, copies):
    own, down = same_clip(i.seg, seq)

    def mask(b, rows):
        key = lax.broadcasted_iota(jnp.int32, (128, 320), 0) + b * 128
        query = lax.broadcasted_iota(jnp.int32, (128, 320), 1) + seq * 320
        seen = (key <= query) & (down(b) == own)
        block = jnp.where(seen, 0.0, -1e30).astype(F32)
        bias[rows, :] = jnp.concatenate([block] * copies, axis=1).astype(BF16)

    tiles(10, 128)(mask)
    slot = lax.broadcasted_iota(jnp.int32, (TEXT_LEN, 320), 0)
    clip = jnp.zeros((TEXT_LEN, 320), jnp.int32)
    bound = jnp.int32(0)
    for k in range(4):
        bound = bound + i.text_len[0, k]
        clip = clip + (slot >= bound).astype(jnp.int32)
    block = jnp.where(clip == own, 0.0, -1e30).astype(F32)
    text_bias[...] = jnp.concatenate([block] * copies, axis=1).astype(BF16)


def shuffle_columns(part, put, back):
    lane = lax.broadcasted_iota(jnp.int32, (32, 128), 1) // 32
    for b in range(32):
        block = jnp.zeros((32, 128), F32)
        for q in range(4):
            source, quarter = (q * 8 + b // 4, b % 4) if back else (b % 8 * 4 + q, b // 8)
            chunk = part(source)
            moved = pltpu.roll(chunk, (q - quarter) % 4 * 32, 1) if q != quarter else chunk
            block = jnp.where(lane == q, moved, block)
        put(b, block)


def forward_kernel(i, o, s):
    at = place()
    z, y, x, c = at
    seq = x * 2 + c
    units = [(s.nin, lambda zz, yy, xx, cc: o.norms.at[zz, yy, xx, cc])]

    def columns(shard, full, count):
        for k in range(count):
            cut = pl.ds(k * 1024, 1024)
            units.append(
                (shard.at[:, cut], lambda zz, yy, xx, cc, cut=cut: full.at[zz, yy, xx, cc, :, cut])
            )

    columns(i.sqkv, o.sqkv, 3)
    columns(i.sout, o.sout, 1)
    columns(i.cqkv, o.cqkv, 3)
    columns(i.cout, o.cout, 1)
    columns(s.upin, o.up, 4)
    for k in range(4):
        units.append(
            (i.down.at[k], lambda zz, yy, xx, cc, k=k: o.down.at[zz, yy, xx, cc, k])
        )
        wide = {12: (0, 1, 2, 10), 16: (6, 7, 8, 16)}
    comm = Gathering(at, units, (1, 2), wide, s.send, s.recv, s.own)
    up_copy = pltpu.make_async_copy(i.up, s.upraw, s.own.at[comm.n + 3])
    up_copy.start()
    s.flat[...] = jnp.zeros_like(s.flat)
    s.flat[0:3, 0:32] = i.gain[...].astype(F32)
    s.flat[3:6, 0:32] = i.shift[...].astype(F32)
    s.nin[...] = s.flat[...].T[:32].astype(BF16)
    greet(*at)
    fr = s.frames
    f = comm.n

    def share(k, dev, xx, cc):
        view = fr.at[xx, cc]
        return comm.copy(view, view, f, k, dev)

    own_frames = pltpu.make_async_copy(i.frames, fr.at[x, c], s.own.at[f])
    own_frames.start()
    cot_copy = pltpu.make_async_copy(i.cot, s.cot, s.own.at[f + 1])
    cot_copy.start()
    text_copy = pltpu.make_async_copy(i.text, s.text, s.own.at[f + 2])
    text_copy.start()
    for u in range(LEAD):
        comm.first(u)
    own_frames.wait()
    comm.go(share(0, comm.to_x, x, c))
    comm.go(share(1, comm.to_c, x, c))
    up_copy.wait()

    def put_up(b, block):
        s.upin[:, b * 128 : b * 128 + 128] = block.astype(BF16)

    shuffle_columns(lambda b: s.upraw[:, b * 128 : b * 128 + 128].astype(F32), put_up, False)

    saves = []

    def save(src, dst):
        copy = pltpu.make_async_copy(src, dst, s.save.at[len(saves)])
        copy.start()
        saves.append(copy)

    set_masks(i, seq, s.bias, s.cbias, 4)

    def weight(u, where):
        comm.need(u)
        src = units[u][1](pl.ds(0, 4), pl.ds(0, 2), pl.ds(0, 2), pl.ds(0, 2))
        dst = s.w.at[where]
        copy = pltpu.make_async_copy(src, dst.reshape(4, 2, 2, 2, 32, 1024), s.load.at[u])
        copy.start()
        copy.wait()
        return dst

    def norm(dst, src_block, k, count):
        gain, bias = s.gb[k : k + 1, :], s.gb[3 + k : 4 + k, :]

        def one(b, rows):
            dst[rows, :] = normalize(src_block(b, rows), gain, bias).astype(BF16)

        tiles(count, 64)(one)

    share(0, comm.to_x, 1 - x, c).wait_recv()
    comm.go(share(2, comm.to_c, 1 - x, c))
    comm.need(0)
    copy = pltpu.make_async_copy(o.norms, s.norms.reshape(4, 2, 2, 2, 32, 128), s.load.at[0])
    copy.start()
    copy.wait()
    s.gb[...] = s.norms[...].astype(F32).T[:8]
    share(1, comm.to_c, x, 1 - c).wait_recv()
    share(2, comm.to_c, 1 - x, 1 - c).wait_recv()
    normed = s.normed

    def frame_block(b, rows):
        return fr[b // 10, lax.rem(b // 5, 2), pl.ds(pl.multiple_of(lax.rem(b, 5) * 64, 64), 64), :].astype(F32)

    norm(normed, frame_block, 0, 20)
    comm.work(4.0)
    save(s.gb, o.gb)
    save(fr, o.frames)
    save(normed, o.normed)

    mine = pl.ds(pl.multiple_of(seq * 320, 64), 320)

    def project(dst, src, w, rows):
        def one(n, cut):
            dst[:, cut] = dot_nn(src[rows, :], w[:, cut]).astype(BF16)

        tiles(4, 256)(one)

    def project_all(dst, w):
        def one(b, rows):
            def two(n, cut):
                dst[rows, cut] = dot_nn(normed[rows, :], w[:, cut]).astype(BF16)

            tiles(4, 256)(two)

        for b in range(4):
            one(b, pl.ds(b * 320, 320))
            comm.work(1.8)

    every_row = pl.ds(0, 320)
    q, k, v = s.q, s.k, s.v
    project(q, normed, weight(1, 0), mine)
    project_all(k, weight(2, 1))
    project_all(v, weight(3, 2))
    save(q, o.q)
    save(k, o.k)
    save(v, o.v)
    for g in range(4):
        attend_group(
            g, q, k, v, s.bias, s.stacked, s.scores, s.total, s.ctx, s.lse, lambda: comm.work(2.0)
        )
        comm.work(2.0)
    save(s.ctx, o.ctx)
    save(s.lse, o.lse)

    def add_project(dst, base, src, w):
        def one(n, cut):
            dst[:, cut] = base(cut) + dot_nn(src[...], w[:, cut])

        tiles(4, 256)(one)

    add_project(s.r1, lambda cut: fr[x, c, :, cut].astype(F32), s.ctx, weight(4, 0))
    save(s.r1, o.r1)
    norm(s.nc, lambda b, rows: s.r1[rows, :], 1, 5)
    save(s.nc, o.nc)
    project(s.cq, s.nc, weight(5, 1), every_row)
    save(s.cq, o.cq)
    text_copy.wait()
    text_rows = pl.ds(0, TEXT_LEN)
    project(s.ck, s.text, weight(6, 2), text_rows)
    project(s.cv, s.text, weight(7, 0), text_rows)
    save(s.ck, o.ck)
    save(s.cv, o.cv)
    for g in range(4):
        attend_group(
            g,
            s.cq,
            s.ck,
            s.cv,
            s.cbias,
            s.stacked,
            s.scores,
            s.total,
            s.cctx,
            s.clse,
            lambda: None,
        )
        comm.work(0.6)
    save(s.cctx, o.cctx)
    save(s.clse, o.clse)
    add_project(s.r2, lambda cut: s.r1[:, cut], s.cctx, weight(8, 1))
    save(s.r2, o.r2)
    norm(s.nf, lambda b, rows: s.r2[rows, :], 2, 5)
    cot_copy.wait()
    act, slope, nf, cot = s.act, s.slope, s.nf, s.cot
    save(nf, o.nf)
    grads = []

    def gradient(dst, left, right):
        m = len(grads)
        if m >= 2:
            grads[m - 2].wait()
        stage = s.stage.at[m % 2]

        def one(n, cut):
            stage[:, cut] = dot_tn(left(), right(cut)).astype(BF16)

        tiles(4, 256)(one)
        copy = pltpu.make_async_copy(stage, dst, s.grad.at[m])
        copy.start()
        grads.append(copy)

    for j in range(4):
        w = weight(9 + j, j % 3)

        def one(n, cut):
            h = dot_nn(nf[...], w[:, cut])
            below = 0.5 * (1.0 + lax.erf(h * 0.7071067811865476))
            act[j, :, cut] = (h * below).astype(BF16)
            slope[j * 320 : (j + 1) * 320, cut] = (
                below + h * jnp.exp(-0.5 * h * h) * 0.3989422804014327
            ).astype(BF16)

        one(0, pl.ds(0, 512))
        comm.work(1.75)
        one(1, pl.ds(512, 512))
        comm.work(1.75)
        gradient(o.ddown.at[j], lambda: act[j], lambda cut: cot[:, cut])
        comm.work(2.0)
    save(slope, o.slope)
    for copy in saves:
        copy.wait()
    for j in range(4):
        w = weight(13 + j, j % 3)

        def onward(n, cut):
            total = s.r2[:, cut] + dot_nn(act[j], w[:, cut])
            if j < 3:
                s.r2[:, cut] = total
            else:
                s.out[:, cut] = total.astype(BF16)

        tiles(4, 256)(onward)
    copy = pltpu.make_async_copy(s.out, o.out, s.save.at[len(saves)])
    copy.start()
    copy.wait()
    for copy in grads[-2:]:
        copy.wait()
    for copy in comm.sent:
        copy.wait_send()


def pallas(kernel, args, shapes, scratch, apart, params):
    def named(*refs):
        a, b = len(args), len(args) + len(shapes)
        kernel(
            types.SimpleNamespace(**dict(zip(args, refs[:a]))),
            types.SimpleNamespace(**dict(zip(shapes, refs[a:b]))),
            types.SimpleNamespace(**dict(zip(scratch, refs[b:]))),
        )

    outs = pl.pallas_call(
        named,
        out_shape=list(shapes.values()),
        in_specs=[pl.BlockSpec(memory_space=apart.get(n, pl.ANY)) for n in args],
        out_specs=[pl.BlockSpec(memory_space=pl.ANY)] * len(shapes),
        scratch_shapes=list(scratch.values()),
        compiler_params=pltpu.CompilerParams(
            has_side_effects=True, vmem_limit_bytes=VMEM_BYTES, **params
        ),
    )(*args.values())
    return dict(zip(shapes, outs))


def run_forward_kernel(args):
    S, V, D_SEM = jax.ShapeDtypeStruct, pltpu.VMEM, pltpu.SemaphoreType.DMA
    a = types.SimpleNamespace(**args)
    rows = (320, 1024)
    scratch = dict(
        send=D_SEM((18, 12)), recv=D_SEM((18, 12)), own=D_SEM((21,)), save=D_SEM((24,)), load=D_SEM((17,)), grad=D_SEM((4,)),
        frames=V((2, 2, 320, 1024), BF16), cot=V(rows, BF16), text=V((64, 1024), BF16), norms=V((1024, 128), BF16), gb=V((8, 1024), F32),
        bias=V((1280, 1280), BF16), cbias=V((64, 1280), BF16), w=V((3, 1024, 1024), BF16), normed=V((1280, 1024), BF16),
        q=V(rows, BF16), k=V((1280, 1024), BF16), v=V((1280, 1024), BF16), stacked=V((1280, 256), BF16), scores=V((1280, 1280), F32),
        total=V((256, 1280), F32), ctx=V(rows, BF16), lse=V((4, 1280), F32), r1=V(rows, F32), nc=V(rows, BF16), cq=V(rows, BF16),
        ck=V((64, 1024), BF16), cv=V((64, 1024), BF16), cctx=V(rows, BF16), clse=V((4, 1280), F32), r2=V(rows, F32), nf=V(rows, BF16),
        act=V((4, 320, 1024), BF16), slope=V((1280, 1024), BF16), out=V(rows, BF16), nin=V((32, 128), BF16), flat=V((128, 128), F32),
        upraw=V((32, 4096), BF16), upin=V((32, 4096), BF16), stage=V((2, 1024, 1024), BF16),
    )
    m = types.SimpleNamespace(**scratch)
    shapes = dict(norms=m.nin, sqkv=a.sqkv, sout=a.sout, cqkv=a.cqkv, cout=a.cout, up=a.up, down=a.down)
    shapes = {n: S((4, 2, 2, 2) + v.shape, BF16) for n, v in shapes.items()}
    saved = dict(
        gb=m.gb, frames=m.frames, normed=m.normed, q=m.q, k=m.k, v=m.v, ctx=m.ctx, lse=m.lse, r1=m.r1, nc=m.nc, cq=m.cq, ck=m.ck,
        cv=m.cv, cctx=m.cctx, clse=m.clse, r2=m.r2, out=m.out, nf=m.nf, slope=m.slope,
    )
    shapes.update({n: S(v.shape, v.dtype) for n, v in saved.items()})
    shapes.update(ddown=S((4, 1024, 1024), BF16))
    apart = dict(seg=pltpu.VMEM, gain=pltpu.VMEM, shift=pltpu.VMEM, text_len=pltpu.SMEM)
    return pallas(forward_kernel, args, shapes, scratch, apart, dict(collective_id=0))


def attend_back_group(group, q, k, v, up, context, bias, logsum, stacked_q, stacked_g, total, grad_q, between):
    rows, keys = q.shape[0], k.shape[0]
    size = min(BLOCK, keys)
    cols = slice(group * 256, group * 256 + 256)
    stack_heads(stacked_q, q, group, HEAD_DIM**-0.5)
    stack_heads(stacked_g, up, group, 1.0)
    four = jnp.concatenate([context[:, cols].astype(F32)] * 4, axis=0)
    inner = lax.dot_general(
        jnp.ones((8, 256), F32),
        stacked_g[...].astype(F32) * four,
        (((1,), (1,)), ((), ())),
        precision=lax.Precision.HIGHEST,
        preferred_element_type=F32,
    )[:1]
    shift = logsum[group : group + 1, :]
    total[...] = jnp.zeros_like(total)

    def step(i, carry):
        at = pl.ds(pl.multiple_of(i * size, size), size)
        key, value = k[at, cols], v[at, cols]
        half = bias[at, :].astype(F32)
        s = dot_nt(key, stacked_q[...]) + jnp.concatenate([half, half], axis=1)
        p = jnp.exp(s - shift)
        ds = (p * (dot_nt(value, stacked_g[...]) - inner)).astype(BF16)
        v[at, cols] = dot_nn(p.astype(BF16), stacked_g[...]).astype(BF16)
        k[at, cols] = dot_nn(ds, stacked_q[...]).astype(BF16)
        total[...] += dot_tn(key, ds)
        return carry

    count = keys // size
    if count == 1:
        step(0, 0)
        between()
    else:
        for start in range(0, count, 2):
            lax.fori_loop(start, min(start + 2, count), step, 0)
            between()
    grad_q[:, cols] = (unstack_heads(total[...], rows) * HEAD_DIM**-0.5).astype(BF16)


DOWN_UNITS = (1, 3, 0, 2)
WIDE = {1: (8, 9), 3: (10, 11)}


class Scattering:
    def __init__(self, at, i, o, s, n, last, wide, over_y):
        self.at, self.o, self.s, self.n, self.last = at, o, s, n, last
        self.wide, self.over_y = wide, over_y
        self.begun, self.done1, self.step = 0, 0, 0
        self.fresh, self.queue2, self.queue3, self.finished, self.odd = [], [], [], [], False
        self.sent, self.source, self.since = {}, {}, 0.0
        z, y, x, c = at
        self.to_x, self.to_y, self.to_c = device(z, y, 1 - x, c), device(z, 1 - y, x, c), device(z, y, x, 1 - c)

    def copy(self, src, dst, u, k, dev):
        return pltpu.make_async_remote_copy(
            src_ref=src,
            dst_ref=dst,
            send_sem=self.s.send.at[u, k],
            recv_sem=self.s.recv.at[u, k],
            device_id=dev,
            device_id_type=MESH,
        )

    def go(self, u, k, copy):
        copy.start()
        self.sent[u, k] = copy

    def left(self, u, k):
        copy = self.sent.pop((u, k), None)
        if copy is not None:
            copy.wait_send()

    def buffer(self, main, last, u, slots=16):
        return last if u == self.last else main.at[u % slots]

    def total(self, u):
        if u in self.wide:
            m = list(self.wide).index(u)
            return self.s.big.at[m * 512 : m * 512 + 512].reshape(4, 2, 2, 32, 1024)
        return self.buffer(self.s.sum, self.s.nsum, u, 4)

    def xr(self, u):
        return self.buffer(self.s.xy, self.s.nxy, u).at[0 : self.cut(u)]

    def yr(self, u):
        return self.buffer(self.s.xy, self.s.nxy, u).at[self.cut(u) : 4]

    def cc(self, u):
        return self.buffer(self.s.cc, self.s.ncc, u)

    def from_core(self, u):
        src = self.source[u].at[:, :, :, 1 - self.at[3]]
        return self.copy(src, self.buffer(self.s.core, self.s.ncore, u, 4), u, 0, self.to_c)

    def cut(self, u):
        return 1 if u in self.over_y else 2

    def first_x(self, u):
        n = self.cut(u)
        return self.copy(self.total(u).at[0:n, :, 1 - self.at[2]], self.xr(u), u, 1, self.to_x)

    def first_y(self, u):
        n = self.cut(u)
        return self.copy(self.total(u).at[n:4, 1 - self.at[1]], self.yr(u), u, 2, self.to_y)

    def second_y(self, u):
        n = self.cut(u)
        return self.copy(self.xr(u).at[:, 1 - self.at[1]], self.cc(u).at[0:n], u, 3, self.to_y)

    def second_x(self, u):
        n = self.cut(u)
        return self.copy(self.yr(u).at[:, 1 - self.at[2]], self.cc(u).at[n:4], u, 4, self.to_x)

    def final(self, u):
        return self.o.nfin if u == self.last else self.o.fin.at[u]

    def across(self, u, k):
        z, y, x, c = self.at
        to = lax.rem(z + k, 4)
        return self.copy(self.cc(u).at[to], self.final(u).at[k - 1], u, 4 + k, device(to, y, x, c))

    def keep(self, u):
        return pltpu.make_async_copy(self.cc(u).at[self.at[0]], self.final(u).at[3], self.s.keep.at[u])

    def load(self, u):
        return pltpu.make_async_copy(self.source[u].at[:, :, :, self.at[3]], self.total(u), self.s.own.at[u])

    def begin(self, u, source, in_hbm):
        while self.done1 < u - 3:
            self.pump()
        self.begun += 1
        self.source[u] = source
        if 4 <= u < self.last:
            pl.semaphore_wait(self.s.free, 1)
        if in_hbm:
            self.load(u).start()
        self.go(u, 0, self.from_core(u))

    def work(self, us):
        self.since += us
        if self.since >= PACE_BACKWARD:
            self.pump()

    def pump(self):
        self.since = 0.0
        self.odd = not self.odd
        if self.odd:
            self.queue2 += self.fresh
            self.fresh = []
            if self.done1 < self.begun:
                new = self.done1
                self.done1 += 1
                self.stage1(new)
                if new not in self.wide:
                    self.fresh = [new]
            return
        seconds, self.queue2 = self.queue2[:1], self.queue2[1:]
        thirds, self.queue3 = self.queue3[:1], self.queue3[1:] + seconds
        for u in seconds:
            self.stage2(u)
        for u in thirds:
            self.stage3(u)
        for u, steps in self.wide.items():
            for stage in range(2):
                if steps[stage] == self.step:
                    (self.wide_plane, self.wide_last)[stage](u)
                    self.finished.append((u, stage))
        self.step += 1

    def stage1(self, u):
        z, y, x, c = self.at
        total, got, source = self.total(u), self.buffer(self.s.core, self.s.ncore, u, 4), self.source[u]
        in_hbm = u < 4
        if in_hbm:
            self.load(u).wait()
        else:
            self.left(u - 4, 1)
            self.left(u - 4, 2)
        self.from_core(u).wait_recv()

        def add(j, carry):
            at = (j // 4, lax.rem(j // 2, 2), lax.rem(j, 2))
            own = total[at] if in_hbm else source[at + (c,)]
            total[at] = own + got[at]
            return carry

        lax.fori_loop(0, 16, add, 0)
        if u + 4 < self.last:
            pl.semaphore_signal(self.s.free, inc=1, device_id=self.to_c, device_id_type=MESH)
        if u in self.wide:
            for k in (1, 2, 3):
                self.go(u, 4 + k, self.wide_across(u, k))
            return
        if self.cut(u):
            self.go(u, 1, self.first_x(u))
        self.go(u, 2, self.first_y(u))

    def stage2(self, u):
        z, y, x, c = self.at
        total, yr, n = self.total(u), self.yr(u), self.cut(u)
        if n:
            xr = self.xr(u)
            self.first_x(u).wait_recv()

            def add_x(j, carry):
                a, b = j // 2, lax.rem(j, 2)
                xr[a, b] = xr[a, b] + total[a, b, x]
                return carry

            lax.fori_loop(0, 2 * n, add_x, 0)
            self.go(u, 3, self.second_y(u))
        self.first_y(u).wait_recv()

        def add_y(j, carry):
            a, b = j // 2, lax.rem(j, 2)
            yr[a, b] = yr[a, b] + total[n + a, y, b]
            return carry

        lax.fori_loop(0, 8 - 2 * n, add_y, 0)
        self.go(u, 4, self.second_x(u))

    def stage3(self, u):
        z, y, x, c = self.at
        yr, cc, n = self.yr(u), self.cc(u), self.cut(u)
        if n:
            xr = self.xr(u)
            self.second_y(u).wait_recv()
            for a in range(n):
                cc[a] = cc[a] + xr[a, y]
        self.second_x(u).wait_recv()
        for a in range(4 - n):
            cc[n + a] = cc[n + a] + yr[a, x]
        for k in (1, 2, 3):
            self.go(u, 4 + k, self.across(u, k))
        self.keep(u).start()

    def wide_got(self, u, k):
        m = list(self.wide).index(u)
        at = 1024 + (m * 3 + k - 1) * 128
        return self.s.big.at[at : at + 128].reshape(2, 2, 32, 1024)

    def wide_across(self, u, k):
        z, y, x, c = self.at
        to = lax.rem(z + k, 4)
        return self.copy(self.total(u).at[to], self.wide_got(u, k), u, 4 + k, device(to, y, x, c))

    def wide_copy(self, u, which):
        z, y, x, c = self.at
        m, total = list(self.wide).index(u), self.total(u)
        xw, yw, top, low = self.s.xw.at[m], self.s.yw.at[m], pl.ds(0, 16), pl.ds(16, 16)
        if which == 0:
            return self.copy(total.at[z, :, 1 - x, top], xw, u, 1, self.to_x)
        if which == 1:
            return self.copy(total.at[z, 1 - y, :, low], yw, u, 2, self.to_y)
        if which == 2:
            return self.copy(xw.at[1 - y], self.o.fin.at[u, 1, top], u, 3, self.to_y)
        if which == 3:
            return self.copy(yw.at[1 - x], self.o.fin.at[u, 1, low], u, 4, self.to_x)
        if which == 4:
            return pltpu.make_async_copy(xw.at[y], self.o.fin.at[u, 0, top], self.s.keep.at[u])
        return pltpu.make_async_copy(yw.at[x], self.o.fin.at[u, 0, low], self.s.own.at[4 + m])

    def wide_plane(self, u):
        z, y, x, c = self.at
        total, got = self.total(u), [self.wide_got(u, k) for k in (1, 2, 3)]
        for k in (1, 2, 3):
            self.wide_across(u, k).wait_recv()

        def add(j, carry):
            a, b = j // 2, lax.rem(j, 2)
            own = total[z, a, b].astype(F32) + got[0][a, b].astype(F32)
            more = got[1][a, b].astype(F32) + got[2][a, b].astype(F32)
            total[z, a, b] = (own + more).astype(BF16)
            return carry

        lax.fori_loop(0, 4, add, 0)
        self.go(u, 1, self.wide_copy(u, 0))
        self.go(u, 2, self.wide_copy(u, 1))

    def wide_last(self, u):
        z, y, x, c = self.at
        m, total = list(self.wide).index(u), self.total(u)
        xw, yw = self.s.xw.at[m], self.s.yw.at[m]
        self.wide_copy(u, 0).wait_recv()
        for a in range(2):
            xw[a] = xw[a] + total[z, a, x, 0:16]
        self.go(u, 3, self.wide_copy(u, 2))
        self.wide_copy(u, 4).start()
        self.wide_copy(u, 1).wait_recv()
        for a in range(2):
            yw[a] = yw[a] + total[z, y, a, 16:32]
        self.go(u, 4, self.wide_copy(u, 3))
        self.wide_copy(u, 5).start()

    def settle(self):
        while len(self.finished) < 2 * len(self.wide):
            self.pump()
        for u in self.wide:
            for k in (1, 2, 5, 6, 7):
                self.left(u, k)

    def finish(self):
        while self.fresh or self.queue2 or self.queue3 or self.done1 < self.begun:
            self.pump()
        for u in range(self.n):
            if u in self.wide:
                for which in (2, 3):
                    self.wide_copy(u, which).wait_recv()
                for which in (4, 5):
                    self.wide_copy(u, which).wait()
                continue
            for k in (1, 2, 3):
                self.across(u, k).wait_recv()
            self.keep(u).wait()
        for key in list(self.sent):
            self.left(*key)


def backward_kernel(i, o, s):
    at = place()
    z, y, x, c = at
    seq = x * 2 + c
    comm = Scattering(at, i, o, s, 17, 16, WIDE, (14, 15))
    greet(*at)
    six = (4, 2, 2, 2, 32, 1024)
    for u in range(4):
        comm.begin(u, i.ddown.at[DOWN_UNITS.index(u)], True)
    waits = {}

    def fetch(src, dst, slot):
        copy = pltpu.make_async_copy(src, dst, s.fetch.at[slot])
        copy.start()
        waits[slot] = copy

    def have(*slots):
        for slot in slots:
            waits.pop(slot).wait()

    def block(full, k):
        return full.at[:, :, :, :, :, pl.ds(k * 1024, 1024)]

    stream = []
    for j in range(4):
        stream += [i.down.at[:, :, :, :, j], block(i.up, j)]
    stream += [block(i.cout, 0), block(i.cqkv, 1), block(i.cqkv, 2), block(i.cqkv, 0), block(i.sout, 0)]
    stream += [block(i.sqkv, k) for k in range(3)]

    def weight(n):
        dst = s.w.at[n % 3]
        return pltpu.make_async_copy(stream[n], dst.reshape(*six), s.load.at[n % 3])

    def loaded(n):
        weight(n).wait()
        return s.w.at[n % 3]

    def used(n):
        if n + 3 < len(stream):
            weight(n + 3).start()

    for n in range(3):
        weight(n).start()
    fetch(i.cot, s.cot, 3)
    fetch(i.slope, s.k, 11)
    fetch(i.nf, s.up, 5)
    fetch(i.gb, s.gb, 0)
    fetch(i.r2, s.r, 1)
    fetch(i.cctx, s.ctx, 4)
    fetch(i.ck, s.ck, 6)
    fetch(i.cv, s.cv, 7)
    fetch(i.clse, s.clse, 8)
    fetch(i.nc, s.nc, 9)
    fetch(i.text, s.text, 10)
    fetch(i.v, s.v, 12)
    fetch(i.lse, s.lse, 13)
    fetch(i.normed, s.normed, 14)
    comm.pump()
    comm.pump()
    set_masks(i, seq, s.bias, s.cbias, 2)
    s.ng[...] = jnp.zeros_like(s.ng)
    have(0)

    def norm_back(values, upstream, k, put):
        gain = s.gb[k : k + 1, :]
        center = values - jnp.mean(values, axis=-1, keepdims=True)
        scale = lax.rsqrt(jnp.mean(center * center, axis=-1, keepdims=True) + 1e-05)
        hat = center * scale
        s.ng[k : k + 1, :] += jnp.sum(upstream * hat, axis=0, keepdims=True)
        s.ng[3 + k : 4 + k, :] += jnp.sum(upstream, axis=0, keepdims=True)
        if put is not None:
            h = upstream * gain
            put((h - jnp.mean(h, axis=-1, keepdims=True) - hat * jnp.mean(h * hat, axis=-1, keepdims=True)) * scale)

    def gradient(u, left, right, cost=2.2):
        while u > 5 and comm.done1 < u - 1:
            comm.pump()
        comm.left(u - 2, 0)
        dw = s.dw.at[u % 2]

        def one(n, cut):
            dw[:, cut] = dot_tn(left(), right(cut)).astype(BF16)

        tiles(4, 256)(one)
        comm.begin(u, dw.reshape(*six), False)
        comm.work(cost)

    gr, branch, g = s.gr, s.branch, s.g
    for j in range(4):
        w, w_up = loaded(2 * j), None
        if j == 0:
            have(3, 5, 11)

        def back(n, rows):
            slope = s.k[j * 320 : (j + 1) * 320, rows].astype(F32)
            branch[:, rows] = (dot_nt(s.cot[...], w[rows, :]) * slope).astype(BF16)

        tiles(4, 256)(back)
        used(2 * j)
        comm.work(1.6)
        gradient(4 + j, lambda: s.up[...], lambda cut: branch[:, cut])
        w_up = loaded(2 * j + 1)

        def onward(n, rows):
            more = dot_nt(branch[...], w_up[rows, :])
            g[:, rows] = more if j == 0 else g[:, rows] + more

        tiles(4, 256)(onward)
        used(2 * j + 1)
        comm.work(1.6)
    fetch(i.k, s.k, 11)
    fetch(i.cq, s.q, 5)
    have(1)

    def back_two(b, rows):
        def put(grad):
            total = s.cot[rows, :].astype(F32) + grad
            gr[rows, :] = total
            branch[rows, :] = total.astype(BF16)

        norm_back(s.r[rows, :], g[rows, :], 2, put)

    tiles(5, 64)(back_two)
    fetch(i.r1, s.r, 1)
    comm.work(1.0)

    def through(dst, src, w):
        def one(n, rows):
            value = dot_nt(src[...], w[rows, :])
            dst[:, rows] = value.astype(dst.dtype)

        tiles(4, 256)(one)

    through(s.up, branch, loaded(8))
    used(8)
    comm.work(1.6)
    have(4)
    gradient(8, lambda: s.ctx[...], lambda cut: branch[:, cut])
    have(5, 6, 7, 8)
    for group in range(4):
        attend_back_group(
            group,
            s.q,
            s.ck,
            s.cv,
            s.up,
            s.ctx,
            s.cbias,
            s.clse,
            s.stacked_q,
            s.stacked_g,
            s.total,
            s.dq,
            lambda: comm.work(1.8),
        )
    fetch(i.q, s.q, 5)
    fetch(i.ctx, s.ctx, 4)
    have(9, 10)
    gradient(9, lambda: s.nc[...], lambda cut: s.dq[:, cut])
    w_key, w_value = loaded(9), loaded(10)

    def text_part(n, rows):
        value = dot_nt(s.ck[...], w_key[rows, :]) + dot_nt(s.cv[...], w_value[rows, :])
        s.tpart[:, :, :, rows] = value.astype(BF16).reshape(2, 2, 16, 256)

    tiles(4, 256)(text_part)
    used(9)
    used(10)
    text_core = comm.copy(s.tpart.at[:, 1 - c], s.tcore, 17, 0, comm.to_c)
    comm.go(17, 0, text_core)
    comm.work(0.8)
    through(g, s.dq, loaded(11))
    used(11)
    comm.work(1.6)
    have(1)

    def back_one(b, rows):
        def put(grad):
            total = gr[rows, :] + grad
            gr[rows, :] = total
            branch[rows, :] = total.astype(BF16)

        norm_back(s.r[rows, :], g[rows, :], 1, put)

    tiles(5, 64)(back_one)
    comm.work(1.0)
    save_gr = pltpu.make_async_copy(gr, o.gr, s.fetch.at[16])
    save_gr.start()
    gradient(10, lambda: s.text[...], lambda cut: s.ck[:, cut])
    through(s.up, branch, loaded(12))
    used(12)
    comm.work(1.6)
    text_core.wait_recv()
    s.tsum[...] = s.tpart[:, c] + s.tcore[...]
    text_x = comm.copy(s.tsum.at[1 - x], o.tmine.at[1], 17, 1, comm.to_x)
    comm.go(17, 1, text_x)
    text_keep = pltpu.make_async_copy(s.tsum.at[x], o.tmine.at[0], s.keep.at[17])
    text_keep.start()
    have(4, 5, 11, 12, 13)
    todo = [
        lambda: gradient(11, lambda: s.text[...], lambda cut: s.cv[:, cut]),
        lambda: gradient(12, lambda: s.ctx[...], lambda cut: branch[:, cut]),
    ]
    for group in range(4):
        attend_back_group(
            group,
            s.q,
            s.k,
            s.v,
            s.up,
            s.ctx,
            s.bias,
            s.lse,
            s.stacked_q,
            s.stacked_g,
            s.total,
            s.dq,
            lambda: comm.work(2.6),
        )
        if group < len(todo):
            todo[group]()
    have(14)
    mine = pl.ds(pl.multiple_of(seq * 320, 64), 320)
    wq, wk, wv = loaded(13), loaded(14), loaded(15)
    comm.settle()
    fpart = s.big.at[0:1280].reshape(2, 2, 320, 1024)

    def frames_part(b, rows):
        block = pltpu.make_async_copy(i.frames.at[b // 2, b % 2], s.cot, s.fetch.at[15])
        block.start()

        def one(n, cut):
            g[:, cut] = dot_nt(s.k[rows, :], wk[cut, :]) + dot_nt(s.v[rows, :], wv[cut, :])

        tiles(4, 256)(one)

        @pl.when(b == seq)
        def _():
            def two(n, cut):
                g[:, cut] = g[:, cut] + dot_nt(s.dq[...], wq[cut, :])

            tiles(4, 256)(two)

        block.wait()

        def three(r, part):
            norm_back(s.cot[part, :].astype(F32), g[part, :], 0, None)
            fpart[b // 2, b % 2, part, :] = g[part, :].astype(BF16)

        tiles(5, 64)(three)

    gradient(13, lambda: s.normed[mine, :], lambda cut: s.dq[:, cut])
    for part_of in range(4):
        frames_part(part_of, pl.ds(part_of * 320, 320))
        comm.work(3.8)
    frames_core = comm.copy(fpart.at[:, 1 - c], s.fcore, 17, 2, comm.to_c)
    comm.go(17, 2, frames_core)
    flat = jnp.concatenate([s.ng[...], jnp.zeros((120, 1024), F32)], axis=0).T
    s.nown[...] = flat.reshape(4, 2, 2, 2, 32, 128)
    comm.source[16] = s.nown
    comm.go(16, 0, comm.from_core(16))
    gradient(14, lambda: s.normed[...], lambda cut: s.k[:, cut], 4.0)
    frames_core.wait_recv()

    def frames_sum(b, carry):
        rows = pl.ds(pl.multiple_of(lax.rem(b, 5) * 64, 64), 64)
        s.fcore[b // 5, rows] = s.fcore[b // 5, rows] + fpart[b // 5, c, rows]
        return carry

    lax.fori_loop(0, 10, frames_sum, 0)
    frames_x = comm.copy(s.fcore.at[1 - x], o.fmine.at[1], 17, 3, comm.to_x)
    comm.go(17, 3, frames_x)
    frames_keep = pltpu.make_async_copy(s.fcore.at[x], o.fmine.at[0], s.keep.at[18])
    frames_keep.start()
    comm.stage1(16)
    gradient(15, lambda: s.normed[...], lambda cut: s.v[:, cut], 4.0)
    comm.stage2(16)
    comm.pump()
    comm.stage3(16)
    comm.finish()
    text_x.wait_recv()
    frames_x.wait_recv()
    text_keep.wait()
    frames_keep.wait()
    save_gr.wait()


def run_backward_kernel(args):
    S, V, D_SEM = jax.ShapeDtypeStruct, pltpu.VMEM, pltpu.SemaphoreType.DMA
    rows, block = (320, 1024), (32, 1024)
    shapes = dict(
        fin=S((16, 4) + block, BF16), nfin=S((4, 32, 128), F32), fmine=S((2,) + rows, BF16), tmine=S((2, 16, 1024), BF16), gr=S(rows, F32)
    )
    scratch = dict(
        send=D_SEM((18, 8)), recv=D_SEM((18, 8)), own=D_SEM((6,)), keep=D_SEM((19,)), fetch=D_SEM((17,)), load=D_SEM((3,)),
        free=pltpu.SemaphoreType.REGULAR,
        sum=V((4, 4, 2, 2) + block, BF16), core=V((4, 4, 2, 2) + block, BF16), xy=V((16, 4, 2) + block, BF16), cc=V((16, 4) + block, BF16), xw=V((2, 2, 16, 1024), BF16), yw=V((2, 2, 16, 1024), BF16),
        big=V((1792, 1024), BF16),
        nsum=V((4, 2, 2, 32, 128), F32), ncore=V((4, 2, 2, 32, 128), F32), nxy=V((4, 2, 32, 128), F32),
        ncc=V((4, 32, 128), F32), nown=V((4, 2, 2, 2, 32, 128), F32),
        gb=V((8, 1024), F32), r=V(rows, F32), g=V(rows, F32), cot=V(rows, BF16), ctx=V(rows, BF16), q=V(rows, BF16),
        ck=V((64, 1024), BF16), cv=V((64, 1024), BF16), clse=V((4, 1280), F32), nc=V(rows, BF16), text=V((64, 1024), BF16),
        k=V((1280, 1024), BF16), v=V((1280, 1024), BF16), lse=V((4, 1280), F32), normed=V((1280, 1024), BF16), w=V((3, 1024, 1024), BF16),
        bias=V((1280, 640), BF16), cbias=V((64, 640), BF16), ng=V((8, 1024), F32), gr=V(rows, F32), branch=V(rows, BF16),
        up=V(rows, BF16), dq=V(rows, BF16), stacked_q=V((1280, 256), BF16), stacked_g=V((1280, 256), BF16),
        total=V((256, 1280), F32), dw=V((2, 1024, 1024), BF16), tpart=V((2, 2, 16, 1024), BF16), tcore=V((2, 16, 1024), BF16),
        tsum=V((2, 16, 1024), BF16), fcore=V((2,) + rows, BF16),
    )
    apart = dict(seg=pltpu.VMEM, text_len=pltpu.SMEM)
    return pallas(backward_kernel, args, shapes, scratch, apart, dict(collective_id=1))


def finish_kernel(i, o, s):
    coming = []

    def fetch(src, dst):
        copy = pltpu.make_async_copy(src, dst, s.fetch.at[len(coming)])
        copy.start()
        coming.append(copy)
        return copy

    fetch(i.out, s.out)
    fetch(i.frames, s.frames)
    fetch(i.gr, s.gr)
    fetch(i.fmine, s.fmine)
    parts = [fetch(i.fin.at[u, 0 : 2 if u in WIDE else 4], s.fin.at[u, 0 : 2 if u in WIDE else 4]) for u in range(16)]
    going = []

    def put(src, dst):
        copy = pltpu.make_async_copy(src, dst, s.put.at[len(going)])
        copy.start()
        going.append(copy)

    coming[0].wait()
    put(s.out, o.out)
    for copy in coming[1:4]:
        copy.wait()
    gain = i.gb[0:1, :]

    def rows_of(b, rows):
        values = s.frames[rows, :].astype(F32)
        center = values - jnp.mean(values, axis=-1, keepdims=True)
        scale = lax.rsqrt(jnp.mean(center * center, axis=-1, keepdims=True) + 1e-05)
        hat = center * scale
        h = (s.fmine[0, rows, :].astype(F32) + s.fmine[1, rows, :].astype(F32)) * gain
        back = (h - jnp.mean(h, axis=-1, keepdims=True) - hat * jnp.mean(h * hat, axis=-1, keepdims=True)) * scale
        s.frames[rows, :] = (s.gr[rows, :] + back).astype(BF16)

    tiles(5, 64)(rows_of)
    put(s.frames, o.frames)

    def total(u):
        parts[u].wait()
        terms = [s.fin[u, k].astype(F32) for k in range(2 if u in WIDE else 4)]
        return sum(terms[1:], terms[0])

    for k in range(4):
        s.down[k * 32 : (k + 1) * 32, :] = total(DOWN_UNITS[k])
    put(s.down, o.down)
    for j in range(4):
        s.upraw[:, j * 1024 : (j + 1) * 1024] = total(4 + j)

    def put_up(b, block):
        s.up[:, b * 128 : b * 128 + 128] = block

    shuffle_columns(lambda b: s.upraw[:, b * 128 : b * 128 + 128], put_up, True)
    put(s.up, o.up)
    for src, dst, first, count in (
        (s.cout, o.cout, 8, 1),
        (s.cqkv, o.cqkv, 9, 3),
        (s.sout, o.sout, 12, 1),
        (s.sqkv, o.sqkv, 13, 3),
    ):
        for k in range(count):
            src[:, k * 1024 : (k + 1) * 1024] = total(first + k)
        put(src, dst)
    n = ((i.nfin[0] + i.nfin[1]) + (i.nfin[2] + i.nfin[3])).T
    s.gain[...] = n[:3]
    s.shift[...] = n[3:6]
    s.text[...] = (i.tmine[0].astype(F32) + i.tmine[1].astype(F32)).astype(BF16)
    put(s.gain, o.gain)
    put(s.shift, o.shift)
    put(s.text, o.text)
    for copy in going:
        copy.wait()


def run_finish_kernel(args):
    S, V, D_SEM = jax.ShapeDtypeStruct, pltpu.VMEM, pltpu.SemaphoreType.DMA
    rows = (320, 1024)
    shapes = dict(
        out=S(rows, BF16), frames=S(rows, BF16), text=S((16, 1024), BF16), gain=S((3, 32), F32), shift=S((3, 32), F32),
        sqkv=S((32, 3072), F32), sout=S((32, 1024), F32), cqkv=S((32, 3072), F32), cout=S((32, 1024), F32), up=S((32, 4096), F32),
        down=S((128, 1024), F32),
    )
    scratch = {n: V(v.shape, v.dtype) for n, v in shapes.items()}
    scratch.update(
        fin=V((16, 4, 32, 1024), BF16), fmine=V((2,) + rows, BF16), gr=V(rows, F32), upraw=V((32, 4096), F32), fetch=D_SEM((20,)),
        put=D_SEM((11,)),
    )
    apart = dict(nfin=pltpu.VMEM, tmine=pltpu.VMEM, gb=pltpu.VMEM)
    return pallas(finish_kernel, args, shapes, scratch, apart, dict())


def fetch_all(norm_gain, norm_bias, self_qkv, self_out, cross_qkv, cross_out, ffn_up, ffn_down):
    first = (
        lax.all_gather(norm_gain, ("dp", "seq"), axis=0, tiled=True),
        lax.all_gather(norm_bias, ("dp", "seq"), axis=0, tiled=True),
        lax.all_gather(self_qkv, ("dp", "seq"), axis=0, tiled=True),
        lax.all_gather(self_out, ("dp", "seq"), axis=0, tiled=True),
    )
    second = (
        lax.all_gather(cross_qkv, ("dp", "seq"), axis=0, tiled=True),
        lax.all_gather(cross_out, ("dp", "seq"), axis=0, tiled=True),
    )
    third = (
        lax.all_gather(ffn_up, ("dp", "seq"), axis=0, tiled=True),
        lax.all_gather(ffn_down, ("dp", "seq"), axis=0, tiled=True),
    )
    return tuple(first) + tuple(second) + tuple(third)


def run_forward(frames, local_seg, frame_seg, text_seg, text_states, offset, weights):
    norm_gain, norm_bias, self_qkv, self_out, cross_qkv, cross_out, ffn_up, ffn_down = weights
    gains = norm_gain.astype(jnp.float32)
    biases = norm_bias.astype(jnp.float32)
    inputs = frames.astype(jnp.float32)
    normed_self = layer_norm(inputs, gains[:, 0], biases[:, 0]).astype(jnp.bfloat16)
    queries = jnp.dot(normed_self, self_qkv[:, :D], preferred_element_type=jnp.float32).astype(
        jnp.bfloat16
    )
    pair_weights = self_qkv[:, D:].reshape(D, 2, D)
    key_value = jnp.einsum(
        "rcd,dje->jrce", normed_self, pair_weights, preferred_element_type=jnp.float32
    ).astype(jnp.bfloat16)
    gathered = lax.all_gather(key_value, "seq", axis=2, tiled=True)
    self_context, self_logsum = lax.map(
        lambda record: attend(
            record[0], record[1], record[2], self_allowed(record[3], record[4], offset)
        ),
        (queries, gathered[0], gathered[1], local_seg, frame_seg),
    )
    self_context = self_context.astype(jnp.bfloat16)
    resid_one = inputs + jnp.dot(self_context, self_out, preferred_element_type=jnp.float32)
    normed_cross = layer_norm(resid_one, gains[:, 1], biases[:, 1]).astype(jnp.bfloat16)
    cross_queries = jnp.dot(
        normed_cross, cross_qkv[:, :D], preferred_element_type=jnp.float32
    ).astype(jnp.bfloat16)
    text_weights = cross_qkv[:, D:].reshape(D, 2, D)
    text_pair = jnp.einsum(
        "rtd,dje->jrte", text_states, text_weights, preferred_element_type=jnp.float32
    ).astype(jnp.bfloat16)
    cross_context, cross_logsum = lax.map(
        lambda record: attend(
            record[0], record[1], record[2], record[3][:, None] == record[4][None, :]
        ),
        (cross_queries, text_pair[0], text_pair[1], local_seg, text_seg),
    )
    cross_context = cross_context.astype(jnp.bfloat16)
    resid_two = resid_one + jnp.dot(cross_context, cross_out, preferred_element_type=jnp.float32)
    normed_ffn = layer_norm(resid_two, gains[:, 2], biases[:, 2]).astype(jnp.bfloat16)
    hidden_pre = jnp.dot(normed_ffn, ffn_up, preferred_element_type=jnp.float32)
    activated = exact_gelu(hidden_pre).astype(jnp.bfloat16)
    outcome = resid_two + jnp.dot(activated, ffn_down, preferred_element_type=jnp.float32)
    saved = (
        inputs,
        normed_self,
        queries,
        gathered,
        self_context,
        self_logsum,
        resid_one,
        normed_cross,
        cross_queries,
        text_pair,
        cross_context,
        cross_logsum,
        resid_two,
        normed_ffn,
        hidden_pre,
        activated,
    )
    return (outcome, saved)


def generic_body(
    frames,
    frame_seg,
    text_states,
    text_len,
    norm_gain,
    norm_bias,
    self_qkv,
    self_out,
    cross_qkv,
    cross_out,
    ffn_up,
    ffn_down,
    cotangent,
):
    width = frames.shape[1]
    offset = lax.axis_index("seq") * width
    local_seg = lax.dynamic_slice_in_dim(frame_seg, offset, width, 1)
    text_seg = text_segments(text_len)
    shards = (norm_gain, norm_bias, self_qkv, self_out, cross_qkv, cross_out, ffn_up, ffn_down)
    weights = fetch_all(*shards)
    outcome, saved = run_forward(
        frames, local_seg, frame_seg, text_seg, text_states, offset, weights
    )
    frames_out = outcome.astype(jnp.bfloat16)
    (
        inputs,
        normed_self,
        queries,
        gathered,
        self_context,
        self_logsum,
        resid_one,
        normed_cross,
        cross_queries,
        text_pair,
        cross_context,
        cross_logsum,
        resid_two,
        normed_ffn,
        hidden_pre,
        activated,
    ) = saved
    gain_full, bias_full, self_full, self_proj, cross_full, cross_proj, up_full, down_full = weights
    gains = gain_full.astype(jnp.float32)
    biases = bias_full.astype(jnp.float32)
    upstream = cotangent.astype(jnp.float32)
    down_grad = jnp.einsum("rcf,rcd->fd", activated, cotangent, preferred_element_type=jnp.float32)
    grad_act = jnp.einsum("rcd,fd->rcf", cotangent, down_full, preferred_element_type=jnp.float32)
    unused_value, gelu_pull = jax.vjp(exact_gelu, hidden_pre)
    grad_pre = gelu_pull(grad_act)[0].astype(jnp.bfloat16)
    up_grad = jnp.einsum("rcd,rcf->df", normed_ffn, grad_pre, preferred_element_type=jnp.float32)
    grad_normed = jnp.einsum("rcf,df->rcd", grad_pre, up_full, preferred_element_type=jnp.float32)
    grad_back, gain_two, bias_two = norm_back(resid_two, gains[:, 2], biases[:, 2], grad_normed)
    grad_resid_two = upstream + grad_back
    ffn_shares = (
        lax.psum_scatter(up_grad, ("dp", "seq"), scatter_dimension=0, tiled=True),
        lax.psum_scatter(down_grad, ("dp", "seq"), scatter_dimension=0, tiled=True),
    )
    branch_two = grad_resid_two.astype(jnp.bfloat16)
    cross_out_grad = jnp.einsum(
        "rcd,rce->de", cross_context, branch_two, preferred_element_type=jnp.float32
    )
    grad_context = jnp.einsum(
        "rce,de->rcd", branch_two, cross_proj, preferred_element_type=jnp.float32
    ).astype(jnp.bfloat16)
    grad_cross_q, grad_cross_k, grad_cross_v = lax.map(
        lambda record: attend_back(
            record[0],
            record[1],
            record[2],
            record[3][:, None] == record[4][None, :],
            record[5],
            record[6],
        ),
        (
            cross_queries,
            text_pair[0],
            text_pair[1],
            local_seg,
            text_seg,
            cross_logsum,
            grad_context,
        ),
    )
    text_joined = jnp.transpose(jnp.concatenate([grad_cross_k, grad_cross_v], axis=2), (1, 0, 2))
    text_summed = lax.psum_scatter(
        text_joined.astype(jnp.bfloat16), "seq", scatter_dimension=0, tiled=True
    ).astype(jnp.float32)
    text_shares = jnp.transpose(text_summed, (1, 0, 2)).astype(jnp.bfloat16)
    share = text_shares.shape[1]
    text_part = lax.dynamic_slice_in_dim(text_states, lax.axis_index("seq") * share, share, 1)
    text_kv_grad = jnp.einsum(
        "rtd,rte->de", text_part, text_shares, preferred_element_type=jnp.float32
    )
    text_grad = jnp.einsum(
        "rte,de->rtd", text_shares, cross_full[:, D:], preferred_element_type=jnp.float32
    ).astype(jnp.bfloat16)
    grad_cross_q = grad_cross_q.astype(jnp.bfloat16)
    cross_q_grad = jnp.einsum(
        "rcd,rce->de", normed_cross, grad_cross_q, preferred_element_type=jnp.float32
    )
    cross_qkv_grad = jnp.concatenate([cross_q_grad, text_kv_grad], axis=1)
    grad_normed = jnp.einsum(
        "rce,de->rcd", grad_cross_q, cross_full[:, :D], preferred_element_type=jnp.float32
    )
    grad_back, gain_one, bias_one = norm_back(resid_one, gains[:, 1], biases[:, 1], grad_normed)
    grad_resid_one = grad_resid_two + grad_back
    cross_shares = (
        lax.psum_scatter(cross_qkv_grad, ("dp", "seq"), scatter_dimension=0, tiled=True),
        lax.psum_scatter(cross_out_grad, ("dp", "seq"), scatter_dimension=0, tiled=True),
    )
    branch_one = grad_resid_one.astype(jnp.bfloat16)
    self_out_grad = jnp.einsum(
        "rcd,rce->de", self_context, branch_one, preferred_element_type=jnp.float32
    )
    grad_context = jnp.einsum(
        "rce,de->rcd", branch_one, self_proj, preferred_element_type=jnp.float32
    ).astype(jnp.bfloat16)
    grad_self_q, grad_self_k, grad_self_v = lax.map(
        lambda record: attend_back(
            record[0],
            record[1],
            record[2],
            self_allowed(record[3], record[4], offset),
            record[5],
            record[6],
        ),
        (queries, gathered[0], gathered[1], local_seg, frame_seg, self_logsum, grad_context),
    )
    joined = jnp.concatenate([grad_self_k, grad_self_v], axis=2)
    summed = lax.psum_scatter(
        jnp.transpose(joined, (1, 0, 2)).astype(jnp.bfloat16),
        "seq",
        scatter_dimension=0,
        tiled=True,
    ).astype(jnp.float32)
    key_shares = jnp.transpose(summed, (1, 0, 2)).astype(jnp.bfloat16)
    all_grads = jnp.concatenate([grad_self_q.astype(jnp.bfloat16), key_shares], axis=2)
    self_qkv_grad = jnp.einsum(
        "rcd,rce->de", normed_self, all_grads, preferred_element_type=jnp.float32
    )
    grad_normed = jnp.einsum(
        "rce,de->rcd", all_grads, self_full, preferred_element_type=jnp.float32
    )
    grad_back, gain_zero, bias_zero = norm_back(inputs, gains[:, 0], biases[:, 0], grad_normed)
    frames_grad = (grad_resid_one + grad_back).astype(jnp.bfloat16)
    gain_grad = jnp.stack([gain_zero, gain_one, gain_two], axis=1)
    bias_grad = jnp.stack([bias_zero, bias_one, bias_two], axis=1)
    self_shares = (
        lax.psum_scatter(gain_grad, ("dp", "seq"), scatter_dimension=0, tiled=True),
        lax.psum_scatter(bias_grad, ("dp", "seq"), scatter_dimension=0, tiled=True),
        lax.psum_scatter(self_qkv_grad, ("dp", "seq"), scatter_dimension=0, tiled=True),
        lax.psum_scatter(self_out_grad, ("dp", "seq"), scatter_dimension=0, tiled=True),
    )
    return (
        frames_out,
        frames_grad,
        text_grad,
        self_shares[0],
        self_shares[1],
        self_shares[2],
        self_shares[3],
        cross_shares[0],
        cross_shares[1],
        ffn_shares[0],
        ffn_shares[1],
    )


def fast_body(
    frames,
    frame_seg,
    text_states,
    text_len,
    norm_gain,
    norm_bias,
    self_qkv,
    self_out,
    cross_qkv,
    cross_out,
    ffn_up,
    ffn_down,
    cotangent,
):
    args = dict(
        frames=frames[0],
        gain=norm_gain.T,
        shift=norm_bias.T,
        sqkv=self_qkv,
        sout=self_out,
        cqkv=cross_qkv,
        cout=cross_out,
        up=ffn_up,
        down=ffn_down.reshape(4, 32, D),
        cot=cotangent[0],
        text=text_states[0],
        seg=frame_seg,
        text_len=text_len,
    )
    f = types.SimpleNamespace(**run_forward_kernel(args))
    a = types.SimpleNamespace(**args)
    units = (4, 4, 2, 2, 2, 32, D)
    back = run_backward_kernel(
        dict(
            ddown=f.ddown.reshape(units),
            slope=f.slope,
            nf=f.nf,
            down=f.down,
            up=f.up,
            cot=a.cot,
            gb=f.gb,
            r2=f.r2,
            r1=f.r1,
            cctx=f.cctx,
            ctx=f.ctx,
            cq=f.cq,
            ck=f.ck,
            cv=f.cv,
            clse=f.clse,
            nc=f.nc,
            text=a.text,
            q=f.q,
            k=f.k,
            v=f.v,
            lse=f.lse,
            normed=f.normed,
            frames=f.frames,
            cout=f.cout,
            cqkv=f.cqkv,
            sout=f.sout,
            sqkv=f.sqkv,
            seg=a.seg,
            text_len=a.text_len,
        )
    )
    b = types.SimpleNamespace(**back)
    outs = run_finish_kernel(
        dict(
            fin=b.fin, nfin=b.nfin, fmine=b.fmine, tmine=b.tmine, gr=b.gr, frames=a.frames, gb=f.gb, out=f.out
        )
    )
    n = types.SimpleNamespace(**outs)
    return (
        n.out[None],
        n.frames[None],
        n.text[None],
        n.gain.T,
        n.shift.T,
        n.sqkv,
        n.sout,
        n.cqkv,
        n.cout,
        n.up,
        n.down,
    )


def solution(mesh):
    return jax.shard_map(
        fast_body if dict(mesh.shape) == {"dp": 8, "seq": 4} else generic_body,
        mesh=mesh,
        in_specs=(
            P("dp", "seq", None),
            P("dp", None),
            P("dp", None, None),
            P("dp", None),
            P(("dp", "seq"), None),
            P(("dp", "seq"), None),
            P(("dp", "seq"), None),
            P(("dp", "seq"), None),
            P(("dp", "seq"), None),
            P(("dp", "seq"), None),
            P(("dp", "seq"), None),
            P(("dp", "seq"), None),
            P("dp", "seq", None),
        ),
        out_specs=(
            P("dp", "seq", None),
            P("dp", "seq", None),
            P("dp", "seq", None),
            P(("dp", "seq"), None),
            P(("dp", "seq"), None),
            P(("dp", "seq"), None),
            P(("dp", "seq"), None),
            P(("dp", "seq"), None),
            P(("dp", "seq"), None),
            P(("dp", "seq"), None),
            P(("dp", "seq"), None),
        ),
        check_vma=False,
    )
```
